128 devices in a mesh: section: 2 (over y_lo), dp: 32 (over z, y_hi, x), tensor: 2 (over core).
Axes of the slice: x: 4, y: 4 (y_hi: 2, y_lo: 2; y = y_hi * 2 + y_lo), z: 4, core: 2. Of those that a mesh axis runs over, the one named last changes fastest.
Arguments:
- tokens: bfloat16 [16384, 768], P('dp'), may hold values from -6 to 6
- cotangent: bfloat16 [16384, 768], P('dp'), may hold values from -6 to 6
- segments: int32 [64, 256], P('dp'), may hold values from 0 to 3, never falling along the last dimension, each value on 1 to 128 neighbouring positions
- routes: int32 [2, 16384], P('section', 'dp'), may hold values from 0 to 31, as said below
- keeps: int32 [2, 16384], P('section', 'dp'), may hold values from 0 to 1, as said below
- attn_gain: bfloat16 [2, 768], P('section', 'dp'), may hold values from 0.25 to 1.75
- moe_gain: bfloat16 [2, 768], P('section', 'dp'), may hold values from 0.25 to 1.75
- qkv_weight: bfloat16 [2, 3, 768, 768], P('section', None, 'dp', 'tensor'), may hold values from -0.3125 to 0.3125
- out_weight: bfloat16 [2, 768, 768], P('section', 'tensor', 'dp'), may hold values from -0.875 to 0.875
- router_weight: bfloat16 [2, 768, 32], P('section', 'dp'), may hold values from -0.109375 to 0.109375
- expert_in: bfloat16 [2, 32, 768, 3072], P('section', 'dp', None, 'tensor'), may hold values from -0.21875 to 0.21875
- expert_out: bfloat16 [2, 32, 3072, 768], P('section', 'dp', 'tensor'), may hold values from -4.156922 to 4.156922, as said below
Outputs:
- layer_outputs: float32 [2, 16384, 768], P('section', 'dp', 'tensor')
- input_grads: float32 [2, 16384, 768], P('section', 'dp', 'tensor')
- attn_gain_grad: float32 [2, 768], P('section', 'dp')
- moe_gain_grad: float32 [2, 768], P('section', 'dp')
- qkv_grad: float32 [2, 3, 768, 768], P('section', None, 'dp', 'tensor')
- out_grad: float32 [2, 768, 768], P('section', 'tensor', 'dp')
- router_grad: float32 [2, 768, 32], P('section', 'dp')
- expert_in_grad: float32 [2, 32, 768, 3072], P('section', 'dp', None, 'tensor')
- expert_out_grad: float32 [2, 32, 3072, 768], P('section', 'dp', 'tensor')
The draws below stay inside these ranges and needn't reach their ends.
Inputs may be any that keep to these rules, and one draw needn't show every extreme that they name: `routes`: in each layer one expert is named by 10 or more tokens of every sequence. keeps[l, i] is 1 exactly when fewer than 10 earlier tokens of the same sequence name the same expert in layer l; so at most 10 kept tokens of one sequence go to one expert. `expert_out`: independent entries of mean zero.
All inputs are finite; a program needn't handle non-finite values.
Results may differ from the reference program's by a relative error of at most 0.035.
Values may be sent and summed in bfloat16 or wider, within the bound.
No kernel may reach another device: no remote copies, remote signals or barrier semaphores. Data moves between devices by JAX's collectives and lax.ppermute only.
A program may use at most 192 MiB of HBM per device.

```python
import math
import jax
import jax.numpy as jnp
import numpy as np
from jax import lax

D = 768
HEADS = 12
HEAD_DIM = 64
FF = 3072
SEQ = 256
MB = 2
E = 32
SEQS = 64
TOKENS = 16384
CAP = 10
N_SECTION = 2


def route_tables(key):
    hot_expert = jax.random.randint(jax.random.fold_in(key, 101), (N_SECTION, 1, 1), 0, E)
    first_draw = jax.random.randint(jax.random.fold_in(key, 102), (N_SECTION, SEQS, SEQ), 0, E)
    second_draw = jax.random.randint(jax.random.fold_in(key, 103), (N_SECTION, SEQS, SEQ), 0, E)
    shuffle = jax.random.permutation(jax.random.fold_in(key, 104), E)
    common = shuffle[jnp.minimum(first_draw, second_draw)]
    scores = jax.random.randint(jax.random.fold_in(key, 105), (N_SECTION, SEQS, SEQ), 0, 1 << 16) * SEQ + jnp.arange(SEQ, dtype=jnp.int32)
    position_rank = jnp.argsort(jnp.argsort(scores, axis=-1), axis=-1)
    route_rows = jnp.where(position_rank < CAP, hot_expert, common).astype(jnp.int32)
    onehot = (route_rows[..., None] == jnp.arange(E, dtype=jnp.int32)).astype(jnp.int32)
    before = jnp.cumsum(onehot, axis=2) - onehot
    rank_rows = jnp.sum(before * onehot, axis=-1)
    keep_rows = (rank_rows < CAP).astype(jnp.int32)
    return (route_rows.reshape(N_SECTION, TOKENS), keep_rows.reshape(N_SECTION, TOKENS))


def draw_routes(key, part):
    shared = route_tables(key)
    return shared[0]


def draw_keeps(key, part):
    shared = route_tables(key)
    return shared[1]


def draw_expert_out(key, part):
    key = jax.random.fold_in(key, 7)
    spread = 1.8 * E / math.sqrt(FF)
    values = jax.random.normal(key, (N_SECTION, E, FF, D), jnp.float32)
    return (jnp.clip(values, -4.0, 4.0) * spread).astype(jnp.bfloat16)


def shard_levels(key, extent, cuts, smallest, largest):
    loudness = 1.0
    for dim, parts in cuts:
        steps = jax.random.uniform(jax.random.fold_in(jax.random.fold_in(key, 6), dim), (parts,), jnp.float32, smallest / len(cuts), largest / len(cuts))
        loudness = loudness * jnp.repeat(jnp.exp(steps), extent[dim] // parts).reshape((-1,) + (1,) * (len(extent) - 1 - dim))
    return loudness


def profile(count, total, reach, skew):
    weights = [(1 << 20) // math.isqrt(standing ** skew) + 1 for standing in range(2, count + 1)]
    rest, given = total - reach - (count - 1), [1] * (count - 1)
    while rest > 0:
        candidates = [i for i in range(count - 1) if given[i] < reach]
        whole, left = sum([weights[i] for i in candidates]), rest
        for i in candidates:
            extra = min(reach - given[i], max(1, left * weights[i] // whole), rest)
            given[i] = given[i] + extra
            rest = rest - extra
    return np.array([reach] + given)


def ragged_sizes(own_key, count, total, bound, skew):
    if count == 2:
        one = jax.random.randint(own_key, (), max(1, total - bound), min(bound, total - 1) + 1)
        return jnp.stack([one, total - one])
    sizes = jnp.asarray(profile(count, total, bound, skew), jnp.int32)
    pairs = (count - 1) // 2
    source_of, receiver = sizes[1:1 + 2 * pairs:2], sizes[2:2 + 2 * pairs:2]
    room = jnp.minimum(source_of - 1, bound - receiver)
    passed = jax.random.randint(jax.random.fold_in(own_key, 1), (pairs,), 0, 1 << 20) % (room + 1)
    sizes = sizes.at[1:1 + 2 * pairs:2].set(source_of - passed).at[2:2 + 2 * pairs:2].set(receiver + passed)
    return sizes[jax.random.permutation(jax.random.fold_in(own_key, 2), count)]


def gaussian(rng, shape, deviation, most, shards=(), kind=jnp.bfloat16):
    drawn = deviation * jax.random.normal(rng, shape, jnp.float32)
    if shards:
        drawn = drawn * shard_levels(rng, shape, shards, -0.22, 0.18)
    return jnp.clip(drawn, -most, most).astype(kind)


def setup_inputs(seed: int = 0) -> dict:
    streams_of = jax.random.split(jax.random.key(seed), 13)
    return {
        "tokens": gaussian(streams_of[0], (TOKENS, D), 1.0, 6.0, ((0, 32),)),
        "cotangent": gaussian(streams_of[1], (TOKENS, D), 1.0, 6.0, ((0, 32),)),
        "segments": jax.vmap(lambda own: jnp.searchsorted(jnp.cumsum(ragged_sizes(own, 4, SEQ, SEQ // 2, 0)), jnp.arange(SEQ), side="right"))(jax.random.split(streams_of[2], SEQS)).reshape((SEQS, SEQ)).astype(jnp.int32),
        "routes": draw_routes(jax.random.fold_in(streams_of[12], 71), 0),
        "keeps": draw_keeps(jax.random.fold_in(streams_of[12], 71), 0),
        "attn_gain": jnp.clip(1.0 + 0.15 * jax.random.normal(streams_of[5], (N_SECTION, D), jnp.float32), 0.25, 1.75).astype(jnp.bfloat16),
        "moe_gain": jnp.clip(1.0 + 0.15 * jax.random.normal(streams_of[6], (N_SECTION, D), jnp.float32), 0.25, 1.75).astype(jnp.bfloat16),
        "qkv_weight": gaussian(streams_of[7], (N_SECTION, 3, D, D), (D // 2) ** -0.5, 0.3125, ((0, 2), (2, 32), (3, 2))),
        "out_weight": gaussian(streams_of[8], (N_SECTION, D, D), (D // 16) ** -0.5, 0.875, ((0, 2), (1, 2), (2, 32))),
        "router_weight": gaussian(streams_of[9], (N_SECTION, D, E), (4 * D) ** -0.5, 0.109375, ((0, 2), (1, 32))),
        "expert_in": gaussian(streams_of[10], (N_SECTION, E, D, FF), D ** -0.5, 0.21875, ((0, 2), (1, 32), (3, 2))),
        "expert_out": draw_expert_out(jax.random.fold_in(streams_of[12], 71), 0),
    }


PRECISE = lax.Precision.HIGHEST
EPS = 1e-06
MASK_FILL = -1e+30

@jax.custom_vjp
def low(v):
    return lax.optimization_barrier(v.astype(jnp.bfloat16)).astype(jnp.float32)

@jax.custom_vjp
def low_back(v):
    return v

def low_keep(v):
    return (low(v), None)

def low_pass(kept, grad):
    return (grad,)

def back_keep(v):
    return (v, None)

def back_low(kept, grad):
    return (low(grad),)
low.defvjp(low_keep, low_pass)
low_back.defvjp(back_keep, back_low)

def rms_scale(rows_in, gain_row):
    return rows_in * lax.rsqrt(lax.optimization_barrier(jnp.mean(rows_in * rows_in, axis=-1, keepdims=True)) + EPS) * gain_row

def attend(block_rows):
    queries, key_rows, value_rows, seg_rows = block_rows
    scores = low_back(jnp.einsum('gqhe,gkhe->ghqk', queries, key_rows, precision=PRECISE) * HEAD_DIM ** (-0.5))
    same_doc = (seg_rows[:, :, None] == seg_rows[:, None, :])[:, None, :, :]
    masked = jnp.where(same_doc, scores, MASK_FILL)
    row_max = lax.optimization_barrier(jnp.max(masked, axis=-1, keepdims=True))
    exponent = jnp.exp(masked - row_max)
    soft_rows = exponent / lax.optimization_barrier(jnp.sum(exponent, axis=-1, keepdims=True))
    return jnp.einsum('ghqk,gkhe->gqhe', low(soft_rows), value_rows, precision=PRECISE)

def slot_table(route_rows, keep_rows):
    expert_hot = (route_rows[..., None] == jnp.arange(E, dtype=jnp.int32)).astype(jnp.int32) * keep_rows[..., None]
    before = jnp.cumsum(expert_hot, axis=1) - expert_hot
    rank_rows = lax.optimization_barrier(jnp.sum(before * expert_hot, axis=-1))
    slot_index = route_rows * CAP + rank_rows
    slot_hot = (slot_index[..., None] == jnp.arange(E * CAP, dtype=jnp.int32)) & (keep_rows[..., None] == 1)
    return slot_hot.astype(jnp.float32)

def encoder_layer(hidden_in, attn_gain, moe_gain, qkv_weight, out_weight, router_weight, expert_in, expert_out, route_rows, keep_rows, segments):
    normed = low(rms_scale(hidden_in, attn_gain))
    qkv_rows = low(low_back(jnp.einsum('gsd,cde->cgse', normed, qkv_weight, precision=PRECISE)))
    head_rows = qkv_rows.reshape(3, SEQS // MB, MB, SEQ, HEADS, HEAD_DIM)
    seg_groups = segments.reshape(SEQS // MB, MB, SEQ)
    mixed_rows = lax.map(jax.checkpoint(attend), (head_rows[0], head_rows[1], head_rows[2], seg_groups))
    mixed_rows = low(low_back(mixed_rows.reshape(SEQS, SEQ, D)))
    attention = low_back(jnp.einsum('gsk,kd->gsd', mixed_rows, out_weight, precision=PRECISE))
    hidden = hidden_in + attention
    moe_in = low(rms_scale(hidden, moe_gain))
    logits = low_back(jnp.einsum('gsd,de->gse', moe_in, router_weight, precision=PRECISE))
    router_prob = jax.nn.softmax(logits, axis=-1)
    chosen = (route_rows[..., None] == jnp.arange(E, dtype=jnp.int32)).astype(jnp.float32)
    gate_prob = lax.optimization_barrier(jnp.sum(router_prob * chosen, axis=-1))
    slot_hot = slot_table(route_rows, keep_rows)
    slot_rows = jnp.einsum('gsc,gsd->gcd', slot_hot, moe_in, precision=PRECISE)
    slot_rows = slot_rows.reshape(SEQS, E, CAP, D).transpose(1, 0, 2, 3).reshape(E, SEQS * CAP, D)
    slot_rows = low_back(slot_rows)
    expert_hidden = low_back(jnp.einsum('erd,edf->erf', slot_rows, expert_in, precision=PRECISE))
    activated = low(jax.nn.gelu(expert_hidden, approximate=True))
    expert_rows = low(low_back(jnp.einsum('erf,efd->erd', activated, expert_out, precision=PRECISE)))
    expert_rows = expert_rows.reshape(E, SEQS, CAP, D).transpose(1, 0, 2, 3).reshape(SEQS, E * CAP, D)
    returned = jnp.einsum('gsc,gcd->gsd', slot_hot, expert_rows, precision=PRECISE)
    return hidden + gate_prob[..., None] * returned

def reference(tokens, cotangent, segments, routes, keeps, attn_gain, moe_gain, qkv_weight, out_weight, router_weight, expert_in, expert_out):
    weights = (attn_gain, moe_gain, qkv_weight, out_weight, router_weight, expert_in, expert_out)

    def section_fn(layer_index):
        route_rows = routes[layer_index].reshape(SEQS, SEQ)
        keep_rows = keeps[layer_index].reshape(SEQS, SEQ)

        def run_layer(hidden_in, *params):
            return encoder_layer(hidden_in, *params, route_rows, keep_rows, segments)
        return run_layer
    first_params = tuple((weight[0].astype(jnp.float32) for weight in weights))
    second_params = tuple((weight[1].astype(jnp.float32) for weight in weights))
    start_rows = tokens.astype(jnp.float32).reshape(SEQS, SEQ, D)
    middle, back_first = jax.vjp(section_fn(0), start_rows, *first_params)
    final_rows, back_second = jax.vjp(section_fn(1), middle, *second_params)
    grads_second = back_second(cotangent.astype(jnp.float32).reshape(SEQS, SEQ, D))
    grads_first = back_first(grads_second[0])
    layer_outputs = jnp.stack([middle, final_rows]).reshape(2, TOKENS, D)
    input_grads = jnp.stack([grads_first[0], grads_second[0]]).reshape(2, TOKENS, D)
    stacked = [jnp.stack([grads_first[slot_number], grads_second[slot_number]]) for slot_number in range(1, 8)]
    return (layer_outputs, input_grads, stacked[0], stacked[1], stacked[2], stacked[3], stacked[4], stacked[5], stacked[6])
```

```python
import jax
import jax.numpy as jnp
from jax import lax
from jax.sharding import PartitionSpec as P

HEAD_DIM = 64
EPS = 1e-06
MASK_FILL = -1e30
SLOT_ROWS = 8

F32 = jnp.float32
BF16 = jnp.bfloat16


def swap(value, axis):
    return lax.ppermute(value, axis, [(0, 1), (1, 0)])


def dot(left, right, dims):
    return lax.dot_general(left, right, (dims, ((), ())), preferred_element_type=F32)


def rms_parts(rows_in, gain_row):
    inv_scale = lax.rsqrt(jnp.mean(rows_in * rows_in, axis=-1, keepdims=True) + EPS)
    normed = rows_in * inv_scale
    return (inv_scale, normed, (normed * gain_row).astype(BF16))


def rms_back(grad_out, inv_scale, normed, gain_row):
    grad_normed = grad_out * gain_row
    gain_grad = jnp.sum(grad_out * normed, axis=0)
    grad_in = inv_scale * (
        grad_normed - normed * jnp.mean(grad_normed * normed, axis=-1, keepdims=True)
    )
    return (grad_in, gain_grad)


def gelu_tanh(values):
    return jax.nn.gelu(values, approximate=True)


def pack_shard(qkv, out, router, attn_gain, moe_gain):
    owned, local_width = qkv.shape[1:]
    small = jnp.concatenate([router.reshape(-1), attn_gain, moe_gain])
    small = jnp.pad(small, (0, 8 * local_width - small.shape[0])).reshape(8, local_width)
    return jnp.concatenate([qkv.reshape(3 * owned, local_width), out.T, small], axis=0)


def unpack_dense(blocks, experts):
    parts, _, local_width = blocks.shape
    owned = 24
    qkv = blocks[:, : 3 * owned].reshape(parts, 3, owned, local_width)
    qkv = qkv.transpose(1, 0, 2, 3).reshape(3, parts * owned, local_width)
    out_t = blocks[:, 3 * owned : 4 * owned].reshape(parts * owned, local_width)
    small = blocks[:, 4 * owned :].reshape(parts, 8 * local_width)
    count = owned * experts
    router = small[:, :count].reshape(parts * owned, experts)
    attn_gain = small[:, count : count + owned].reshape(parts * owned).astype(F32)
    moe_gain = small[:, count + owned : count + 2 * owned].reshape(parts * owned).astype(F32)
    return (attn_gain, moe_gain, qkv, out_t, router)


def pack_grads(grads, parts):
    attn_gain_grad, moe_gain_grad, qkv_grad, out_grad_t, router_grad = grads
    model_width, local_width = out_grad_t.shape
    owned = model_width // parts
    qkv = qkv_grad.astype(BF16).reshape(3, parts, owned, local_width).transpose(1, 0, 2, 3)
    small = jnp.concatenate(
        [
            router_grad.reshape(parts, -1),
            attn_gain_grad.reshape(parts, owned),
            moe_gain_grad.reshape(parts, owned),
        ],
        axis=1,
    ).astype(BF16)
    small = jnp.pad(small, ((0, 0), (0, 8 * local_width - small.shape[1])))
    return jnp.concatenate(
        [
            qkv.reshape(parts, 3 * owned, local_width),
            out_grad_t.astype(BF16).reshape(parts, owned, local_width),
            small.reshape(parts, 8, local_width),
        ],
        axis=1,
    )


def slot_masks(route_row, keep_row, experts, capacity, core):
    chosen = (route_row[:, None] == jnp.arange(experts, dtype=jnp.int32)[None, :]).astype(F32)
    kept_hot = chosen * keep_row[:, None].astype(F32)
    count = route_row.shape[0]
    earlier = (jnp.arange(count)[:, None] > jnp.arange(count)[None, :]).astype(BF16)
    before = dot(earlier, kept_hot.astype(BF16), ((1,), (0,)))
    rank_row = jnp.sum(before * kept_hot, axis=1).astype(jnp.int32)
    half = capacity // 2
    slot = route_row * SLOT_ROWS + rank_row % half
    slot = jnp.where(keep_row == 1, slot, -1)
    in_half = rank_row // half
    columns = jnp.arange(experts * SLOT_ROWS, dtype=jnp.int32)[None, :]
    placed = slot[:, None] == columns
    own = (placed & (in_half == core)[:, None]).astype(BF16)
    other = (placed & (in_half == 1 - core)[:, None]).astype(BF16)
    return (chosen, own, other)


def head_scores(queries, key_rows, seg_row):
    scores = jnp.einsum(
        "qhe,khe->hqk", queries, key_rows, preferred_element_type=F32
    ) * HEAD_DIM ** (-0.5)
    same_doc = (seg_row[:, None] == seg_row[None, :])[None]
    return (scores, same_doc)


def attention_forward(hidden_in, seg_row, dense_full):
    attn_gain, moe_gain, qkv_full, out_t, router_full = dense_full
    row_count = hidden_in.shape[0]
    local_width = qkv_full.shape[2]
    head_count = local_width // HEAD_DIM
    scale_one, normed_one, normed_low = rms_parts(hidden_in, attn_gain)
    qkv_rows = jnp.einsum(
        "sd,cde->cse", normed_low, qkv_full, preferred_element_type=F32
    ).astype(BF16)
    queries = qkv_rows[0].reshape(row_count, head_count, HEAD_DIM)
    key_rows = qkv_rows[1].reshape(row_count, head_count, HEAD_DIM)
    value_rows = qkv_rows[2].reshape(row_count, head_count, HEAD_DIM)
    scores, same_doc = head_scores(queries, key_rows, seg_row)
    masked = jnp.where(same_doc, scores, MASK_FILL)
    row_max = jnp.max(masked, axis=-1, keepdims=True)
    exponent = jnp.exp(masked - row_max)
    row_total = jnp.sum(exponent, axis=-1, keepdims=True)
    soft_rows = (exponent / row_total).astype(BF16)
    log_total = row_max + jnp.log(row_total)
    mixed_heads = (
        jnp.einsum("hqk,khe->qhe", soft_rows, value_rows, preferred_element_type=F32)
        .astype(BF16)
        .reshape(row_count, local_width)
    )
    partial_attn = dot(mixed_heads, out_t, ((1,), (1,)))
    hidden = hidden_in + (partial_attn + swap(partial_attn, "tensor"))
    scale_two, normed_two, moe_in = rms_parts(hidden, moe_gain)
    logits = dot(moe_in, router_full, ((1,), (0,)))
    router_prob = jax.nn.softmax(logits, axis=-1)
    saved = (
        normed_low,
        scale_one,
        normed_one,
        queries,
        key_rows,
        value_rows,
        log_total,
        mixed_heads,
        scale_two,
        normed_two,
        moe_in,
        router_prob,
    )
    return (hidden, moe_in, router_prob, saved)


def attention_backward(grad_out, grad_back, grad_gate, gate_prob, chosen, saved, seg_row, dense_full):
    (
        normed_low,
        scale_one,
        normed_one,
        queries,
        key_rows,
        value_rows,
        log_total,
        mixed_heads,
        scale_two,
        normed_two,
        moe_in,
        router_prob,
    ) = saved
    attn_gain, moe_gain, qkv_full, out_t, router_full = dense_full
    row_count = grad_out.shape[0]
    local_width = qkv_full.shape[2]
    head_count = local_width // HEAD_DIM
    scaling = HEAD_DIM ** (-0.5)
    grad_logits = ((grad_gate * gate_prob)[:, None] * (chosen - router_prob)).astype(BF16)
    router_grad = dot(moe_in, grad_logits, ((0,), (0,)))
    grad_moe_in = grad_back + dot(grad_logits, router_full, ((1,), (1,)))
    grad_norm_two, moe_gain_grad = rms_back(grad_moe_in, scale_two, normed_two, moe_gain)
    grad_hidden = grad_out + grad_norm_two
    grad_attention = grad_hidden.astype(BF16)
    out_grad_t = dot(grad_attention, mixed_heads, ((0,), (0,)))
    grad_mixed = (
        dot(grad_attention, out_t, ((1,), (0,)))
        .astype(BF16)
        .reshape(row_count, head_count, HEAD_DIM)
    )
    scores, same_doc = head_scores(queries, key_rows, seg_row)
    soft_rows = jnp.where(same_doc, jnp.exp(scores - log_total), 0.0)
    grad_soft = jnp.einsum("qhe,khe->hqk", grad_mixed, value_rows, preferred_element_type=F32)
    row_delta = jnp.sum(soft_rows * grad_soft, axis=-1, keepdims=True)
    grad_scores = (soft_rows * (grad_soft - row_delta)).astype(BF16)
    grad_values = jnp.einsum(
        "hqk,qhe->khe", soft_rows.astype(BF16), grad_mixed, preferred_element_type=F32
    )
    grad_queries = (
        jnp.einsum("hqk,khe->qhe", grad_scores, key_rows, preferred_element_type=F32) * scaling
    )
    grad_keys = (
        jnp.einsum("hqk,qhe->khe", grad_scores, queries, preferred_element_type=F32) * scaling
    )
    grad_qkv = (
        jnp.stack([grad_queries, grad_keys, grad_values])
        .astype(BF16)
        .reshape(3, row_count, local_width)
    )
    qkv_grad = jnp.einsum("sd,cse->cde", normed_low, grad_qkv, preferred_element_type=F32)
    partial_norm = jnp.einsum("cse,cde->sd", grad_qkv, qkv_full, preferred_element_type=F32)
    grad_normed = partial_norm + swap(partial_norm, "tensor")
    grad_norm_one, attn_gain_grad = rms_back(grad_normed, scale_one, normed_one, attn_gain)
    grad_in = grad_hidden + grad_norm_one
    return (grad_in, (attn_gain_grad, moe_gain_grad, qkv_grad, out_grad_t, router_grad))


def to_experts(rows):
    doubled = jnp.concatenate([rows, rows], axis=0)
    return lax.all_to_all(doubled, ("section", "dp"), split_axis=0, concat_axis=0, tiled=True)


def from_experts(blocks, layer):
    arrived = lax.all_to_all(blocks, ("section", "dp"), split_axis=0, concat_axis=0, tiled=True)
    experts = blocks.shape[0] // 2
    return arrived[layer * experts : (layer + 1) * experts]


def to_slots(mask, rows, experts):
    return dot(mask, rows, ((0,), (0,))).astype(BF16).reshape(experts, SLOT_ROWS, rows.shape[1])


def to_tokens(own, other, slot_rows):
    flat = slot_rows.reshape(-1, slot_rows.shape[-1])
    return dot(own, flat, ((1,), (0,))) + dot(other, swap(flat, "tensor"), ((1,), (0,)))


def expert_forward(rows, halves_in, halves_out):
    hidden = [dot(rows, half, ((1,), (0,))) for half in halves_in]
    total = 0.0
    for part, half in zip(hidden, halves_out):
        total = total + dot(gelu_tanh(part).astype(BF16), half, ((1,), (0,)))
    return (hidden, total.astype(BF16))


def expert_backward(hidden, grad_rows, halves_in, halves_out):
    total = 0.0
    for part, half_in, half_out in zip(hidden, halves_in, halves_out):
        grad_act = dot(grad_rows, half_out, ((1,), (1,)))
        grad_pre = jax.vjp(gelu_tanh, part)[1](grad_act)[0].astype(BF16)
        total = total + dot(grad_pre, half_in, ((1,), (1,)))
    return total.astype(BF16)


def expert_weight_grads(rows, grad_rows, half_in, half_out):
    hidden = dot(rows, half_in, ((1,), (0,)))
    activated = gelu_tanh(hidden).astype(BF16)
    grad_act = dot(grad_rows, half_out, ((1,), (1,)))
    grad_pre = jax.vjp(gelu_tanh, hidden)[1](grad_act)[0].astype(BF16)
    return (dot(rows, grad_pre, ((0,), (0,))), dot(activated, grad_rows, ((0,), (0,))))


def local(
    tokens,
    cotangent,
    segments,
    routes,
    keeps,
    attn_gain,
    moe_gain,
    qkv_weight,
    out_weight,
    router_weight,
    expert_in,
    expert_out,
):
    section = lax.axis_index("section")
    core = lax.axis_index("tensor")
    first = section == 0
    _, seq_len = segments.shape
    model_width = tokens.shape[1]
    experts = router_weight.shape[2]
    parts = lax.axis_size("dp")
    capacity = max(2, 5 * seq_len // (4 * experts))

    mine = pack_shard(
        qkv_weight[0], out_weight[0], router_weight[0], attn_gain[0], moe_gain[0]
    )
    theirs = swap(mine, "section")
    shard_zero = jnp.where(first, mine, theirs)
    shard_one = jnp.where(first, theirs, mine)
    blocks_zero = lax.all_to_all(
        jnp.broadcast_to(shard_zero[None], (parts,) + shard_zero.shape),
        "dp",
        split_axis=0,
        concat_axis=0,
        tiled=True,
    )
    blocks_one = lax.all_gather(shard_one, "dp", axis=0, tiled=False)
    dense_zero = unpack_dense(blocks_zero, experts)
    dense_one = unpack_dense(blocks_one, experts)

    half_in = expert_in[0, 0]
    half_out = expert_out[0, 0]
    halves_in = (half_in, swap(half_in, "tensor"))
    halves_out = (half_out, swap(half_out, "tensor"))

    hidden_in = lax.dynamic_slice_in_dim(tokens, section * seq_len, seq_len, 0).astype(F32)
    target = lax.dynamic_slice_in_dim(cotangent, section * seq_len, seq_len, 0).astype(F32)
    seg_row = jnp.where(first, segments[0], segments[1])
    coded = (routes[0] + experts * keeps[0]).reshape(2, seq_len)
    coded_own = jnp.where(first, coded[0], coded[1])
    coded_other = swap(jnp.where(first, coded[1], coded[0]), "section")
    masks = []
    for code in (
        jnp.where(first, coded_own, coded_other),
        jnp.where(first, coded_other, coded_own),
    ):
        masks.append(slot_masks(code % experts, code // experts, experts, capacity, core))

    chosen_zero, own_zero, other_zero = masks[0]
    hidden_zero, moe_zero, prob_zero, saved_zero = attention_forward(
        hidden_in, seg_row, dense_zero
    )
    gate_zero = jnp.sum(prob_zero * chosen_zero, axis=1)
    arrived_zero = to_experts(to_slots(own_zero, moe_zero, experts))
    rows_zero = arrived_zero.reshape(-1, model_width)
    pre_zero, result_zero = expert_forward(rows_zero, halves_in, halves_out)
    returned_zero = to_tokens(
        own_zero, other_zero, from_experts(result_zero.reshape(arrived_zero.shape), 0)
    )
    layer_zero = hidden_zero + gate_zero[:, None] * returned_zero

    chosen_one, own_one, other_one = masks[1]
    hidden_one, moe_one, prob_one, saved_one = attention_forward(layer_zero, seg_row, dense_one)
    gate_one = jnp.sum(prob_one * chosen_one, axis=1)
    grad_tokens = (gate_one[:, None] * target).astype(BF16)
    arrived_one = to_experts(
        jnp.concatenate(
            [to_slots(own_one, moe_one, experts), to_slots(own_one, grad_tokens, experts)], axis=1
        )
    )
    rows_one = arrived_one[:, :SLOT_ROWS].reshape(-1, model_width)
    grad_rows_one = arrived_one[:, SLOT_ROWS:].reshape(-1, model_width)
    pre_one, result_one = expert_forward(rows_one, halves_in, halves_out)
    grad_x_one = expert_backward(pre_one, grad_rows_one, halves_in, halves_out)
    back_one = from_experts(
        jnp.concatenate(
            [
                result_one.reshape(-1, SLOT_ROWS, model_width),
                grad_x_one.reshape(-1, SLOT_ROWS, model_width),
            ],
            axis=1,
        ),
        1,
    )
    returned_one = to_tokens(own_one, other_one, back_one[:, :SLOT_ROWS])
    layer_one = hidden_one + gate_one[:, None] * returned_one
    grad_back_one = to_tokens(own_one, other_one, back_one[:, SLOT_ROWS:])

    grad_gate_one = jnp.sum(target * returned_one, axis=1)
    grad_mid, grads_one = attention_backward(
        target,
        grad_back_one,
        grad_gate_one,
        gate_one,
        chosen_one,
        saved_one,
        seg_row,
        dense_one,
    )

    grad_tokens = (gate_zero[:, None] * grad_mid).astype(BF16)
    grad_gate_zero = jnp.sum(grad_mid * returned_zero, axis=1)
    grad_rows_zero = to_experts(to_slots(own_zero, grad_tokens, experts)).reshape(-1, model_width)
    grad_x_zero = expert_backward(pre_zero, grad_rows_zero, halves_in, halves_out)
    grad_back_zero = to_tokens(
        own_zero, other_zero, from_experts(grad_x_zero.reshape(-1, SLOT_ROWS, model_width), 0)
    )
    grad_first, grads_zero = attention_backward(
        grad_mid,
        grad_back_zero,
        grad_gate_zero,
        gate_zero,
        chosen_zero,
        saved_zero,
        seg_row,
        dense_zero,
    )

    rows_own = jnp.where(first, rows_zero, rows_one)
    grad_rows_own = jnp.where(first, grad_rows_zero, grad_rows_one)
    expert_in_grad, expert_out_grad = expert_weight_grads(
        jnp.concatenate([rows_own, swap(rows_own, "tensor")], axis=0),
        jnp.concatenate([grad_rows_own, swap(grad_rows_own, "tensor")], axis=0),
        half_in,
        half_out,
    )

    sums = []
    for grads in (grads_zero, grads_one):
        pieces = lax.all_to_all(
            pack_grads(grads, parts), "dp", split_axis=0, concat_axis=0, tiled=True
        )
        sums.append(jnp.sum(pieces.astype(F32), axis=0))
    owned = jnp.where(first, sums[0], sums[1]) + swap(
        jnp.where(first, sums[1], sums[0]), "section"
    )
    width = owned.shape[1]
    share = model_width // parts
    qkv_grad = owned[: 3 * share].reshape(3, share, width)
    out_grad = owned[3 * share : 4 * share].T
    small = owned[4 * share :].reshape(-1)
    count = share * experts
    router_grad = small[:count].reshape(share, experts)
    attn_gain_grad = small[count : count + share]
    moe_gain_grad = small[count + share : count + 2 * share]

    def settle(of_zero, of_one):
        offset = core * width
        of_zero = lax.dynamic_slice_in_dim(of_zero, offset, width, 1)
        of_one = lax.dynamic_slice_in_dim(of_one, offset, width, 1)
        kept = jnp.where(first, of_zero, of_one)
        came = swap(jnp.where(first, of_one, of_zero), "section")
        return jnp.concatenate(
            [jnp.where(first, kept, came), jnp.where(first, came, kept)], axis=0
        )[None]

    return (
        settle(layer_zero, layer_one),
        settle(grad_first, grad_mid),
        attn_gain_grad[None],
        moe_gain_grad[None],
        qkv_grad[None],
        out_grad[None],
        router_grad[None],
        expert_in_grad[None, None],
        expert_out_grad[None, None],
    )


def solution(mesh):
    placed = (
        P("dp", None),
        P("dp", None),
        P("dp", None),
        P("section", "dp"),
        P("section", "dp"),
        P("section", "dp"),
        P("section", "dp"),
        P("section", None, "dp", "tensor"),
        P("section", "tensor", "dp"),
        P("section", "dp", None),
        P("section", "dp", None, "tensor"),
        P("section", "dp", "tensor", None),
    )
    return jax.shard_map(
        local,
        mesh=mesh,
        in_specs=placed,
        out_specs=(
            P("section", "dp", "tensor"),
            P("section", "dp", "tensor"),
            P("section", "dp"),
            P("section", "dp"),
            P("section", None, "dp", "tensor"),
            P("section", "tensor", "dp"),
            P("section", "dp", None),
            P("section", "dp", None, "tensor"),
            P("section", "dp", "tensor", None),
        ),
        check_vma=False,
    )
```

```python
import functools

import jax
import jax.numpy as jnp
from jax import lax
from jax.experimental import pallas as pl
from jax.experimental.pallas import tpu as pltpu
from jax.sharding import PartitionSpec as P

HEAD_DIM = 64
EPS = 1e-06
MASK_FILL = -1e30
LANES = 128

F32 = jnp.float32
BF16 = jnp.bfloat16


def swap(value, axis):
    return lax.ppermute(value, axis, [(0, 1), (1, 0)])


def dot(left, right, left_dim, right_dim):
    return lax.dot_general(
        left, right, (((left_dim,), (right_dim,)), ((), ())), preferred_element_type=F32
    )


def unpack_rows(block_ref, wide_ref, rows_ref, base, per, half):
    count = block_ref.shape[0] // per
    wide_ref[...] = block_ref[...].astype(F32)
    for c in range(half):
        for j in range(rows_ref.shape[1] // LANES):
            piece = wide_ref[pl.ds(base + j * half + c, count, stride=per), :]
            rows_ref[c * count : (c + 1) * count, j * LANES : (j + 1) * LANES] = piece.astype(BF16)


def pack_rows(rows, wide_ref, base, per, half):
    count = rows.shape[0] // half
    for c in range(half):
        for j in range(rows.shape[1] // LANES):
            wide_ref[pl.ds(base + j * half + c, count, stride=per), :] = rows[
                c * count : (c + 1) * count, j * LANES : (j + 1) * LANES
            ]


def mean_of(values):
    return jnp.sum(values, axis=-1, keepdims=True) * (1.0 / values.shape[-1])


def norm_parts(rows):
    inv_scale = lax.rsqrt(mean_of(rows * rows) + EPS)
    return (inv_scale, rows * inv_scale)


def norm_back(grad_out, inv_scale, normed, gain_row):
    grad_normed = grad_out * gain_row
    gain_grad = jnp.sum(grad_out * normed, axis=0, keepdims=True)
    return (inv_scale * (grad_normed - normed * mean_of(grad_normed * normed)), gain_grad)


def gain_rows(weight_ref, layout):
    turned = weight_ref[:, layout["tail"] :].astype(F32).T
    at = layout["experts"]
    return (turned[at : at + 1], turned[at + 1 : at + 2])


def one_hot_columns(slot_col, count):
    return (slot_col == lax.broadcasted_iota(jnp.int32, (slot_col.shape[0], count), 1)).astype(BF16)


def one_hot_rows(slot_row, count):
    return (slot_row == lax.broadcasted_iota(jnp.int32, (count, slot_row.shape[1]), 0)).astype(BF16)


def attend(hidden, weight_ref, layout, seg_col, seg_row, qkv_ref, mixed_ref, lse_ref, normed_ref, part_ref):
    width = layout["width"]
    attn_gain, _ = gain_rows(weight_ref, layout)
    _, normed = norm_parts(hidden)
    low = (normed * attn_gain).astype(BF16)
    normed_ref[...] = low
    qkv_ref[...] = dot(low, weight_ref[:, : 3 * width], 1, 0).astype(BF16)
    same = seg_col == seg_row
    for head in range(width // HEAD_DIM):
        at = head * HEAD_DIM
        queries = qkv_ref[:, at : at + HEAD_DIM]
        keys = qkv_ref[:, width + at : width + at + HEAD_DIM]
        values = qkv_ref[:, 2 * width + at : 2 * width + at + HEAD_DIM]
        scores = dot(queries, keys, 1, 1) * HEAD_DIM ** (-0.5)
        scores = jnp.where(same, scores, MASK_FILL)
        top = jnp.max(scores, axis=-1, keepdims=True)
        exponent = jnp.exp(scores - top)
        total = jnp.sum(exponent, axis=-1, keepdims=True)
        soft = (exponent * (1.0 / total)).astype(BF16)
        mixed_ref[:, at : at + HEAD_DIM] = dot(soft, values, 1, 0).astype(BF16)
        lse_ref[:, head : head + 1] = top + jnp.log(total)
    part_ref[...] = dot(mixed_ref[...], weight_ref[:, 3 * width : 4 * width], 1, 1)


def attend_first_kernel(layout, hidden_ref, weight_ref, seg_col, seg_row, *outs):
    attend(hidden_ref[...], weight_ref, layout, seg_col[...], seg_row[...], *outs)


def attend_next_kernel(
    layout,
    hidden_ref,
    gate_ref,
    block_own,
    block_other,
    slots_ref,
    weight_ref,
    seg_col,
    seg_row,
    layer_ref,
    back_ref,
    qkv_ref,
    mixed_ref,
    lse_ref,
    normed_ref,
    part_ref,
    wide_ref,
    rows_ref,
):
    returned = gather_back(layout, block_own, block_other, slots_ref, wide_ref, rows_ref, 0)
    back_ref[...] = returned.astype(BF16)
    layer_ref[...] = hidden_ref[...] + gate_ref[...] * returned
    attend(
        layer_ref[...],
        weight_ref,
        layout,
        seg_col[...],
        seg_row[...],
        qkv_ref,
        mixed_ref,
        lse_ref,
        normed_ref,
        part_ref,
    )


def gather_back(layout, block_own, block_other, slots_ref, wide_ref, rows_ref, base):
    half = layout["half"]
    per = block_own.shape[0] // layout["experts"]
    count = rows_ref.shape[0]
    total = 0.0
    for which, block in enumerate((block_own, block_other)):
        unpack_rows(block, wide_ref, rows_ref, base, per, half)
        total = total + dot(
            one_hot_columns(slots_ref[:, which : which + 1], count), rows_ref[...], 1, 0
        )
    return total


def send_slots(layout, slot_row, pieces, wide_ref, out_ref):
    half, experts = layout["half"], layout["experts"]
    per = wide_ref.shape[0] // experts
    placed = one_hot_rows(slot_row, half * experts)
    wide_ref[...] = jnp.zeros_like(wide_ref)
    for index, piece in enumerate(pieces):
        pack_rows(dot(placed, piece, 1, 0), wide_ref, index * layout["block"], per, half)
    low = wide_ref[...].astype(BF16)
    size = wide_ref.shape[0]
    out_ref[:size] = low
    out_ref[size:] = low


def route_kernel(
    layout,
    with_grad,
    hidden_ref,
    part_own,
    part_other,
    weight_ref,
    slots_ref,
    slot_row,
    *rest,
):
    if with_grad:
        target_ref, h1_ref, moe_ref, prob_ref, gate_ref, send_ref, wide_ref = rest
    else:
        h1_ref, moe_ref, prob_ref, gate_ref, send_ref, wide_ref = rest
    _, moe_gain = gain_rows(weight_ref, layout)
    hidden = hidden_ref[...] + (part_own[...] + part_other[...])
    h1_ref[...] = hidden
    _, normed = norm_parts(hidden)
    low = (normed * moe_gain).astype(BF16)
    moe_ref[...] = low
    logits = dot(low, weight_ref[:, layout["tail"] :], 1, 0)
    lane = lax.broadcasted_iota(jnp.int32, logits.shape, 1)
    logits = jnp.where(lane < layout["experts"], logits, MASK_FILL)
    exponent = jnp.exp(logits - jnp.max(logits, axis=-1, keepdims=True))
    prob = exponent * (1.0 / jnp.sum(exponent, axis=-1, keepdims=True))
    prob_ref[...] = prob
    chosen = lane == slots_ref[:, 2:3]
    gate = jnp.sum(jnp.where(chosen, prob, 0.0), axis=-1, keepdims=True)
    gate_ref[...] = gate
    pieces = [low]
    if with_grad:
        pieces.append((gate * target_ref[...]).astype(BF16))
    send_slots(layout, slot_row[...], pieces, wide_ref, send_ref)


def backward_kernel(layout, last, hidden_ref, prob_ref, gate_ref, block_own, block_other, slots_ref, grad_ref, *rest):
    if last:
        (weight_ref, qkv_ref, lse_ref, moe_ref, seg_col, seg_row) = rest[:6]
        (layer_ref, grad_hidden_ref, part_ref, grad_qkv_ref, grad_low_ref, small_ref, moe_gain_ref) = rest[6:13]
    else:
        (returned_ref, weight_ref, qkv_ref, lse_ref, moe_ref, seg_col, seg_row) = rest[:7]
        (grad_hidden_ref, part_ref, grad_qkv_ref, grad_low_ref, small_ref, moe_gain_ref) = rest[7:13]
    wide_ref, rows_ref, mixed_ref = rest[13:]
    width = layout["width"]
    scaling = HEAD_DIM ** (-0.5)
    hidden = hidden_ref[...]
    gate = gate_ref[...]
    grad_out = grad_ref[...]
    if last:
        returned = gather_back(layout, block_own, block_other, slots_ref, wide_ref, rows_ref, 0)
        layer_ref[...] = hidden + gate * returned
    else:
        returned = returned_ref[...].astype(F32)
    base = layout["block"] if last else 0
    grad_back = gather_back(layout, block_own, block_other, slots_ref, wide_ref, rows_ref, base)
    grad_gate = jnp.sum(grad_out * returned, axis=-1, keepdims=True)
    prob = prob_ref[...]
    lane = lax.broadcasted_iota(jnp.int32, prob.shape, 1)
    chosen = (lane == slots_ref[:, 2:3]).astype(F32)
    grad_logits = (grad_gate * gate * (chosen - prob)).astype(BF16)
    small_ref[...] = dot(moe_ref[...], grad_logits, 0, 0)
    grad_moe = grad_back + dot(grad_logits, weight_ref[:, layout["tail"] :], 1, 1)
    _, moe_gain = gain_rows(weight_ref, layout)
    inv_scale, normed = norm_parts(hidden)
    grad_norm, gain_grad = norm_back(grad_moe, inv_scale, normed, moe_gain)
    moe_gain_ref[...] = gain_grad
    grad_hidden = grad_out + grad_norm
    grad_hidden_ref[...] = grad_hidden
    low = grad_hidden.astype(BF16)
    grad_low_ref[...] = low
    mixed_ref[...] = dot(low, weight_ref[:, 3 * width : 4 * width], 1, 0).astype(BF16)
    same = seg_col[...] == seg_row[...]
    for head in range(width // HEAD_DIM):
        at = head * HEAD_DIM
        queries = qkv_ref[:, at : at + HEAD_DIM]
        keys = qkv_ref[:, width + at : width + at + HEAD_DIM]
        values = qkv_ref[:, 2 * width + at : 2 * width + at + HEAD_DIM]
        grad_mixed = mixed_ref[:, at : at + HEAD_DIM]
        scores = dot(queries, keys, 1, 1) * scaling
        soft = jnp.exp(jnp.where(same, scores - lse_ref[:, head : head + 1], MASK_FILL))
        grad_soft = dot(grad_mixed, values, 1, 1)
        delta = jnp.sum(soft * grad_soft, axis=-1, keepdims=True)
        grad_scores = (soft * (grad_soft - delta)).astype(BF16)
        grad_qkv_ref[:, at : at + HEAD_DIM] = (dot(grad_scores, keys, 1, 0) * scaling).astype(BF16)
        grad_qkv_ref[:, width + at : width + at + HEAD_DIM] = (
            dot(grad_scores, queries, 0, 0) * scaling
        ).astype(BF16)
        grad_qkv_ref[:, 2 * width + at : 2 * width + at + HEAD_DIM] = dot(
            soft.astype(BF16), grad_mixed, 0, 0
        ).astype(BF16)
    part_ref[...] = dot(grad_qkv_ref[...], weight_ref[:, : 3 * width], 1, 1)


def dense_grad_kernel(
    layout, low_ref, grad_qkv_ref, grad_low_ref, mixed_ref, part_ref, hidden_ref, small_ref, moe_gain_ref, out_ref
):
    width = layout["width"]
    experts = layout["experts"]
    out_ref[:, : 3 * width] = dot(low_ref[...], grad_qkv_ref[...], 0, 0).astype(BF16)
    out_ref[:, 3 * width : 4 * width] = dot(grad_low_ref[...], mixed_ref[...], 0, 0).astype(BF16)
    _, normed = norm_parts(hidden_ref[...])
    attn_gain = jnp.sum(part_ref[...] * normed, axis=0, keepdims=True)
    lane = lax.broadcasted_iota(jnp.int32, small_ref.shape, 1)
    small = small_ref[...]
    size = small.shape[0]
    attn_col = jnp.broadcast_to(attn_gain, (LANES, size)).T
    moe_col = jnp.broadcast_to(moe_gain_ref[...], (LANES, size)).T
    small = jnp.where(lane == experts, attn_col, small)
    small = jnp.where(lane == experts + 1, moe_col, small)
    out_ref[:, 4 * width :] = small.astype(BF16)


def input_grad_kernel(layout, send, part_own, part_other, hidden_ref, grad_hidden_ref, weight_ref, *rest):
    attn_gain, _ = gain_rows(weight_ref, layout)
    inv_scale, normed = norm_parts(hidden_ref[...])
    grad_norm, _ = norm_back(part_own[...] + part_other[...], inv_scale, normed, attn_gain)
    grad_in = grad_hidden_ref[...] + grad_norm
    if send:
        gate_ref, slot_row, grad_ref, send_ref, wide_ref = rest
        pieces = [(gate_ref[...] * grad_in).astype(BF16)]
        send_slots(layout, slot_row[...], pieces, wide_ref, send_ref)
    else:
        (grad_ref,) = rest
    grad_ref[...] = grad_in


GELU_SCALE = 0.7978845608028654
GELU_CUBE = 0.044715


def gelu_parts(values):
    square = values * values
    bend = jnp.tanh(GELU_SCALE * (values + GELU_CUBE * (values * square)))
    return (square, bend)


def gelu_of(values, bend):
    return 0.5 * values * (1.0 + bend)


def gelu_slope(values, square, bend):
    inner = GELU_SCALE * (1.0 + 3.0 * GELU_CUBE * square)
    return 0.5 * (1.0 + bend) + 0.5 * values * (1.0 - bend * bend) * inner


def expert_kernel(layout, mode, *refs):
    half = layout["half"]
    step = pl.program_id(0)
    block_ref, refs = refs[0], refs[1:]
    if mode == "backward":
        x_ref, refs = refs[0], refs[1:]
    in_a, in_b, out_a, out_b = refs[:4]
    refs = refs[4:]
    if mode == "forward":
        send_ref, x_ref, wide_ref, y_acc = refs
    elif mode == "both":
        send_ref, x_ref, g_ref, wide_ref, y_acc, dx_acc = refs
    else:
        send_ref, g_ref, wide_ref, dx_acc = refs
    per = block_ref.shape[0] // layout["sequences"]

    @pl.when(step == 0)
    def _():
        if mode != "backward":
            unpack_rows(block_ref, wide_ref, x_ref, 0, per, half)
            y_acc[...] = jnp.zeros_like(y_acc)
        if mode != "forward":
            unpack_rows(
                block_ref, wide_ref, g_ref, layout["block"] if mode == "both" else 0, per, half
            )
            dx_acc[...] = jnp.zeros_like(dx_acc)

    rows = x_ref[...]
    for w_in, w_out in ((in_a, out_a), (in_b, out_b)):
        hidden = dot(rows, w_in[...], 1, 0)
        square, bend = gelu_parts(hidden)
        if mode != "backward":
            y_acc[...] += dot(gelu_of(hidden, bend).astype(BF16), w_out[...], 1, 0)
        if mode != "forward":
            grad_act = dot(g_ref[...], w_out[...], 1, 1)
            grad_pre = (grad_act * gelu_slope(hidden, square, bend)).astype(BF16)
            dx_acc[...] += dot(grad_pre, w_in[...], 1, 1)

    @pl.when(step == pl.num_programs(0) - 1)
    def _():
        wide_ref[...] = jnp.zeros_like(wide_ref)
        if mode != "backward":
            pack_rows(y_acc[...], wide_ref, 0, per, half)
        if mode != "forward":
            pack_rows(dx_acc[...], wide_ref, layout["block"] if mode == "both" else 0, per, half)
        send_ref[...] = wide_ref[...].astype(BF16)


def shape(dims, dtype):
    return jax.ShapeDtypeStruct(dims, dtype)


def call(kernel, outs, *args, scratch=(), flops=0, size=0):
    return pl.pallas_call(
        kernel,
        out_shape=outs,
        scratch_shapes=list(scratch),
        compiler_params=pltpu.CompilerParams(vmem_limit_bytes=14 << 20),
        cost_estimate=pl.CostEstimate(flops=flops, bytes_accessed=size, transcendentals=0),
    )(*args)


def run_experts(layout, mode, block, x_rows, halves_in, halves_out):
    rows = layout["half"] * layout["sequences"]
    width, hidden = halves_in[0].shape
    chunk = 384
    whole = lambda array: pl.BlockSpec(array.shape, lambda i: (0, 0))
    args, specs = [block], [whole(block)]
    if mode == "backward":
        args.append(x_rows)
        specs.append(whole(x_rows))
    args += [*halves_in, *halves_out]
    specs += [pl.BlockSpec((width, chunk), lambda i: (0, i))] * 2
    specs += [pl.BlockSpec((chunk, width), lambda i: (i, 0))] * 2
    row_shape = shape((rows, width), BF16)
    outs = [shape(block.shape, BF16)]
    if mode != "backward":
        outs.append(row_shape)
    if mode != "forward":
        outs.append(row_shape)
    scratch = [pltpu.VMEM(block.shape, F32), pltpu.VMEM((rows, width), F32)]
    if mode == "both":
        scratch.append(pltpu.VMEM((rows, width), F32))
    passes = {"forward": 4, "both": 8, "backward": 6}[mode]
    return pl.pallas_call(
        functools.partial(expert_kernel, layout, mode),
        grid=(hidden // chunk,),
        in_specs=specs,
        out_specs=[whole(out) for out in outs],
        out_shape=outs,
        scratch_shapes=scratch,
        compiler_params=pltpu.CompilerParams(
            vmem_limit_bytes=20 << 20, dimension_semantics=("arbitrary",)
        ),
        cost_estimate=pl.CostEstimate(
            flops=2 * passes * rows * width * hidden, bytes_accessed=8 * width * hidden, transcendentals=0
        ),
    )(*args)


def gelu_tanh(values):
    return jax.nn.gelu(values, approximate=True)


def expert_weight_grads(rows, grad_rows, half_in, half_out):
    hidden = dot(rows, half_in, 1, 0)
    activated = gelu_tanh(hidden).astype(BF16)
    grad_act = dot(grad_rows, half_out, 1, 1)
    grad_pre = jax.vjp(gelu_tanh, hidden)[1](grad_act)[0].astype(BF16)
    return (dot(rows, grad_pre, 0, 0), dot(activated, grad_rows, 0, 0))


def exchange(blocks, sequences):
    cut = blocks.reshape(sequences, -1, blocks.shape[1])
    came = lax.all_to_all(cut, ("section", "dp"), split_axis=0, concat_axis=0, tiled=True)
    return came.reshape(blocks.shape)


def local(
    tokens,
    cotangent,
    segments,
    routes,
    keeps,
    attn_gain,
    moe_gain,
    qkv_weight,
    out_weight,
    router_weight,
    expert_in,
    expert_out,
):
    section = lax.axis_index("section")
    core = lax.axis_index("tensor")
    first = section == 0
    seq_len = segments.shape[1]
    model_width = tokens.shape[1]
    experts = router_weight.shape[2]
    parts = lax.axis_size("dp")
    capacity = max(2, 5 * seq_len // (4 * experts))
    half = capacity // 2
    width = qkv_weight.shape[3]
    share = model_width // parts
    sequences = parts * lax.axis_size("section")
    block = -(-half * (model_width // LANES) // 16) * 16
    layout = {
        "width": width,
        "tail": 4 * width,
        "experts": experts,
        "half": half,
        "block": block,
        "sequences": sequences,
    }
    packed = 4 * width + LANES

    small = jnp.concatenate(
        [router_weight[0], attn_gain[0][:, None], moe_gain[0][:, None]], axis=1
    )
    small = jnp.pad(small, ((0, 0), (0, LANES - small.shape[1])))
    mine = jnp.concatenate(
        [qkv_weight[0, 0], qkv_weight[0, 1], qkv_weight[0, 2], out_weight[0].T, small], axis=1
    )
    theirs = swap(mine, "section")
    shard_zero = jnp.where(first, mine, theirs)
    shard_one = jnp.where(first, theirs, mine)
    dense_zero = lax.all_to_all(
        jnp.broadcast_to(shard_zero[None], (parts,) + shard_zero.shape),
        "dp",
        split_axis=0,
        concat_axis=0,
        tiled=True,
    ).reshape(model_width, packed)
    dense_one = lax.all_gather(shard_one, "dp", axis=0, tiled=True)

    half_in = expert_in[0, 0]
    half_out = expert_out[0, 0]
    halves_in = (half_in, swap(half_in, "tensor"))
    halves_out = (half_out, swap(half_out, "tensor"))

    hidden_in = lax.dynamic_slice_in_dim(tokens, section * seq_len, seq_len, 0).astype(F32)
    target = lax.dynamic_slice_in_dim(cotangent, section * seq_len, seq_len, 0).astype(F32)
    seg_row = jnp.where(first, segments[0], segments[1])
    seg_col, seg_row = seg_row[:, None], seg_row[None, :]
    coded = (routes[0] + experts * keeps[0]).reshape(2, seq_len)
    coded_own = jnp.where(first, coded[0], coded[1])
    coded_other = swap(jnp.where(first, coded[1], coded[0]), "section")
    slot_cols, slot_rows = [], []
    for code in (
        jnp.where(first, coded_own, coded_other),
        jnp.where(first, coded_other, coded_own),
    ):
        route, keep = code % experts, code // experts
        index = jnp.arange(seq_len)
        earlier = (route[:, None] == route[None, :]) & (index[:, None] > index[None, :])
        rank = jnp.sum(jnp.where(earlier, keep[None, :], 0), axis=1)
        slot = (rank % half) * experts + route
        kept = keep == 1
        own = jnp.where(kept & (rank // half == core), slot, -1)
        other = jnp.where(kept & (rank // half == 1 - core), slot, -1)
        slot_cols.append(jnp.stack([own, other, route], axis=1))
        slot_rows.append(own[None, :])

    rows_shape = (seq_len, model_width)
    attend_outs = [
        shape((seq_len, 3 * width), BF16),
        shape((seq_len, width), BF16),
        shape((seq_len, LANES), F32),
        shape(rows_shape, BF16),
        shape(rows_shape, F32),
    ]
    route_outs = [
        shape(rows_shape, F32),
        shape(rows_shape, BF16),
        shape((seq_len, LANES), F32),
        shape((seq_len, 1), F32),
    ]
    back_outs = [
        shape(rows_shape, F32),
        shape(rows_shape, F32),
        shape((seq_len, 3 * width), BF16),
        shape(rows_shape, BF16),
        shape((model_width, LANES), F32),
        shape((1, model_width), F32),
    ]
    slot_scratch = pltpu.VMEM((half * experts, model_width), BF16)
    wide_one = pltpu.VMEM((experts * block, LANES), F32)
    wide_two = pltpu.VMEM((experts * 2 * block, LANES), F32)
    mixed_scratch = pltpu.VMEM((seq_len, width), BF16)
    attn_cost = dict(flops=2 * seq_len * model_width * 5 * width, size=8 << 20)

    def returned(blocks, layer):
        size = blocks.shape[0] // 2
        own = blocks[layer * size : (layer + 1) * size]
        return (own, swap(own, "tensor"))

    qkv_zero, mixed_zero, lse_zero, low_zero, part = call(
        functools.partial(attend_first_kernel, layout),
        attend_outs,
        hidden_in,
        dense_zero,
        seg_col,
        seg_row,
        **attn_cost,
    )
    h1_zero, moe_zero, prob_zero, gate_zero, send = call(
        functools.partial(route_kernel, layout, False),
        route_outs + [shape((sequences * block, LANES), BF16)],
        hidden_in,
        part,
        swap(part, "tensor"),
        dense_zero,
        slot_cols[0],
        slot_rows[0],
        scratch=[wide_one],
        size=4 << 20,
    )
    send, x_zero = run_experts(
        layout, "forward", exchange(send, sequences), None, halves_in, halves_out
    )
    own, other = returned(exchange(send, sequences), 0)

    layer_zero, back_zero, qkv_one, mixed_one, lse_one, low_one, part = call(
        functools.partial(attend_next_kernel, layout),
        [shape(rows_shape, F32), shape(rows_shape, BF16)] + attend_outs,
        h1_zero,
        gate_zero,
        own,
        other,
        slot_cols[0],
        dense_one,
        seg_col,
        seg_row,
        scratch=[wide_one, slot_scratch],
        **attn_cost,
    )
    h1_one, moe_one, prob_one, gate_one, send = call(
        functools.partial(route_kernel, layout, True),
        route_outs + [shape((2 * sequences * block, LANES), BF16)],
        layer_zero,
        part,
        swap(part, "tensor"),
        dense_one,
        slot_cols[1],
        slot_rows[1],
        target,
        scratch=[wide_two],
        size=4 << 20,
    )
    send, x_one, g_one = run_experts(
        layout, "both", exchange(send, sequences), None, halves_in, halves_out
    )
    own, other = returned(exchange(send, sequences), 1)

    layer_one, hidden_grad, part, grad_qkv, grad_low, small, moe_gain_grad = call(
        functools.partial(backward_kernel, layout, True),
        [shape(rows_shape, F32)] + back_outs,
        h1_one,
        prob_one,
        gate_one,
        own,
        other,
        slot_cols[1],
        target,
        dense_one,
        qkv_one,
        lse_one,
        moe_one,
        seg_col,
        seg_row,
        scratch=[wide_two, slot_scratch, mixed_scratch],
        **attn_cost,
    )
    grad_mid, send = call(
        functools.partial(input_grad_kernel, layout, True),
        [shape(rows_shape, F32), shape((sequences * block, LANES), BF16)],
        part,
        swap(part, "tensor"),
        layer_zero,
        hidden_grad,
        dense_one,
        gate_zero,
        slot_rows[0],
        scratch=[wide_one],
        size=4 << 20,
    )
    grads_one = call(
        functools.partial(dense_grad_kernel, layout),
        shape((model_width, packed), BF16),
        low_one,
        grad_qkv,
        grad_low,
        mixed_one,
        part,
        layer_zero,
        small,
        moe_gain_grad,
        **attn_cost,
    )

    send, g_zero = run_experts(
        layout, "backward", exchange(send, sequences), x_zero, halves_in, halves_out
    )
    own, other = returned(exchange(send, sequences), 0)
    hidden_grad, part, grad_qkv, grad_low, small, moe_gain_grad = call(
        functools.partial(backward_kernel, layout, False),
        back_outs,
        h1_zero,
        prob_zero,
        gate_zero,
        own,
        other,
        slot_cols[0],
        grad_mid,
        back_zero,
        dense_zero,
        qkv_zero,
        lse_zero,
        moe_zero,
        seg_col,
        seg_row,
        scratch=[wide_one, slot_scratch, mixed_scratch],
        **attn_cost,
    )
    grads_zero = call(
        functools.partial(dense_grad_kernel, layout),
        shape((model_width, packed), BF16),
        low_zero,
        grad_qkv,
        grad_low,
        mixed_zero,
        part,
        hidden_in,
        small,
        moe_gain_grad,
        **attn_cost,
    )
    grad_first = call(
        functools.partial(input_grad_kernel, layout, False),
        shape(rows_shape, F32),
        part,
        swap(part, "tensor"),
        hidden_in,
        hidden_grad,
        dense_zero,
        size=4 << 20,
    )

    rows_own = jnp.where(first, x_zero, x_one)
    grad_rows_own = jnp.where(first, g_zero, g_one)
    expert_in_grad, expert_out_grad = expert_weight_grads(
        jnp.concatenate([rows_own, swap(rows_own, "tensor")], axis=0),
        jnp.concatenate([grad_rows_own, swap(grad_rows_own, "tensor")], axis=0),
        half_in,
        half_out,
    )

    sums = []
    for grads in (grads_zero, grads_one):
        pieces = lax.all_to_all(
            grads.reshape(parts, share, packed), "dp", split_axis=0, concat_axis=0, tiled=True
        )
        sums.append(jnp.sum(pieces.astype(F32), axis=0))
    owned = jnp.where(first, sums[0], sums[1]) + swap(
        jnp.where(first, sums[1], sums[0]), "section"
    )
    qkv_grad = jnp.stack([owned[:, :width], owned[:, width : 2 * width], owned[:, 2 * width : 3 * width]])
    out_grad = owned[:, 3 * width : 4 * width].T
    tail = 4 * width + experts
    router_grad = owned[:, 4 * width : tail]
    attn_gain_grad = owned[:, tail]
    attn_gain_grad = attn_gain_grad + swap(attn_gain_grad, "tensor")
    moe_gain_grad = owned[:, tail + 1]

    def settle(of_zero, of_one):
        offset = core * width
        of_zero = lax.dynamic_slice_in_dim(of_zero, offset, width, 1)
        of_one = lax.dynamic_slice_in_dim(of_one, offset, width, 1)
        kept = jnp.where(first, of_zero, of_one)
        came = swap(jnp.where(first, of_one, of_zero), "section")
        return jnp.concatenate(
            [jnp.where(first, kept, came), jnp.where(first, came, kept)], axis=0
        )[None]

    return (
        settle(layer_zero, layer_one),
        settle(grad_first, grad_mid),
        attn_gain_grad[None],
        moe_gain_grad[None],
        qkv_grad[None],
        out_grad[None],
        router_grad[None],
        expert_in_grad[None, None],
        expert_out_grad[None, None],
    )


def solution(mesh):
    placed = (
        P("dp", None),
        P("dp", None),
        P("dp", None),
        P("section", "dp"),
        P("section", "dp"),
        P("section", "dp"),
        P("section", "dp"),
        P("section", None, "dp", "tensor"),
        P("section", "tensor", "dp"),
        P("section", "dp", None),
        P("section", "dp", None, "tensor"),
        P("section", "dp", "tensor", None),
    )
    return jax.shard_map(
        local,
        mesh=mesh,
        in_specs=placed,
        out_specs=(
            P("section", "dp", "tensor"),
            P("section", "dp", "tensor"),
            P("section", "dp"),
            P("section", "dp"),
            P("section", None, "dp", "tensor"),
            P("section", "tensor", "dp"),
            P("section", "dp", None),
            P("section", "dp", None, "tensor"),
            P("section", "dp", "tensor", None),
        ),
        check_vma=False,
    )
```

```python
import functools

import jax
import jax.numpy as jnp
from jax import lax
from jax.experimental import pallas as pl
from jax.experimental.pallas import tpu as pltpu
from jax.sharding import PartitionSpec as P

HEAD_DIM = 64
EPS = 1e-06
MASK_FILL = -1e30
LANES = 128

F32 = jnp.float32
BF16 = jnp.bfloat16


def swap(value, axis):
    return lax.ppermute(value, axis, [(0, 1), (1, 0)])


def dot(left, right, left_dim, right_dim):
    return lax.dot_general(
        left, right, (((left_dim,), (right_dim,)), ((), ())), preferred_element_type=F32
    )


def unpack_rows(block_ref, wide_ref, rows_ref, base, per, half):
    count = block_ref.shape[0] // per
    wide_ref[...] = block_ref[...].astype(F32)
    for c in range(half):
        for j in range(rows_ref.shape[1] // LANES):
            piece = wide_ref[pl.ds(base + j * half + c, count, stride=per), :]
            rows_ref[c * count : (c + 1) * count, j * LANES : (j + 1) * LANES] = piece.astype(BF16)


def pack_rows(rows, wide_ref, base, per, half):
    count = rows.shape[0] // half
    for c in range(half):
        for j in range(rows.shape[1] // LANES):
            wide_ref[pl.ds(base + j * half + c, count, stride=per), :] = rows[
                c * count : (c + 1) * count, j * LANES : (j + 1) * LANES
            ]


def mean_of(values):
    return jnp.sum(values, axis=-1, keepdims=True) * (1.0 / values.shape[-1])


def norm_parts(rows):
    inv_scale = lax.rsqrt(mean_of(rows * rows) + EPS)
    return (inv_scale, rows * inv_scale)


def norm_back(grad_out, inv_scale, normed, gain_row):
    grad_normed = grad_out * gain_row
    gain_grad = jnp.sum(grad_out * normed, axis=0, keepdims=True)
    return (inv_scale * (grad_normed - normed * mean_of(grad_normed * normed)), gain_grad)


def tail_rows(tail_ref):
    return tail_ref[...].astype(F32).T


def one_hot_columns(slot_col, count):
    return (slot_col == lax.broadcasted_iota(jnp.int32, (slot_col.shape[0], count), 1)).astype(BF16)


def one_hot_rows(slot_row, count):
    return (slot_row == lax.broadcasted_iota(jnp.int32, (count, slot_row.shape[1]), 0)).astype(BF16)


class Staged:
    def __init__(self, ref, copy=None):
        self.ref, self.copy, self.waited, self.started = ref, copy, False, False

    def start(self):
        if self.copy is not None and not self.started:
            self.copy.start()
            self.started = True

    def __call__(self):
        if self.copy is not None and not self.waited:
            self.copy.wait()
            self.waited = True
        return self.ref

    def put(self, value):
        self.ref[...] = value
        self.start()


def shape(dims, dtype):
    return jax.ShapeDtypeStruct(dims, dtype)


class After:
    def __init__(self, what):
        self.what = what


class Far:
    def __init__(self, what, lane=0):
        self.what, self.lane = what, lane


def staged_kernel(kernel, ins, outs, scratch_count, *refs):
    count = len(ins) + len(outs)
    rest = list(refs[count:])
    scratch, rest = rest[:scratch_count], rest[scratch_count:]
    far = [item for item in list(ins) + list(outs) if isinstance(item, Far)]
    rooms, sems = rest[: len(far)], rest[len(far)] if far else None
    staged = []
    index = 0
    for place, (item, ref) in enumerate(zip(list(ins) + list(outs), refs)):
        if isinstance(item, After):
            continue
        if not isinstance(item, Far):
            staged.append(Staged(ref))
            continue
        if place < len(ins):
            source = ref if item.lane == 0 else ref.at[:, item.lane :]
            copy = pltpu.make_async_copy(source, rooms[index], sems.at[index])
        else:
            copy = pltpu.make_async_copy(rooms[index], ref, sems.at[index])
        staged.append(Staged(rooms[index], copy))
        index += 1
    given = sum(not isinstance(item, After) for item in ins)
    for item in staged[:given]:
        item.start()
    kernel(*staged, *scratch)
    for item in staged[:given]:
        item()
    for item in staged[given:]:
        item.start()
    for item in staged[given:]:
        item()


def call(kernel, outs, *ins, scratch=(), flops=0, size=0):
    far = [item for item in list(ins) + list(outs) if isinstance(item, Far)]
    rooms = [
        pltpu.VMEM(item.what.shape[:-1] + (item.what.shape[-1] - item.lane,), item.what.dtype)
        for item in far
    ]
    if far:
        rooms.append(pltpu.SemaphoreType.DMA((len(far),)))

    def spec(item):
        if isinstance(item, (Far, After)):
            return pl.BlockSpec(memory_space=pl.ANY)
        return pl.BlockSpec(memory_space=pltpu.SMEM if len(item.shape) == 1 else pltpu.VMEM)


    def operand(item):
        if isinstance(item, Far):
            return pltpu.with_memory_space_constraint(item.what, pltpu.HBM)
        return item.what if isinstance(item, After) else item

    args = [operand(item) for item in ins]
    shapes = [
        pltpu.HBM(item.what.shape, item.what.dtype) if isinstance(item, Far) else item
        for item in outs
    ]
    return pl.pallas_call(
        functools.partial(staged_kernel, kernel, ins, outs, len(scratch)),
        out_shape=shapes,
        in_specs=[spec(item) for item in ins],
        out_specs=[spec(item) for item in outs],
        scratch_shapes=list(scratch) + rooms,
        compiler_params=pltpu.CompilerParams(vmem_limit_bytes=24 << 20),
        cost_estimate=pl.CostEstimate(flops=flops, bytes_accessed=size, transcendentals=0),
    )(*args)


def pack_kernel(qkv, out, router, attn_gain, moe_gain, mine):
    to = mine.ref
    share = router()[0].shape[0]
    width = qkv()[0, 0].shape[1]
    experts = router()[0].shape[1]
    for c in range(3):
        to[:, c * width : (c + 1) * width] = qkv()[0, c]
    row = lax.broadcasted_iota(jnp.int32, (share, share), 0)
    lane = lax.broadcasted_iota(jnp.int32, (share, share), 1)
    eye = row == lane
    to[:, 3 * width : 4 * width] = dot(eye.astype(BF16), out()[0], 1, 1).astype(BF16)
    to[:, 4 * width :] = jnp.zeros((share, LANES), BF16)
    to[:, 4 * width : 4 * width + experts] = router()[0]
    for index, gain in enumerate((attn_gain, moe_gain)):
        spread = jnp.where(eye, jnp.broadcast_to(gain()[...].astype(F32), (share, share)), 0.0)
        at = 4 * width + experts + index
        to[:, at : at + 1] = jnp.sum(spread, axis=1, keepdims=True).astype(BF16)


def spread_kernel(parts, mine, theirs, section, copies, other):
    share = mine().shape[0]
    first = section()[0] == 0
    own, came = mine()[...].astype(F32), theirs()[...].astype(F32)
    zero = jnp.where(first, own, came)
    other.ref[...] = jnp.where(first, came, own).astype(BF16)
    several = 2
    block = jnp.concatenate([zero] * several, axis=0).astype(BF16)
    for part in range(parts // several):
        copies.ref[part * several * share : (part + 1) * several * share] = block


def attend(hidden, weight, layout, marks, rows, qkv, mixed, lse, part):
    width = layout["width"]
    weight_ref = weight()
    turned = tail_rows(weight_ref.at[:, layout["tail"] :])
    attn_gain = turned[layout["experts"] : layout["experts"] + 1]
    _, normed = norm_parts(hidden)
    low = (normed * attn_gain).astype(BF16)
    qkv.put(dot(low, weight_ref[:, : 3 * width], 1, 0).astype(BF16))
    same = marks()[:, 6:7] == rows()[2:3]
    for head in range(width // HEAD_DIM):
        at = head * HEAD_DIM
        queries = qkv.ref[:, at : at + HEAD_DIM]
        keys = qkv.ref[:, width + at : width + at + HEAD_DIM]
        values = qkv.ref[:, 2 * width + at : 2 * width + at + HEAD_DIM]
        scores = dot(queries, keys, 1, 1) * HEAD_DIM ** (-0.5)
        scores = jnp.where(same, scores, MASK_FILL)
        top = jnp.max(scores, axis=-1, keepdims=True)
        exponent = jnp.exp(scores - top)
        total = jnp.sum(exponent, axis=-1, keepdims=True)
        soft = (exponent * (1.0 / total)).astype(BF16)
        mixed.ref[:, at : at + HEAD_DIM] = dot(soft, values, 1, 0).astype(BF16)
        lse.ref[:, head : head + 1] = top + jnp.log(total)
    mixed.start()
    lse.start()
    part.ref[...] = dot(mixed.ref[...], weight_ref[:, 3 * width : 4 * width], 1, 1)


def attend_first_kernel(layout, hidden, weight, marks, rows, *outs):
    attend(hidden()[...].astype(F32), weight, layout, marks, rows, *outs)


def attend_next_kernel(
    layout, hidden, gate, block_own, block_other, weight, marks, rows, layer, back, qkv, mixed, lse, part, wide_ref, rows_ref
):
    returned = gather_back(layout, block_own(), block_other(), marks, 0, wide_ref, rows_ref, 0)
    back.put(returned.astype(BF16))
    layer.put(hidden()[...] + gate()[...] * returned)
    attend(layer.ref[...], weight, layout, marks, rows, qkv, mixed, lse, part)


def gather_back(layout, block_own, block_other, marks, layer, wide_ref, rows_ref, base):
    half = layout["half"]
    per = block_own.shape[0] // layout["experts"]
    count = rows_ref.shape[0]
    total = 0.0
    for which, block in enumerate((block_own, block_other)):
        at = 3 * layer + which
        unpack_rows(block, wide_ref, rows_ref, base, per, half)
        total = total + dot(
            one_hot_columns(marks()[:, at : at + 1], count), rows_ref[...], 1, 0
        )
    return total


def send_slots(layout, slot_row, pieces, wide_ref, out_ref):
    half, experts = layout["half"], layout["experts"]
    per = wide_ref.shape[0] // experts
    placed = one_hot_rows(slot_row, half * experts)
    wide_ref[...] = jnp.zeros_like(wide_ref)
    for index, piece in enumerate(pieces):
        pack_rows(dot(placed, piece, 1, 0), wide_ref, index * layout["block"], per, half)
    low = wide_ref[...].astype(BF16)
    size = wide_ref.shape[0]
    out_ref[:size] = low
    out_ref[size:] = low


def router_parts(layout, layer, hidden, tail_ref, marks):
    experts = layout["experts"]
    moe_gain = tail_rows(tail_ref)[experts + 1 : experts + 2]
    inv_scale, normed = norm_parts(hidden)
    low = (normed * moe_gain).astype(BF16)
    logits = dot(low, tail_ref[...], 1, 0)
    lane = lax.broadcasted_iota(jnp.int32, logits.shape, 1)
    logits = jnp.where(lane < experts, logits, MASK_FILL)
    exponent = jnp.exp(logits - jnp.max(logits, axis=-1, keepdims=True))
    prob = exponent * (1.0 / jnp.sum(exponent, axis=-1, keepdims=True))
    at = 3 * layer + 2
    chosen = lane == marks()[:, at : at + 1]
    gate = jnp.sum(jnp.where(chosen, prob, 0.0), axis=-1, keepdims=True)
    return (inv_scale, normed, moe_gain, low, prob, chosen.astype(F32), gate)


def route_kernel(layout, layer, hidden_in, part_own, part_other, tail, marks, rows, *rest):
    if layer == 1:
        target, h1, gate_out, send, wide_ref = rest
    else:
        h1, gate_out, send, wide_ref = rest
    hidden = hidden_in()[...].astype(F32) + (part_own()[...] + part_other()[...])
    h1.put(hidden)
    _, _, _, low, _, _, gate = router_parts(layout, layer, hidden, tail(), marks)
    gate_out.put(gate)
    pieces = [low]
    if layer == 1:
        pieces.append((gate * target()[...].astype(F32)).astype(BF16))
    send_slots(layout, rows()[layer : layer + 1], pieces, wide_ref, send.ref)


def backward_kernel(layout, layer, h1, block_own, block_other, grad, weight, marks, rows, qkv, lse, *rest):
    if layer == 1:
        layer_out, hidden_grad, part, grad_qkv, small, moe_gain_grad = rest[:6]
        rest = rest[6:]
    else:
        returned_in, mixed_in, layer_in, hidden_grad, part, dense_out = rest[:6]
        rest = rest[6:]
    wide_ref, rows_ref, mixed_ref = rest[:3]
    grad_qkv_ref = grad_qkv.ref if layer == 1 else rest[3]
    width = layout["width"]
    experts = layout["experts"]
    scaling = HEAD_DIM ** (-0.5)
    grad_out = grad()[...].astype(F32)
    hidden = h1()[...]
    weight_ref = weight()
    tail_ref = weight_ref.at[:, layout["tail"] :]
    inv_scale, normed, moe_gain, moe, prob, chosen, gate = router_parts(
        layout, layer, hidden, tail_ref, marks
    )
    own, other = block_own(), block_other()
    if layer == 1:
        returned = gather_back(layout, own, other, marks, layer, wide_ref, rows_ref, 0)
        layer_out.put(hidden + gate * returned)
    else:
        returned = returned_in()[...].astype(F32)
    base = layout["block"] if layer == 1 else 0
    grad_back = gather_back(layout, own, other, marks, layer, wide_ref, rows_ref, base)
    grad_gate = jnp.sum(grad_out * returned, axis=-1, keepdims=True)
    grad_logits = (grad_gate * gate * (chosen - prob)).astype(BF16)
    router_grad = dot(moe, grad_logits, 0, 0)
    grad_moe = grad_back + dot(grad_logits, tail_ref[...], 1, 1)
    grad_norm, gain_grad = norm_back(grad_moe, inv_scale, normed, moe_gain)
    if layer == 1:
        small.put(router_grad)
        moe_gain_grad.put(gain_grad)
    grad_hidden = grad_out + grad_norm
    hidden_grad.put(grad_hidden)
    mixed_ref[...] = dot(
        grad_hidden.astype(BF16), weight_ref[:, 3 * width : 4 * width], 1, 0
    ).astype(BF16)
    same = marks()[:, 6:7] == rows()[2:3]
    qkv_ref, lse_ref = qkv(), lse()
    for head in range(width // HEAD_DIM):
        at = head * HEAD_DIM
        queries = qkv_ref[:, at : at + HEAD_DIM]
        keys = qkv_ref[:, width + at : width + at + HEAD_DIM]
        values = qkv_ref[:, 2 * width + at : 2 * width + at + HEAD_DIM]
        grad_mixed = mixed_ref[:, at : at + HEAD_DIM]
        scores = dot(queries, keys, 1, 1) * scaling
        soft = jnp.exp(jnp.where(same, scores - lse_ref[:, head : head + 1], MASK_FILL))
        grad_soft = dot(grad_mixed, values, 1, 1)
        delta = jnp.sum(soft * grad_soft, axis=-1, keepdims=True)
        grad_scores = (soft * (grad_soft - delta)).astype(BF16)
        grad_qkv_ref[:, at : at + HEAD_DIM] = (dot(grad_scores, keys, 1, 0) * scaling).astype(BF16)
        grad_qkv_ref[:, width + at : width + at + HEAD_DIM] = (
            dot(grad_scores, queries, 0, 0) * scaling
        ).astype(BF16)
        grad_qkv_ref[:, 2 * width + at : 2 * width + at + HEAD_DIM] = dot(
            soft.astype(BF16), grad_mixed, 0, 0
        ).astype(BF16)
    if layer == 1:
        grad_qkv.start()
    part.ref[...] = dot(grad_qkv_ref[...], weight_ref[:, : 3 * width], 1, 1)
    if layer == 0:
        dense_grads(
            layout,
            layer_in()[...].astype(F32),
            tail_ref,
            grad_qkv_ref,
            grad_hidden,
            mixed_in(),
            part.ref,
            router_grad,
            gain_grad,
            dense_out.ref,
        )


def dense_grads(
    layout, layer_in, tail_ref, grad_qkv_ref, grad_hidden, mixed_ref, part_ref, router_grad, moe_gain_grad, out_ref
):
    width = layout["width"]
    experts = layout["experts"]
    _, normed = norm_parts(layer_in)
    attn_gain = tail_rows(tail_ref)[experts : experts + 1]
    low = (normed * attn_gain).astype(BF16)
    out_ref[:, : 3 * width] = dot(low, grad_qkv_ref[...], 0, 0).astype(BF16)
    out_ref[:, 3 * width : 4 * width] = dot(
        grad_hidden.astype(BF16), mixed_ref[...], 0, 0
    ).astype(BF16)
    attn_gain_grad = jnp.sum(part_ref[...] * normed, axis=0, keepdims=True)
    lane = lax.broadcasted_iota(jnp.int32, router_grad.shape, 1)
    size = router_grad.shape[0]
    attn_col = jnp.broadcast_to(attn_gain_grad, (LANES, size)).T
    moe_col = jnp.broadcast_to(moe_gain_grad, (LANES, size)).T
    small = jnp.where(lane == experts, attn_col, router_grad)
    small = jnp.where(lane == experts + 1, moe_col, small)
    out_ref[:, 4 * width :] = small.astype(BF16)


def dense_grad_kernel(
    layout, place, layer_in, tail, grad_qkv, hidden_grad, mixed, part, small, moe_gain_grad, *rest
):
    *pieces, out_ref = rest
    dense_grads(
        layout,
        layer_in()[...],
        tail(),
        grad_qkv(),
        hidden_grad()[...],
        mixed(),
        part(),
        small()[...],
        moe_gain_grad()[...],
        out_ref,
    )
    size = pieces[0].ref.shape[0]
    count = out_ref.shape[0] // size
    for step, piece in enumerate(pieces):
        at = lax.rem(place()[0] + step, count)
        piece.put(out_ref[pl.ds(pl.multiple_of(at * size, size), size), :])


def stage_kernel(count, place, own, *rest):
    *rest, wide_ref = rest
    came, outs = rest[:count], rest[count:]
    total = own()[...].astype(F32)
    for piece in came:
        total = total + piece()[...].astype(F32)
    if len(outs) == 1:
        outs[0].put(total)
        return
    wide_ref[...] = total
    size = outs[0].ref.shape[0]
    for step, out in enumerate(outs):
        at = lax.rem(place()[0] + step, len(outs))
        piece = wide_ref[pl.ds(pl.multiple_of(at * size, size), size), :]
        out.put(piece.astype(out.ref.dtype))


def choose_kernel(section, *refs):
    half = len(refs) // 3
    ins, outs = refs[: 2 * half], refs[2 * half :]
    first = section()[0] == 0
    for index, out in enumerate(outs):
        zero, one = ins[2 * index]()[...], ins[2 * index + 1]()[...]
        out.put(jnp.where(first, zero.astype(F32), one.astype(F32)).astype(out.ref.dtype))


def settle_kernel(place, zero, one, kept, going):
    first = place()[0] == 0
    width = kept.ref.shape[1]
    left = place()[1] == 0
    of_zero = jnp.where(left, zero()[:, :width], zero()[:, width:])
    of_one = jnp.where(left, one()[:, :width], one()[:, width:])
    going.put(jnp.where(first, of_one, of_zero))
    kept.put(jnp.where(first, of_zero, of_one))


def join_kernel(section, kept, came, out):
    count = kept().shape[0]
    first = section()[0] == 0
    out.ref[:count] = jnp.where(first, kept()[...], came()[...])
    out.ref[count:] = jnp.where(first, came()[...], kept()[...])
    out.start()


def input_grad_kernel(layout, send, part_own, part_other, layer_in, hidden_grad, tail, *rest):
    experts = layout["experts"]
    attn_gain = tail_rows(tail())[experts : experts + 1]
    inv_scale, normed = norm_parts(layer_in()[...].astype(F32))
    grad_norm, _ = norm_back(part_own()[...] + part_other()[...], inv_scale, normed, attn_gain)
    grad_in = hidden_grad()[...] + grad_norm
    if send:
        gate, rows, grad, send_out, wide_ref = rest
        grad.put(grad_in)
        pieces = [(gate()[...] * grad_in).astype(BF16)]
        send_slots(layout, rows()[0:1], pieces, wide_ref, send_out.ref)
    else:
        (grad,) = rest
        grad.put(grad_in)


def sum_kernel(parts, pieces, total):
    share = total.ref.shape[0]
    pair = 2 * share
    value = pieces()[:pair].astype(F32)
    for part in range(1, parts // 2):
        value = value + pieces()[part * pair : (part + 1) * pair].astype(F32)
    total.ref[...] = value[:share] + value[share:]


def finish_kernel(layout, section, *refs):
    sums, (qkv, out, router, attn_gain, moe_gain) = refs[:8], refs[8:]
    width, experts = layout["width"], layout["experts"]
    first = section()[0] == 0
    lane = lax.broadcasted_iota(jnp.int32, sums[2]().shape, 1)
    wholes, tails = [], []
    for mine, theirs, core, both in (sums[:4], sums[4:]):
        whole = mine()[...] + theirs()[...]
        extra = core()[...] + both()[...]
        wholes.append(whole)
        tails.append(whole[:, 4 * width :] + jnp.where(lane == experts, extra, 0.0))
    whole = jnp.where(first, wholes[0], wholes[1])
    tail = jnp.where(first, tails[0], tails[1])
    for c in range(3):
        qkv.ref[c] = whole[:, c * width : (c + 1) * width]
    share = whole.shape[0]
    turned = jnp.concatenate(
        [whole[:, 3 * width : 4 * width], jnp.zeros((LANES - share, width), F32)], axis=0
    ).T
    out.ref[...] = turned[:, :share]
    router.ref[...] = tail[:, :experts]
    turned = jnp.concatenate([tail, jnp.zeros((LANES - share, LANES), F32)], axis=0).T
    attn_gain.ref[...] = turned[experts : experts + 1, :share]
    moe_gain.ref[...] = turned[experts + 1 : experts + 2, :share]


GELU_SCALE = 0.7978845608028654
GELU_CUBE = 0.044715


def gelu_parts(values):
    square = values * values
    bend = jnp.tanh(GELU_SCALE * (values + GELU_CUBE * (values * square)))
    return (square, bend)


def gelu_of(values, bend):
    return 0.5 * values * (1.0 + bend)


def gelu_slope(values, square, bend):
    inner = GELU_SCALE * (1.0 + 3.0 * GELU_CUBE * square)
    return 0.5 * (1.0 + bend) + 0.5 * values * (1.0 - bend * bend) * inner


def expert_kernel(layout, mode, *refs):
    half = layout["half"]
    step = pl.program_id(0)
    block_ref, refs = refs[0], refs[1:]
    if mode == "backward":
        x_ref, refs = refs[0], refs[1:]
    in_a, in_b, out_a, out_b = refs[:4]
    refs = refs[4:]
    if mode == "forward":
        send_ref, x_ref, wide_ref, y_acc = refs
    elif mode == "both":
        send_ref, x_ref, g_ref, wide_ref, y_acc, dx_acc = refs
    else:
        send_ref, g_ref, wide_ref, dx_acc = refs
    per = block_ref.shape[0] // layout["sequences"]

    @pl.when(step == 0)
    def _():
        if mode != "backward":
            unpack_rows(block_ref, wide_ref, x_ref, 0, per, half)
            y_acc[...] = jnp.zeros_like(y_acc)
        if mode != "forward":
            unpack_rows(
                block_ref, wide_ref, g_ref, layout["block"] if mode == "both" else 0, per, half
            )
            dx_acc[...] = jnp.zeros_like(dx_acc)

    rows = x_ref[...]
    for w_in, w_out in ((in_a, out_a), (in_b, out_b)):
        hidden = dot(rows, w_in[...], 1, 0)
        square, bend = gelu_parts(hidden)
        if mode != "backward":
            y_acc[...] += dot(gelu_of(hidden, bend).astype(BF16), w_out[...], 1, 0)
        if mode != "forward":
            grad_act = dot(g_ref[...], w_out[...], 1, 1)
            grad_pre = (grad_act * gelu_slope(hidden, square, bend)).astype(BF16)
            dx_acc[...] += dot(grad_pre, w_in[...], 1, 1)

    @pl.when(step == pl.num_programs(0) - 1)
    def _():
        wide_ref[...] = jnp.zeros_like(wide_ref)
        if mode != "backward":
            pack_rows(y_acc[...], wide_ref, 0, per, half)
        if mode != "forward":
            pack_rows(dx_acc[...], wide_ref, layout["block"] if mode == "both" else 0, per, half)
        send_ref[...] = wide_ref[...].astype(BF16)


def run_experts(layout, mode, block, x_rows, halves_in, halves_out):
    rows = layout["half"] * layout["sequences"]
    width, hidden = halves_in[0].shape
    chunk = 384
    whole = lambda array: pl.BlockSpec(array.shape, lambda i: (0, 0))
    args, specs = [block], [whole(block)]
    if mode == "backward":
        args.append(pltpu.with_memory_space_constraint(x_rows, pltpu.HBM))
        specs.append(whole(x_rows))
    args += [pltpu.with_memory_space_constraint(w, pltpu.HBM) for w in (*halves_in, *halves_out)]
    specs += [pl.BlockSpec((width, chunk), lambda i: (0, i))] * 2
    specs += [pl.BlockSpec((chunk, width), lambda i: (i, 0))] * 2
    outs = [shape(block.shape, BF16)]
    row_far = pltpu.HBM((rows, width), BF16)
    if mode != "backward":
        outs.append(row_far)
    if mode != "forward":
        outs.append(row_far)
    scratch = [pltpu.VMEM(block.shape, F32), pltpu.VMEM((rows, width), F32)]
    if mode == "both":
        scratch.append(pltpu.VMEM((rows, width), F32))
    passes = {"forward": 4, "both": 8, "backward": 6}[mode]
    return pl.pallas_call(
        functools.partial(expert_kernel, layout, mode),
        grid=(hidden // chunk,),
        in_specs=specs,
        out_specs=[whole(out) for out in outs],
        out_shape=outs,
        scratch_shapes=scratch,
        compiler_params=pltpu.CompilerParams(
            vmem_limit_bytes=24 << 20, dimension_semantics=("arbitrary",)
        ),
        cost_estimate=pl.CostEstimate(
            flops=2 * passes * rows * width * hidden, bytes_accessed=8 * width * hidden, transcendentals=0
        ),
    )(*args)


def gelu_tanh(values):
    return jax.nn.gelu(values, approximate=True)


def expert_weight_grads(rows, grad_rows, half_in, half_out):
    hidden = dot(rows, half_in, 1, 0)
    activated = gelu_tanh(hidden).astype(BF16)
    grad_act = dot(grad_rows, half_out, 1, 1)
    grad_pre = jax.vjp(gelu_tanh, hidden)[1](grad_act)[0].astype(BF16)
    return (dot(rows, grad_pre, 0, 0), dot(activated, grad_rows, 0, 0))


def exchange(blocks, sequences):
    cut = blocks.reshape(sequences, -1, blocks.shape[1])
    came = lax.all_to_all(cut, ("section", "dp"), split_axis=0, concat_axis=0, tiled=True)
    return came.reshape(blocks.shape)


def ring_pairs(parts, stride, size, step):
    pairs = []
    for source in range(parts):
        at = source // stride % size
        pairs.append((source, source + ((at + step) % size - at) * stride))
    return pairs


def local(
    tokens,
    cotangent,
    segments,
    routes,
    keeps,
    attn_gain,
    moe_gain,
    qkv_weight,
    out_weight,
    router_weight,
    expert_in,
    expert_out,
):
    section = lax.axis_index("section")
    core = lax.axis_index("tensor")
    first = section == 0
    seq_len = segments.shape[1]
    model_width = tokens.shape[1]
    experts = router_weight.shape[2]
    parts = lax.axis_size("dp")
    capacity = max(2, 5 * seq_len // (4 * experts))
    half = capacity // 2
    width = qkv_weight.shape[3]
    share = model_width // parts
    sequences = parts * lax.axis_size("section")
    block = -(-half * (model_width // LANES) // 16) * 16
    tail = 4 * width
    layout = {
        "width": width,
        "tail": tail,
        "experts": experts,
        "half": half,
        "block": block,
        "sequences": sequences,
    }
    packed = tail + LANES
    section_ref = section.reshape(1).astype(jnp.int32)

    (mine,) = call(
        pack_kernel,
        [shape((share, packed), BF16)],
        qkv_weight,
        out_weight,
        router_weight,
        attn_gain,
        moe_gain,
    )
    copies, shard_one = call(
        functools.partial(spread_kernel, parts),
        [shape((parts * share, packed), BF16), shape((share, packed), BF16)],
        mine,
        swap(mine, "section"),
        section_ref,
    )
    dense_zero = lax.all_to_all(
        copies.reshape(parts, share, packed), "dp", split_axis=0, concat_axis=0, tiled=True
    ).reshape(model_width, packed)
    dense_one = lax.all_gather(shard_one, "dp", axis=0, tiled=True)

    half_in = expert_in[0, 0]
    half_out = expert_out[0, 0]
    halves_in = (half_in, swap(half_in, "tensor"))
    halves_out = (half_out, swap(half_out, "tensor"))

    hidden_in = lax.dynamic_slice_in_dim(tokens, section * seq_len, seq_len, 0)
    target = lax.dynamic_slice_in_dim(cotangent, section * seq_len, seq_len, 0)
    seg_row = jnp.where(first, segments[0], segments[1])
    coded = (routes[0] + experts * keeps[0]).reshape(2, seq_len)
    coded_own = jnp.where(first, coded[0], coded[1])
    coded_other = swap(jnp.where(first, coded[1], coded[0]), "section")
    columns, slot_rows = [], []
    for code in (
        jnp.where(first, coded_own, coded_other),
        jnp.where(first, coded_other, coded_own),
    ):
        route, keep = code % experts, code // experts
        index = jnp.arange(seq_len)
        earlier = (route[:, None] == route[None, :]) & (index[:, None] > index[None, :])
        rank = jnp.sum(jnp.where(earlier, keep[None, :], 0), axis=1)
        slot = (rank % half) * experts + route
        kept = keep == 1
        own = jnp.where(kept & (rank // half == core), slot, -1)
        other = jnp.where(kept & (rank // half == 1 - core), slot, -1)
        columns += [own, other, route]
        slot_rows.append(own)
    columns = jnp.stack(columns + [seg_row], axis=1)
    marks = Far(jnp.pad(columns, ((0, 0), (0, LANES - columns.shape[1]))))
    rows = Far(jnp.pad(jnp.stack(slot_rows + [seg_row], axis=0), ((0, 5), (0, 0))))

    rows_shape = (seq_len, model_width)
    far = lambda dims, dtype: Far(shape(dims, dtype))
    wide_rows = far(rows_shape, F32)
    near_rows = shape(rows_shape, F32)
    attend_outs = [
        far((seq_len, 3 * width), BF16),
        far((seq_len, width), BF16),
        far((seq_len, LANES), F32),
        near_rows,
    ]
    gate_shape = far((seq_len, 1), F32)
    slot_scratch = pltpu.VMEM((half * experts, model_width), BF16)
    wide_one = pltpu.VMEM((experts * block, LANES), F32)
    wide_two = pltpu.VMEM((experts * 2 * block, LANES), F32)
    mixed_scratch = pltpu.VMEM((seq_len, width), BF16)
    attn_cost = dict(flops=2 * seq_len * model_width * 5 * width, size=8 << 20)

    def returned(blocks, layer):
        size = blocks.shape[0] // 2
        own = blocks[layer * size : (layer + 1) * size]
        return (own, swap(own, "tensor"))

    qkv_zero, mixed_zero, lse_zero, part = call(
        functools.partial(attend_first_kernel, layout),
        attend_outs,
        Far(hidden_in),
        dense_zero,
        marks,
        rows,
        **attn_cost,
    )
    h1_zero, gate_zero, send = call(
        functools.partial(route_kernel, layout, 0),
        [wide_rows, gate_shape, shape((sequences * block, LANES), BF16)],
        Far(hidden_in),
        part,
        swap(part, "tensor"),
        Far(dense_zero, tail),
        marks,
        rows,
        scratch=[wide_one],
        size=4 << 20,
    )
    send, x_zero = run_experts(
        layout, "forward", exchange(send, sequences), None, halves_in, halves_out
    )
    own, other = returned(exchange(send, sequences), 0)

    layer_zero, back_zero, qkv_one, mixed_one, lse_one, part = call(
        functools.partial(attend_next_kernel, layout),
        [wide_rows, far(rows_shape, BF16)] + attend_outs,
        Far(h1_zero),
        Far(gate_zero),
        own,
        other,
        Far(dense_one),
        marks,
        rows,
        scratch=[wide_one, slot_scratch],
        **attn_cost,
    )
    h1_one, _, send = call(
        functools.partial(route_kernel, layout, 1),
        [wide_rows, gate_shape, shape((2 * sequences * block, LANES), BF16)],
        Far(layer_zero),
        part,
        swap(part, "tensor"),
        Far(dense_one, tail),
        marks,
        rows,
        Far(target),
        scratch=[wide_two],
        size=4 << 20,
    )
    send, x_one, g_one = run_experts(
        layout, "both", exchange(send, sequences), None, halves_in, halves_out
    )
    own, other = returned(exchange(send, sequences), 1)

    layer_one, hidden_grad, part, grad_qkv, small, moe_gain_grad = call(
        functools.partial(backward_kernel, layout, 1),
        [
            wide_rows,
            wide_rows,
            near_rows,
            far((seq_len, 3 * width), BF16),
            far((model_width, LANES), F32),
            far((1, model_width), F32),
        ],
        Far(h1_one),
        own,
        other,
        Far(target),
        Far(dense_one),
        marks,
        rows,
        Far(qkv_one),
        Far(lse_one),
        scratch=[wide_two, slot_scratch, mixed_scratch],
        **attn_cost,
    )
    grad_mid, send = call(
        functools.partial(input_grad_kernel, layout, True),
        [wide_rows, shape((sequences * block, LANES), BF16)],
        part,
        swap(part, "tensor"),
        Far(layer_zero),
        Far(hidden_grad),
        Far(dense_one, tail),
        Far(gate_zero),
        rows,
        scratch=[wide_one],
        size=4 << 20,
    )
    here = lax.axis_index("dp").astype(jnp.int32)
    across, mid = 4, parts // 16
    piece = lambda rows, dtype: shape((rows, packed), dtype)
    big, medium = model_width // across, model_width // across // mid

    def sent(pieces, stride, size):
        return [
            lax.ppermute(piece, "dp", ring_pairs(parts, stride, size, step + 1))
            for step, piece in enumerate(pieces)
        ]

    own, *pieces = call(
        functools.partial(dense_grad_kernel, layout),
        [Far(piece(big, BF16))] + [piece(big, BF16)] * (across - 1),
        (here // (across * mid)).reshape(1),
        Far(layer_zero),
        Far(dense_one, tail),
        Far(grad_qkv),
        Far(hidden_grad),
        Far(mixed_one),
        part,
        Far(small),
        Far(moe_gain_grad),
        After(send),
        scratch=[pltpu.VMEM((model_width, packed), BF16)],
        **attn_cost,
    )
    stage_one = (own, sent(pieces, across * mid, across))

    def settle(of_zero, of_one, *after):
        place = jnp.stack([section, core]).astype(jnp.int32)
        kept, going = call(
            settle_kernel,
            [far((seq_len, width), F32), shape((seq_len, width), F32)],
            place,
            Far(of_zero),
            Far(of_one),
            *after,
        )
        return (kept, swap(going, "section"))

    def join(kept, came, *after):
        (out,) = call(
            join_kernel,
            [far((2 * seq_len, width), F32)],
            section_ref,
            Far(kept),
            came,
            *after,
        )
        return out[None]

    send, g_zero = run_experts(
        layout, "backward", exchange(send, sequences), x_zero, halves_in, halves_out
    )
    own, other = returned(exchange(send, sequences), 0)
    hidden_grad, part, grads_zero = call(
        functools.partial(backward_kernel, layout, 0),
        [wide_rows, near_rows, shape((model_width, packed), BF16)],
        Far(h1_zero),
        own,
        other,
        Far(grad_mid),
        Far(dense_zero),
        marks,
        rows,
        Far(qkv_zero),
        Far(lse_zero),
        Far(back_zero),
        Far(mixed_zero),
        Far(hidden_in),
        scratch=[wide_one, slot_scratch, mixed_scratch, pltpu.VMEM((seq_len, 3 * width), BF16)],
        **attn_cost,
    )
    (grad_first,) = call(
        functools.partial(input_grad_kernel, layout, False),
        [wide_rows],
        part,
        swap(part, "tensor"),
        Far(hidden_in),
        Far(hidden_grad),
        Far(dense_zero, tail),
        size=4 << 20,
    )

    rows_own, grad_rows_own = call(
        choose_kernel,
        [shape(x_zero.shape, BF16)] * 2,
        section_ref,
        Far(x_zero),
        Far(x_one),
        Far(g_zero),
        Far(g_one),
        After(grads_zero),
    )
    expert_in_grad, expert_out_grad = expert_weight_grads(
        jnp.concatenate([rows_own, swap(rows_own, "tensor")], axis=0),
        jnp.concatenate([grad_rows_own, swap(grad_rows_own, "tensor")], axis=0),
        half_in,
        half_out,
    )

    pieces = lax.all_to_all(
        grads_zero.reshape(parts, share, packed), "dp", split_axis=0, concat_axis=0, tiled=True
    ).reshape(model_width, packed)
    (sum_zero,) = call(
        functools.partial(sum_kernel, parts), [shape((share, packed), F32)], pieces
    )
    own, came = stage_one
    own, *pieces = call(
        functools.partial(stage_kernel, across - 1),
        [piece(medium, F32)] + [piece(medium, BF16)] * (mid - 1),
        (here // across % mid).reshape(1),
        Far(own),
        *came,
        After(grads_zero),
        scratch=[pltpu.VMEM((big, packed), F32)],
    )
    came = sent(pieces, across, mid)
    own, *pieces = call(
        functools.partial(stage_kernel, mid - 1),
        [piece(share, F32)] + [piece(share, BF16)] * (across - 1),
        (here % across).reshape(1),
        own,
        *came,
        scratch=[pltpu.VMEM((medium, packed), F32)],
    )
    came = sent(pieces, 1, across)
    (sum_one,) = call(
        functools.partial(stage_kernel, across - 1),
        [piece(share, F32)],
        (here % across).reshape(1),
        own,
        *came,
        scratch=[pltpu.VMEM((8, LANES), F32)],
    )
    diagonal = [(i, 3 - i) for i in range(4)]
    sums = []
    for total in (sum_zero, sum_one):
        small = total[:, tail:]
        sums += [
            total,
            swap(total, "section"),
            swap(small, "tensor"),
            lax.ppermute(small, ("section", "tensor"), diagonal),
        ]
    qkv_grad, out_grad, router_grad, attn_gain_grad, moe_gain_grad = call(
        functools.partial(finish_kernel, layout),
        [
            shape((3, share, width), F32),
            shape((width, share), F32),
            shape((share, experts), F32),
            shape((1, share), F32),
            shape((1, share), F32),
        ],
        section_ref,
        *sums,
    )

    layer_pair = settle(layer_zero, layer_one, After(grads_zero))
    grad_pair = settle(grad_first, grad_mid)

    return (
        join(*layer_pair),
        join(*grad_pair),
        attn_gain_grad,
        moe_gain_grad,
        qkv_grad[None],
        out_grad[None],
        router_grad[None],
        expert_in_grad[None, None],
        expert_out_grad[None, None],
    )


def solution(mesh):
    placed = (
        P("dp", None),
        P("dp", None),
        P("dp", None),
        P("section", "dp"),
        P("section", "dp"),
        P("section", "dp"),
        P("section", "dp"),
        P("section", None, "dp", "tensor"),
        P("section", "tensor", "dp"),
        P("section", "dp", None),
        P("section", "dp", None, "tensor"),
        P("section", "dp", "tensor", None),
    )
    return jax.shard_map(
        local,
        mesh=mesh,
        in_specs=placed,
        out_specs=(
            P("section", "dp", "tensor"),
            P("section", "dp", "tensor"),
            P("section", "dp"),
            P("section", "dp"),
            P("section", None, "dp", "tensor"),
            P("section", "tensor", "dp"),
            P("section", "dp", None),
            P("section", "dp", None, "tensor"),
            P("section", "dp", "tensor", None),
        ),
        check_vma=False,
    )
```

```python
import functools

import jax
import jax.numpy as jnp
from jax import lax
from jax.experimental import pallas as pl
from jax.experimental.pallas import tpu as pltpu
from jax.sharding import PartitionSpec as P

HEAD_DIM = 64
EPS = 1e-06
MASK_FILL = -1e30
LANES = 128

F32 = jnp.float32
BF16 = jnp.bfloat16


def swap(value, axis):
    return lax.ppermute(value, axis, [(0, 1), (1, 0)])


def dot(left, right, left_dim, right_dim):
    return lax.dot_general(
        left, right, (((left_dim,), (right_dim,)), ((), ())), preferred_element_type=F32
    )


def unpack_rows(block_ref, wide_ref, rows_ref, base, per, half):
    count = block_ref.shape[0] // per
    wide_ref[...] = block_ref[...].astype(F32)
    for c in range(half):
        for j in range(rows_ref.shape[1] // LANES):
            piece = wide_ref[pl.ds(base + j * half + c, count, stride=per), :]
            rows_ref[c * count : (c + 1) * count, j * LANES : (j + 1) * LANES] = piece.astype(BF16)


def pack_rows(rows, wide_ref, base, per, half):
    count = rows.shape[0] // half
    for c in range(half):
        for j in range(rows.shape[1] // LANES):
            wide_ref[pl.ds(base + j * half + c, count, stride=per), :] = rows[
                c * count : (c + 1) * count, j * LANES : (j + 1) * LANES
            ]


def mean_of(values):
    return jnp.sum(values, axis=-1, keepdims=True) * (1.0 / values.shape[-1])


def norm_parts(rows):
    inv_scale = lax.rsqrt(mean_of(rows * rows) + EPS)
    return (inv_scale, rows * inv_scale)


def norm_back(grad_out, inv_scale, normed, gain_row):
    grad_normed = grad_out * gain_row
    gain_grad = jnp.sum(grad_out * normed, axis=0, keepdims=True)
    return (inv_scale * (grad_normed - normed * mean_of(grad_normed * normed)), gain_grad)


def tail_rows(tail_ref):
    return tail_ref[...].astype(F32).T


def one_hot_columns(slot_col, count):
    return (slot_col == lax.broadcasted_iota(jnp.int32, (slot_col.shape[0], count), 1)).astype(BF16)


def one_hot_rows(slot_row, count):
    return (slot_row == lax.broadcasted_iota(jnp.int32, (count, slot_row.shape[1]), 0)).astype(BF16)


class Staged:
    def __init__(self, ref, copy=None):
        self.ref, self.copy, self.waited, self.started = ref, copy, False, False

    def start(self):
        if self.copy is not None and not self.started:
            self.copy.start()
            self.started = True

    def __call__(self):
        if self.copy is not None and not self.waited:
            self.copy.wait()
            self.waited = True
        return self.ref

    def put(self, value):
        self.ref[...] = value
        self.start()


def shape(dims, dtype):
    return jax.ShapeDtypeStruct(dims, dtype)


class After:
    def __init__(self, what):
        self.what = what


class Far:
    def __init__(self, what, lane=0):
        self.what, self.lane = what, lane


def staged_kernel(kernel, ins, outs, scratch_count, *refs):
    count = len(ins) + len(outs)
    rest = list(refs[count:])
    scratch, rest = rest[:scratch_count], rest[scratch_count:]
    far = [item for item in list(ins) + list(outs) if isinstance(item, Far)]
    rooms, sems = rest[: len(far)], rest[len(far)] if far else None
    staged = []
    index = 0
    for place, (item, ref) in enumerate(zip(list(ins) + list(outs), refs)):
        if isinstance(item, After):
            continue
        if not isinstance(item, Far):
            staged.append(Staged(ref))
            continue
        if place < len(ins):
            source = ref if item.lane == 0 else ref.at[:, item.lane :]
            copy = pltpu.make_async_copy(source, rooms[index], sems.at[index])
        else:
            copy = pltpu.make_async_copy(rooms[index], ref, sems.at[index])
        staged.append(Staged(rooms[index], copy))
        index += 1
    given = sum(not isinstance(item, After) for item in ins)
    for item in staged[:given]:
        item.start()
    kernel(*staged, *scratch)
    for item in staged[:given]:
        item()
    for item in staged[given:]:
        item.start()
    for item in staged[given:]:
        item()


def call(kernel, outs, *ins, scratch=(), flops=0, size=0):
    far = [item for item in list(ins) + list(outs) if isinstance(item, Far)]
    rooms = [
        pltpu.VMEM(item.what.shape[:-1] + (item.what.shape[-1] - item.lane,), item.what.dtype)
        for item in far
    ]
    if far:
        rooms.append(pltpu.SemaphoreType.DMA((len(far),)))

    def spec(item):
        if isinstance(item, (Far, After)):
            return pl.BlockSpec(memory_space=pl.ANY)
        return pl.BlockSpec(memory_space=pltpu.SMEM if len(item.shape) == 1 else pltpu.VMEM)


    def operand(item):
        if isinstance(item, Far):
            return pltpu.with_memory_space_constraint(item.what, pltpu.HBM)
        return item.what if isinstance(item, After) else item

    args = [operand(item) for item in ins]
    shapes = [
        pltpu.HBM(item.what.shape, item.what.dtype) if isinstance(item, Far) else item
        for item in outs
    ]
    return pl.pallas_call(
        functools.partial(staged_kernel, kernel, ins, outs, len(scratch)),
        out_shape=shapes,
        in_specs=[spec(item) for item in ins],
        out_specs=[spec(item) for item in outs],
        scratch_shapes=list(scratch) + rooms,
        compiler_params=pltpu.CompilerParams(vmem_limit_bytes=24 << 20),
        cost_estimate=pl.CostEstimate(flops=flops, bytes_accessed=size, transcendentals=0),
    )(*args)


def pack_kernel(qkv, out, router, attn_gain, moe_gain, mine):
    to = mine.ref
    share = router()[0].shape[0]
    width = qkv()[0, 0].shape[1]
    experts = router()[0].shape[1]
    for c in range(3):
        to[:, c * width : (c + 1) * width] = qkv()[0, c]
    row = lax.broadcasted_iota(jnp.int32, (share, share), 0)
    lane = lax.broadcasted_iota(jnp.int32, (share, share), 1)
    eye = row == lane
    to[:, 3 * width : 4 * width] = out()[0]
    to[:, 4 * width :] = jnp.zeros((share, LANES), BF16)
    to[:, 4 * width : 4 * width + experts] = router()[0]
    for index, gain in enumerate((attn_gain, moe_gain)):
        spread = jnp.where(eye, jnp.broadcast_to(gain()[...].astype(F32), (share, share)), 0.0)
        at = 4 * width + experts + index
        to[:, at : at + 1] = jnp.sum(spread, axis=1, keepdims=True).astype(BF16)


def spread_kernel(parts, mine, theirs, section, copies, other):
    share = mine().shape[0]
    first = section()[0] == 0
    own, came = mine()[...].astype(F32), theirs()[...].astype(F32)
    zero = jnp.where(first, own, came)
    other.ref[...] = jnp.where(first, came, own).astype(BF16)
    several = 2
    block = jnp.concatenate([zero] * several, axis=0).astype(BF16)
    for part in range(parts // several):
        copies.ref[part * several * share : (part + 1) * several * share] = block


def attend(hidden, weight, layout, marks, rows, qkv, mixed, lse, part):
    width = layout["width"]
    weight_ref = weight()
    turned = tail_rows(weight_ref.at[:, layout["tail"] :])
    attn_gain = turned[layout["experts"] : layout["experts"] + 1]
    _, normed = norm_parts(hidden)
    low = (normed * attn_gain).astype(BF16)
    qkv.put(dot(low, weight_ref[:, : 3 * width], 1, 0).astype(BF16))
    same = marks()[:, 6:7] == rows()[2:3]
    for head in range(width // HEAD_DIM):
        at = head * HEAD_DIM
        queries = qkv.ref[:, at : at + HEAD_DIM]
        keys = qkv.ref[:, width + at : width + at + HEAD_DIM]
        values = qkv.ref[:, 2 * width + at : 2 * width + at + HEAD_DIM]
        scores = dot(queries, keys, 1, 1) * HEAD_DIM ** (-0.5)
        scores = jnp.where(same, scores, MASK_FILL)
        top = jnp.max(scores, axis=-1, keepdims=True)
        exponent = jnp.exp(scores - top)
        total = jnp.sum(exponent, axis=-1, keepdims=True)
        soft = (exponent * (1.0 / total)).astype(BF16)
        mixed.ref[:, at : at + HEAD_DIM] = dot(soft, values, 1, 0).astype(BF16)
        lse.ref[:, head : head + 1] = top + jnp.log(total)
    mixed.start()
    lse.start()
    part.ref[...] = dot(mixed.ref[...], weight_ref[:, 3 * width : 4 * width], 1, 1)


def attend_first_kernel(layout, hidden, weight, marks, rows, *outs):
    attend(hidden()[...].astype(F32), weight, layout, marks, rows, *outs)


def attend_next_kernel(
    layout, hidden, gate, block_own, block_other, weight, marks, rows, layer, back, qkv, mixed, lse, part, wide_ref, rows_ref
):
    returned = gather_back(layout, block_own(), block_other(), marks, 0, wide_ref, rows_ref, 0)
    back.put(returned.astype(BF16))
    layer.put(hidden()[...] + gate()[...] * returned)
    attend(layer.ref[...], weight, layout, marks, rows, qkv, mixed, lse, part)


def gather_back(layout, block_own, block_other, marks, layer, wide_ref, rows_ref, base):
    half = layout["half"]
    per = block_own.shape[0] // layout["experts"]
    count = rows_ref.shape[0]
    total = 0.0
    for which, block in enumerate((block_own, block_other)):
        at = 3 * layer + which
        unpack_rows(block, wide_ref, rows_ref, base, per, half)
        total = total + dot(
            one_hot_columns(marks()[:, at : at + 1], count), rows_ref[...], 1, 0
        )
    return total


def send_slots(layout, slot_row, pieces, wide_ref, out_ref):
    half, experts = layout["half"], layout["experts"]
    per = wide_ref.shape[0] // experts
    placed = one_hot_rows(slot_row, half * experts)
    wide_ref[...] = jnp.zeros_like(wide_ref)
    for index, piece in enumerate(pieces):
        pack_rows(dot(placed, piece, 1, 0), wide_ref, index * layout["block"], per, half)
    low = wide_ref[...].astype(BF16)
    size = wide_ref.shape[0]
    out_ref[:size] = low
    out_ref[size:] = low


def router_parts(layout, layer, hidden, tail_ref, marks):
    experts = layout["experts"]
    moe_gain = tail_rows(tail_ref)[experts + 1 : experts + 2]
    inv_scale, normed = norm_parts(hidden)
    low = (normed * moe_gain).astype(BF16)
    logits = dot(low, tail_ref[...], 1, 0)
    lane = lax.broadcasted_iota(jnp.int32, logits.shape, 1)
    logits = jnp.where(lane < experts, logits, MASK_FILL)
    exponent = jnp.exp(logits - jnp.max(logits, axis=-1, keepdims=True))
    prob = exponent * (1.0 / jnp.sum(exponent, axis=-1, keepdims=True))
    at = 3 * layer + 2
    chosen = lane == marks()[:, at : at + 1]
    gate = jnp.sum(jnp.where(chosen, prob, 0.0), axis=-1, keepdims=True)
    return (inv_scale, normed, moe_gain, low, prob, chosen.astype(F32), gate)


def route_kernel(layout, layer, hidden_in, part_own, part_other, tail, marks, rows, *rest):
    if layer == 1:
        target, h1, gate_out, send, wide_ref = rest
    else:
        h1, gate_out, send, wide_ref = rest
    hidden = hidden_in()[...].astype(F32) + (part_own()[...] + part_other()[...])
    h1.put(hidden)
    _, _, _, low, _, _, gate = router_parts(layout, layer, hidden, tail(), marks)
    gate_out.put(gate)
    pieces = [low]
    if layer == 1:
        pieces.append((gate * target()[...].astype(F32)).astype(BF16))
    send_slots(layout, rows()[layer : layer + 1], pieces, wide_ref, send.ref)


def backward_kernel(layout, layer, h1, block_own, block_other, grad, weight, marks, rows, qkv, lse, *rest):
    if layer == 1:
        layer_out, hidden_grad, part, grad_qkv, small, moe_gain_grad = rest[:6]
        rest = rest[6:]
    else:
        returned_in, mixed_in, layer_in, hidden_grad, part, dense_out = rest[:6]
        rest = rest[6:]
    wide_ref, rows_ref, mixed_ref = rest[:3]
    grad_qkv_ref = grad_qkv.ref if layer == 1 else rest[3]
    width = layout["width"]
    experts = layout["experts"]
    scaling = HEAD_DIM ** (-0.5)
    grad_out = grad()[...].astype(F32)
    hidden = h1()[...]
    weight_ref = weight()
    tail_ref = weight_ref.at[:, layout["tail"] :]
    inv_scale, normed, moe_gain, moe, prob, chosen, gate = router_parts(
        layout, layer, hidden, tail_ref, marks
    )
    own, other = block_own(), block_other()
    if layer == 1:
        returned = gather_back(layout, own, other, marks, layer, wide_ref, rows_ref, 0)
        layer_out.put(hidden + gate * returned)
    else:
        returned = returned_in()[...].astype(F32)
    base = layout["block"] if layer == 1 else 0
    grad_back = gather_back(layout, own, other, marks, layer, wide_ref, rows_ref, base)
    grad_gate = jnp.sum(grad_out * returned, axis=-1, keepdims=True)
    grad_logits = (grad_gate * gate * (chosen - prob)).astype(BF16)
    router_grad = dot(moe, grad_logits, 0, 0)
    grad_moe = grad_back + dot(grad_logits, tail_ref[...], 1, 1)
    grad_norm, gain_grad = norm_back(grad_moe, inv_scale, normed, moe_gain)
    if layer == 1:
        small.put(router_grad)
        moe_gain_grad.put(gain_grad)
    grad_hidden = grad_out + grad_norm
    hidden_grad.put(grad_hidden)
    mixed_ref[...] = dot(
        grad_hidden.astype(BF16), weight_ref[:, 3 * width : 4 * width], 1, 0
    ).astype(BF16)
    same = marks()[:, 6:7] == rows()[2:3]
    qkv_ref, lse_ref = qkv(), lse()
    for head in range(width // HEAD_DIM):
        at = head * HEAD_DIM
        queries = qkv_ref[:, at : at + HEAD_DIM]
        keys = qkv_ref[:, width + at : width + at + HEAD_DIM]
        values = qkv_ref[:, 2 * width + at : 2 * width + at + HEAD_DIM]
        grad_mixed = mixed_ref[:, at : at + HEAD_DIM]
        scores = dot(queries, keys, 1, 1) * scaling
        soft = jnp.exp(jnp.where(same, scores - lse_ref[:, head : head + 1], MASK_FILL))
        grad_soft = dot(grad_mixed, values, 1, 1)
        delta = jnp.sum(soft * grad_soft, axis=-1, keepdims=True)
        grad_scores = (soft * (grad_soft - delta)).astype(BF16)
        grad_qkv_ref[:, at : at + HEAD_DIM] = (dot(grad_scores, keys, 1, 0) * scaling).astype(BF16)
        grad_qkv_ref[:, width + at : width + at + HEAD_DIM] = (
            dot(grad_scores, queries, 0, 0) * scaling
        ).astype(BF16)
        grad_qkv_ref[:, 2 * width + at : 2 * width + at + HEAD_DIM] = dot(
            soft.astype(BF16), grad_mixed, 0, 0
        ).astype(BF16)
    if layer == 1:
        grad_qkv.start()
    part.ref[...] = dot(grad_qkv_ref[...], weight_ref[:, : 3 * width], 1, 1)
    if layer == 0:
        dense_grads(
            layout,
            layer_in()[...].astype(F32),
            tail_ref,
            grad_qkv_ref,
            grad_hidden,
            mixed_in(),
            part.ref,
            router_grad,
            gain_grad,
            dense_out.ref,
        )


def dense_grads(
    layout, layer_in, tail_ref, grad_qkv_ref, grad_hidden, mixed_ref, part_ref, router_grad, moe_gain_grad, out_ref
):
    width = layout["width"]
    experts = layout["experts"]
    _, normed = norm_parts(layer_in)
    attn_gain = tail_rows(tail_ref)[experts : experts + 1]
    low = (normed * attn_gain).astype(BF16)
    out_ref[:, : 3 * width] = dot(low, grad_qkv_ref[...], 0, 0).astype(BF16)
    out_ref[:, 3 * width : 4 * width] = dot(
        grad_hidden.astype(BF16), mixed_ref[...], 0, 0
    ).astype(BF16)
    attn_gain_grad = jnp.sum(part_ref[...] * normed, axis=0, keepdims=True)
    lane = lax.broadcasted_iota(jnp.int32, router_grad.shape, 1)
    size = router_grad.shape[0]
    attn_col = jnp.broadcast_to(attn_gain_grad, (LANES, size)).T
    moe_col = jnp.broadcast_to(moe_gain_grad, (LANES, size)).T
    small = jnp.where(lane == experts, attn_col, router_grad)
    small = jnp.where(lane == experts + 1, moe_col, small)
    out_ref[:, 4 * width : 4 * width + LANES] = small.astype(BF16)


def dense_grad_kernel(
    layout, layer_in, tail, grad_qkv, hidden_grad, mixed, part, small, moe_gain_grad, out
):
    dense_grads(
        layout,
        layer_in()[...],
        tail(),
        grad_qkv(),
        hidden_grad()[...],
        mixed(),
        part(),
        small()[...],
        moe_gain_grad()[...],
        out.ref,
    )


def choose_kernel(section, *refs):
    half = len(refs) // 3
    ins, outs = refs[: 2 * half], refs[2 * half :]
    first = section()[0] == 0
    for index, out in enumerate(outs):
        zero, one = ins[2 * index]()[...], ins[2 * index + 1]()[...]
        out.put(jnp.where(first, zero.astype(F32), one.astype(F32)).astype(out.ref.dtype))


def settle_kernel(place, zero, one, kept, going):
    first = place()[0] == 0
    width = kept.ref.shape[1]
    left = place()[1] == 0
    of_zero = jnp.where(left, zero()[:, :width], zero()[:, width:])
    of_one = jnp.where(left, one()[:, :width], one()[:, width:])
    going.put(jnp.where(first, of_one, of_zero).astype(BF16))
    kept.put(jnp.where(first, of_zero, of_one))


def join_kernel(section, kept, came, out):
    count = kept().shape[0]
    first = section()[0] == 0
    arrived = came()[...].astype(F32)
    out.ref[:count] = jnp.where(first, kept()[...], arrived)
    out.ref[count:] = jnp.where(first, arrived, kept()[...])
    out.start()


def input_grad_kernel(layout, send, part_own, part_other, layer_in, hidden_grad, tail, *rest):
    experts = layout["experts"]
    attn_gain = tail_rows(tail())[experts : experts + 1]
    inv_scale, normed = norm_parts(layer_in()[...].astype(F32))
    grad_norm, _ = norm_back(part_own()[...] + part_other()[...], inv_scale, normed, attn_gain)
    grad_in = hidden_grad()[...] + grad_norm
    if send:
        gate, rows, grad, send_out, wide_ref = rest
        grad.put(grad_in)
        pieces = [(gate()[...] * grad_in).astype(BF16)]
        send_slots(layout, rows()[0:1], pieces, wide_ref, send_out.ref)
    else:
        (grad,) = rest
        grad.put(grad_in)


def sum_pieces(pieces, total, parts):
    share, cols = total.shape
    pair = 2 * share
    for at in range(0, cols, LANES):
        value = pieces[:pair, at : at + LANES].astype(F32)
        for part in range(1, parts // 2):
            value = value + pieces[part * pair : (part + 1) * pair, at : at + LANES].astype(F32)
        total[:, at : at + LANES] = value[:share] + value[share:]


def sum_one_kernel(parts, pieces, total):
    sum_pieces(pieces(), total.ref, parts)


def sum_both_kernel(parts, section, pieces, one, mine, going, wide_ref):
    sum_pieces(pieces(), wide_ref, parts)
    first = section()[0] == 0
    zero, one = wide_ref[...], one()[...]
    mine.ref[...] = jnp.where(first, zero, one)
    going.ref[...] = jnp.where(first, one, zero)


def finish_kernel(layout, mine, theirs, core, across, qkv, out, router, attn_gain, moe_gain):
    width, experts = layout["width"], layout["experts"]
    whole = mine()[...] + theirs()[...]
    small = whole[:, 4 * width :]
    lane = lax.broadcasted_iota(jnp.int32, small.shape, 1)
    small = small + jnp.where(lane == experts, core()[...] + across()[...], 0.0)
    for c in range(3):
        qkv.ref[c] = whole[:, c * width : (c + 1) * width]
    out.ref[...] = whole[:, 3 * width : 4 * width]
    router.ref[...] = small[:, :experts]
    share = small.shape[0]
    turned = jnp.concatenate([small, jnp.zeros((LANES - share, LANES), F32)], axis=0).T
    attn_gain.ref[...] = turned[experts : experts + 1, :share]
    moe_gain.ref[...] = turned[experts + 1 : experts + 2, :share]


GELU_SCALE = 0.7978845608028654
GELU_CUBE = 0.044715


def gelu_parts(values):
    square = values * values
    bend = jnp.tanh(GELU_SCALE * (values + GELU_CUBE * (values * square)))
    return (square, bend)


def gelu_of(values, bend):
    return 0.5 * values * (1.0 + bend)


def gelu_slope(values, square, bend):
    inner = GELU_SCALE * (1.0 + 3.0 * GELU_CUBE * square)
    return 0.5 * (1.0 + bend) + 0.5 * values * (1.0 - bend * bend) * inner


def expert_kernel(layout, mode, *refs):
    half = layout["half"]
    step = pl.program_id(0)
    block_ref, refs = refs[0], refs[1:]
    if mode == "backward":
        x_ref, refs = refs[0], refs[1:]
    in_a, in_b, out_a, out_b = refs[:4]
    refs = refs[4:]
    if mode == "forward":
        send_ref, x_ref, wide_ref, y_acc = refs
    elif mode == "both":
        send_ref, x_ref, g_ref, wide_ref, y_acc, dx_acc = refs
    else:
        send_ref, g_ref, wide_ref, dx_acc = refs
    per = block_ref.shape[0] // layout["sequences"]

    @pl.when(step == 0)
    def _():
        if mode != "backward":
            unpack_rows(block_ref, wide_ref, x_ref, 0, per, half)
            y_acc[...] = jnp.zeros_like(y_acc)
        if mode != "forward":
            unpack_rows(
                block_ref, wide_ref, g_ref, layout["block"] if mode == "both" else 0, per, half
            )
            dx_acc[...] = jnp.zeros_like(dx_acc)

    rows = x_ref[...]
    for w_in, w_out in ((in_a, out_a), (in_b, out_b)):
        hidden = dot(rows, w_in[...], 1, 0)
        square, bend = gelu_parts(hidden)
        if mode != "backward":
            y_acc[...] += dot(gelu_of(hidden, bend).astype(BF16), w_out[...], 1, 0)
        if mode != "forward":
            grad_act = dot(g_ref[...], w_out[...], 1, 1)
            grad_pre = (grad_act * gelu_slope(hidden, square, bend)).astype(BF16)
            dx_acc[...] += dot(grad_pre, w_in[...], 1, 1)

    @pl.when(step == pl.num_programs(0) - 1)
    def _():
        wide_ref[...] = jnp.zeros_like(wide_ref)
        if mode != "backward":
            pack_rows(y_acc[...], wide_ref, 0, per, half)
        if mode != "forward":
            pack_rows(dx_acc[...], wide_ref, layout["block"] if mode == "both" else 0, per, half)
        send_ref[...] = wide_ref[...].astype(BF16)


def run_experts(layout, mode, block, x_rows, halves_in, halves_out):
    rows = layout["half"] * layout["sequences"]
    width, hidden = halves_in[0].shape
    chunk = 384
    whole = lambda array: pl.BlockSpec(array.shape, lambda i: (0, 0))
    args, specs = [block], [whole(block)]
    if mode == "backward":
        args.append(pltpu.with_memory_space_constraint(x_rows, pltpu.HBM))
        specs.append(whole(x_rows))
    args += [pltpu.with_memory_space_constraint(w, pltpu.HBM) for w in (*halves_in, *halves_out)]
    specs += [pl.BlockSpec((width, chunk), lambda i: (0, i))] * 2
    specs += [pl.BlockSpec((chunk, width), lambda i: (i, 0))] * 2
    outs = [shape(block.shape, BF16)]
    row_far = pltpu.HBM((rows, width), BF16)
    if mode != "backward":
        outs.append(row_far)
    if mode != "forward":
        outs.append(row_far)
    scratch = [pltpu.VMEM(block.shape, F32), pltpu.VMEM((rows, width), F32)]
    if mode == "both":
        scratch.append(pltpu.VMEM((rows, width), F32))
    passes = {"forward": 4, "both": 8, "backward": 6}[mode]
    return pl.pallas_call(
        functools.partial(expert_kernel, layout, mode),
        grid=(hidden // chunk,),
        in_specs=specs,
        out_specs=[whole(out) for out in outs],
        out_shape=outs,
        scratch_shapes=scratch,
        compiler_params=pltpu.CompilerParams(
            vmem_limit_bytes=24 << 20, dimension_semantics=("arbitrary",)
        ),
        cost_estimate=pl.CostEstimate(
            flops=2 * passes * rows * width * hidden, bytes_accessed=8 * width * hidden, transcendentals=0
        ),
    )(*args)


def expert_grad_kernel(rows_own, rows_other, grad_own, grad_other, w_in, w_out, grad_in, grad_out, x_ref, g_ref):
    size = rows_own.shape[0]

    @pl.when(pl.program_id(0) == 0)
    def _():
        x_ref[:size] = rows_own[...]
        x_ref[size:] = rows_other[...]
        g_ref[:size] = grad_own[...]
        g_ref[size:] = grad_other[...]

    hidden = dot(x_ref[...], w_in[...], 1, 0)
    square, bend = gelu_parts(hidden)
    grad_act = dot(g_ref[...], w_out[...], 1, 1)
    grad_pre = (grad_act * gelu_slope(hidden, square, bend)).astype(BF16)
    grad_in[...] = dot(x_ref[...], grad_pre, 0, 0)
    grad_out[...] = dot(gelu_of(hidden, bend).astype(BF16), g_ref[...], 0, 0)


def expert_weight_grads(rows_own, rows_other, grad_own, grad_other, half_in, half_out):
    size, width = rows_own.shape
    hidden = half_in.shape[1]
    chunk = 256
    whole = pl.BlockSpec((size, width), lambda i: (0, 0))
    by_in = pl.BlockSpec((width, chunk), lambda i: (0, i))
    by_out = pl.BlockSpec((chunk, width), lambda i: (i, 0))
    pin = lambda array: pltpu.with_memory_space_constraint(array, pltpu.HBM)
    return pl.pallas_call(
        expert_grad_kernel,
        grid=(hidden // chunk,),
        in_specs=[whole] * 4 + [by_in, by_out],
        out_specs=[by_in, by_out],
        out_shape=[pltpu.HBM((width, hidden), F32), pltpu.HBM((hidden, width), F32)],
        scratch_shapes=[pltpu.VMEM((2 * size, width), BF16)] * 2,
        compiler_params=pltpu.CompilerParams(
            vmem_limit_bytes=24 << 20, dimension_semantics=("arbitrary",)
        ),
        cost_estimate=pl.CostEstimate(
            flops=16 * size * width * hidden, bytes_accessed=12 * width * hidden, transcendentals=0
        ),
    )(rows_own, rows_other, grad_own, grad_other, pin(half_in), pin(half_out))


def exchange(blocks, sequences):
    cut = blocks.reshape(sequences, -1, blocks.shape[1])
    came = lax.all_to_all(cut, ("section", "dp"), split_axis=0, concat_axis=0, tiled=True)
    return came.reshape(blocks.shape)


def local(
    tokens,
    cotangent,
    segments,
    routes,
    keeps,
    attn_gain,
    moe_gain,
    qkv_weight,
    out_weight,
    router_weight,
    expert_in,
    expert_out,
):
    section = lax.axis_index("section")
    core = lax.axis_index("tensor")
    first = section == 0
    seq_len = segments.shape[1]
    model_width = tokens.shape[1]
    experts = router_weight.shape[2]
    parts = lax.axis_size("dp")
    capacity = max(2, 5 * seq_len // (4 * experts))
    half = capacity // 2
    width = qkv_weight.shape[3]
    share = model_width // parts
    sequences = parts * lax.axis_size("section")
    block = -(-half * (model_width // LANES) // 16) * 16
    tail = 4 * width
    layout = {
        "width": width,
        "tail": tail,
        "experts": experts,
        "half": half,
        "block": block,
        "sequences": sequences,
    }
    packed = tail + LANES
    section_ref = section.reshape(1).astype(jnp.int32)

    (mine,) = call(
        pack_kernel,
        [shape((share, packed), BF16)],
        Far(qkv_weight),
        Far(out_weight.swapaxes(1, 2)),
        Far(router_weight),
        Far(attn_gain),
        Far(moe_gain),
    )
    coded = (routes[0] + experts * keeps[0]).reshape(2, seq_len)
    coded_own = jnp.where(first, coded[0], coded[1])
    coded_other = swap(jnp.where(first, coded[1], coded[0]), "section")
    copies, shard_one = call(
        functools.partial(spread_kernel, parts),
        [shape((parts * share, packed), BF16), shape((share, packed), BF16)],
        mine,
        swap(mine, "section"),
        section_ref,
        After(coded_other),
    )
    dense_zero = lax.all_to_all(
        copies.reshape(parts, share, packed), "dp", split_axis=0, concat_axis=0, tiled=True
    ).reshape(model_width, packed)
    dense_one = lax.all_gather(shard_one, "dp", axis=0, tiled=True)

    half_in = expert_in[0, 0]
    half_out = expert_out[0, 0]
    halves_in = (half_in, swap(half_in, "tensor"))
    halves_out = (half_out, swap(half_out, "tensor"))

    hidden_in = lax.dynamic_slice_in_dim(tokens, section * seq_len, seq_len, 0)
    target = lax.dynamic_slice_in_dim(cotangent, section * seq_len, seq_len, 0)
    seg_row = jnp.where(first, segments[0], segments[1])
    columns, slot_rows = [], []
    for code in (
        jnp.where(first, coded_own, coded_other),
        jnp.where(first, coded_other, coded_own),
    ):
        route, keep = code % experts, code // experts
        index = jnp.arange(seq_len)
        earlier = (route[:, None] == route[None, :]) & (index[:, None] > index[None, :])
        rank = jnp.sum(jnp.where(earlier, keep[None, :], 0), axis=1)
        slot = (rank % half) * experts + route
        kept = keep == 1
        own = jnp.where(kept & (rank // half == core), slot, -1)
        other = jnp.where(kept & (rank // half == 1 - core), slot, -1)
        columns += [own, other, route]
        slot_rows.append(own)
    columns = jnp.stack(columns + [seg_row], axis=1)
    marks = Far(jnp.pad(columns, ((0, 0), (0, LANES - columns.shape[1]))))
    rows = Far(jnp.pad(jnp.stack(slot_rows + [seg_row], axis=0), ((0, 5), (0, 0))))

    rows_shape = (seq_len, model_width)
    far = lambda dims, dtype: Far(shape(dims, dtype))
    wide_rows = far(rows_shape, F32)
    near_rows = shape(rows_shape, F32)
    attend_outs = [
        far((seq_len, 3 * width), BF16),
        far((seq_len, width), BF16),
        far((seq_len, LANES), F32),
        near_rows,
    ]
    gate_shape = far((seq_len, 1), F32)
    slot_scratch = pltpu.VMEM((half * experts, model_width), BF16)
    wide_one = pltpu.VMEM((experts * block, LANES), F32)
    wide_two = pltpu.VMEM((experts * 2 * block, LANES), F32)
    mixed_scratch = pltpu.VMEM((seq_len, width), BF16)
    attn_cost = dict(flops=2 * seq_len * model_width * 5 * width, size=8 << 20)

    def returned(blocks, layer):
        size = blocks.shape[0] // 2
        own = blocks[layer * size : (layer + 1) * size]
        return (own, swap(own, "tensor"))

    qkv_zero, mixed_zero, lse_zero, part = call(
        functools.partial(attend_first_kernel, layout),
        attend_outs,
        Far(hidden_in),
        dense_zero,
        marks,
        rows,
        **attn_cost,
    )
    h1_zero, gate_zero, send = call(
        functools.partial(route_kernel, layout, 0),
        [wide_rows, gate_shape, shape((sequences * block, LANES), BF16)],
        Far(hidden_in),
        part,
        swap(part, "tensor"),
        Far(dense_zero, tail),
        marks,
        rows,
        scratch=[wide_one],
        size=4 << 20,
    )
    send, x_zero = run_experts(
        layout, "forward", exchange(send, sequences), None, halves_in, halves_out
    )
    own, other = returned(exchange(send, sequences), 0)

    layer_zero, back_zero, qkv_one, mixed_one, lse_one, part = call(
        functools.partial(attend_next_kernel, layout),
        [wide_rows, far(rows_shape, BF16)] + attend_outs,
        Far(h1_zero),
        Far(gate_zero),
        own,
        other,
        Far(dense_one),
        marks,
        rows,
        scratch=[wide_one, slot_scratch],
        **attn_cost,
    )
    h1_one, _, send = call(
        functools.partial(route_kernel, layout, 1),
        [wide_rows, gate_shape, shape((2 * sequences * block, LANES), BF16)],
        Far(layer_zero),
        part,
        swap(part, "tensor"),
        Far(dense_one, tail),
        marks,
        rows,
        Far(target),
        scratch=[wide_two],
        size=4 << 20,
    )
    send, x_one, g_one = run_experts(
        layout, "both", exchange(send, sequences), None, halves_in, halves_out
    )
    own, other = returned(exchange(send, sequences), 1)

    layer_one, hidden_grad, part, grad_qkv, small, moe_gain_grad = call(
        functools.partial(backward_kernel, layout, 1),
        [
            wide_rows,
            wide_rows,
            near_rows,
            far((seq_len, 3 * width), BF16),
            far((model_width, LANES), F32),
            far((1, model_width), F32),
        ],
        Far(h1_one),
        own,
        other,
        Far(target),
        Far(dense_one),
        marks,
        rows,
        Far(qkv_one),
        Far(lse_one),
        scratch=[wide_two, slot_scratch, mixed_scratch],
        **attn_cost,
    )
    grad_mid, send = call(
        functools.partial(input_grad_kernel, layout, True),
        [wide_rows, shape((sequences * block, LANES), BF16)],
        part,
        swap(part, "tensor"),
        Far(layer_zero),
        Far(hidden_grad),
        Far(dense_one, tail),
        Far(gate_zero),
        rows,
        scratch=[wide_one],
        size=4 << 20,
    )
    (grads_one,) = call(
        functools.partial(dense_grad_kernel, layout),
        [shape((model_width, packed), BF16)],
        Far(layer_zero),
        Far(dense_one, tail),
        Far(grad_qkv),
        Far(hidden_grad),
        Far(mixed_one),
        part,
        Far(small),
        Far(moe_gain_grad),
        After(send),
        **attn_cost,
    )

    def settle(of_zero, of_one, *after):
        place = jnp.stack([section, core]).astype(jnp.int32)
        kept, going = call(
            settle_kernel,
            [far((seq_len, width), F32), shape((seq_len, width), BF16)],
            place,
            Far(of_zero),
            Far(of_one),
            *after,
        )
        return (kept, swap(going, "section"))

    def join(kept, came, *after):
        (out,) = call(
            join_kernel,
            [far((2 * seq_len, width), F32)],
            section_ref,
            Far(kept),
            came,
            *after,
        )
        return out[None]

    send, g_zero = run_experts(
        layout, "backward", exchange(send, sequences), x_zero, halves_in, halves_out
    )
    layer_pair = settle(layer_zero, layer_one, After(send))
    own, other = returned(exchange(send, sequences), 0)
    hidden_grad, part, grads_zero = call(
        functools.partial(backward_kernel, layout, 0),
        [wide_rows, near_rows, shape((model_width, packed), BF16)],
        Far(h1_zero),
        own,
        other,
        Far(grad_mid),
        Far(dense_zero),
        marks,
        rows,
        Far(qkv_zero),
        Far(lse_zero),
        Far(back_zero),
        Far(mixed_zero),
        Far(hidden_in),
        After(layer_pair[0]),
        scratch=[wide_one, slot_scratch, mixed_scratch, pltpu.VMEM((seq_len, 3 * width), BF16)],
        **attn_cost,
    )
    (grad_first,) = call(
        functools.partial(input_grad_kernel, layout, False),
        [wide_rows],
        part,
        swap(part, "tensor"),
        Far(hidden_in),
        Far(hidden_grad),
        Far(dense_zero, tail),
        size=4 << 20,
    )

    rows_own, grad_rows_own = call(
        choose_kernel,
        [shape(x_zero.shape, BF16)] * 2,
        section_ref,
        Far(x_zero),
        Far(x_one),
        Far(g_zero),
        Far(g_one),
        After(grads_zero),
    )
    expert_in_grad, expert_out_grad = expert_weight_grads(
        rows_own,
        swap(rows_own, "tensor"),
        grad_rows_own,
        swap(grad_rows_own, "tensor"),
        half_in,
        half_out,
    )

    def spread(grads):
        cut = grads.reshape(parts, share, packed)
        pieces = lax.all_to_all(cut, "dp", split_axis=0, concat_axis=0, tiled=True)
        return pieces.reshape(model_width, packed)

    (sum_one,) = call(
        functools.partial(sum_one_kernel, parts), [far((share, packed), F32)], spread(grads_one)
    )
    grad_pair = settle(grad_first, grad_mid)
    mine, going = call(
        functools.partial(sum_both_kernel, parts),
        [shape((share, packed), F32), shape((share, packed), F32)],
        section_ref,
        spread(grads_zero),
        Far(sum_one),
        After(expert_in_grad),
        After(grad_pair[0]),
        scratch=[pltpu.VMEM((share, packed), F32)],
    )
    diagonal = [(i, 3 - i) for i in range(4)]
    qkv_grad, out_grad, router_grad, attn_gain_grad, moe_gain_grad = call(
        functools.partial(finish_kernel, layout),
        [
            shape((3, share, width), F32),
            shape((share, width), F32),
            shape((share, experts), F32),
            shape((1, share), F32),
            shape((1, share), F32),
        ],
        mine,
        swap(going, "section"),
        swap(mine[:, tail:], "tensor"),
        lax.ppermute(going[:, tail:], ("section", "tensor"), diagonal),
    )

    layer_outputs = join(*layer_pair, After(mine))
    input_grads = join(*grad_pair, After(mine))

    return (
        layer_outputs,
        input_grads,
        attn_gain_grad,
        moe_gain_grad,
        qkv_grad[None],
        out_grad.T[None],
        router_grad[None],
        expert_in_grad[None, None],
        expert_out_grad[None, None],
    )


def solution(mesh):
    placed = (
        P("dp", None),
        P("dp", None),
        P("dp", None),
        P("section", "dp"),
        P("section", "dp"),
        P("section", "dp"),
        P("section", "dp"),
        P("section", None, "dp", "tensor"),
        P("section", "tensor", "dp"),
        P("section", "dp", None),
        P("section", "dp", None, "tensor"),
        P("section", "dp", "tensor", None),
    )
    return jax.shard_map(
        local,
        mesh=mesh,
        in_specs=placed,
        out_specs=(
            P("section", "dp", "tensor"),
            P("section", "dp", "tensor"),
            P("section", "dp"),
            P("section", "dp"),
            P("section", None, "dp", "tensor"),
            P("section", "tensor", "dp"),
            P("section", "dp", None),
            P("section", "dp", None, "tensor"),
            P("section", "dp", "tensor", None),
        ),
        check_vma=False,
    )
```

```python
import functools

import jax
import jax.numpy as jnp
from jax import lax
from jax.experimental import pallas as pl
from jax.experimental.pallas import tpu as pltpu
from jax.sharding import PartitionSpec as P

HEAD_DIM = 64
EPS = 1e-06
MASK_FILL = -1e30
LANES = 128

F32 = jnp.float32
BF16 = jnp.bfloat16


def swap(value, axis):
    return lax.ppermute(value, axis, [(0, 1), (1, 0)])


def dot(left, right, left_dim, right_dim):
    return lax.dot_general(
        left, right, (((left_dim,), (right_dim,)), ((), ())), preferred_element_type=F32
    )


def unpack_rows(block_ref, wide_ref, rows_ref, base, per, half):
    count = block_ref.shape[0] // per
    wide_ref[...] = block_ref[...].astype(F32)
    for c in range(half):
        for j in range(rows_ref.shape[1] // LANES):
            piece = wide_ref[pl.ds(base + j * half + c, count, stride=per), :]
            rows_ref[c * count : (c + 1) * count, j * LANES : (j + 1) * LANES] = piece.astype(BF16)


def pack_rows(rows, wide_ref, base, per, half):
    count = rows.shape[0] // half
    for c in range(half):
        for j in range(rows.shape[1] // LANES):
            wide_ref[pl.ds(base + j * half + c, count, stride=per), :] = rows[
                c * count : (c + 1) * count, j * LANES : (j + 1) * LANES
            ]


def mean_of(values):
    return jnp.sum(values, axis=-1, keepdims=True) * (1.0 / values.shape[-1])


def norm_parts(rows):
    inv_scale = lax.rsqrt(mean_of(rows * rows) + EPS)
    return (inv_scale, rows * inv_scale)


def norm_back(grad_out, inv_scale, normed, gain_row):
    grad_normed = grad_out * gain_row
    gain_grad = jnp.sum(grad_out * normed, axis=0, keepdims=True)
    return (inv_scale * (grad_normed - normed * mean_of(grad_normed * normed)), gain_grad)


def tail_rows(tail_ref):
    return tail_ref[...].astype(F32).T


def one_hot_columns(slot_col, count):
    return (slot_col == lax.broadcasted_iota(jnp.int32, (slot_col.shape[0], count), 1)).astype(BF16)


def one_hot_rows(slot_row, count):
    return (slot_row == lax.broadcasted_iota(jnp.int32, (count, slot_row.shape[1]), 0)).astype(BF16)


class Staged:
    def __init__(self, ref, copy=None):
        self.ref, self.copy, self.waited, self.started = ref, copy, False, False

    def start(self):
        if self.copy is not None and not self.started:
            self.copy.start()
            self.started = True

    def __call__(self):
        if self.copy is not None and not self.waited:
            self.copy.wait()
            self.waited = True
        return self.ref

    def put(self, value):
        self.ref[...] = value
        self.start()


def shape(dims, dtype):
    return jax.ShapeDtypeStruct(dims, dtype)


class After:
    def __init__(self, what):
        self.what = what


class Far:
    def __init__(self, what, lane=0):
        self.what, self.lane = what, lane


def staged_kernel(kernel, ins, outs, scratch_count, *refs):
    count = len(ins) + len(outs)
    rest = list(refs[count:])
    scratch, rest = rest[:scratch_count], rest[scratch_count:]
    far = [item for item in list(ins) + list(outs) if isinstance(item, Far)]
    rooms, sems = rest[: len(far)], rest[len(far)] if far else None
    staged = []
    index = 0
    for place, (item, ref) in enumerate(zip(list(ins) + list(outs), refs)):
        if isinstance(item, After):
            continue
        if not isinstance(item, Far):
            staged.append(Staged(ref))
            continue
        if place < len(ins):
            source = ref if item.lane == 0 else ref.at[:, item.lane :]
            copy = pltpu.make_async_copy(source, rooms[index], sems.at[index])
        else:
            copy = pltpu.make_async_copy(rooms[index], ref, sems.at[index])
        staged.append(Staged(rooms[index], copy))
        index += 1
    given = sum(not isinstance(item, After) for item in ins)
    for item in staged[:given]:
        item.start()
    kernel(*staged, *scratch)
    for item in staged[:given]:
        item()
    for item in staged[given:]:
        item.start()
    for item in staged[given:]:
        item()


def call(kernel, outs, *ins, scratch=(), flops=0, size=0):
    far = [item for item in list(ins) + list(outs) if isinstance(item, Far)]
    rooms = [
        pltpu.VMEM(item.what.shape[:-1] + (item.what.shape[-1] - item.lane,), item.what.dtype)
        for item in far
    ]
    if far:
        rooms.append(pltpu.SemaphoreType.DMA((len(far),)))

    def spec(item):
        if isinstance(item, (Far, After)):
            return pl.BlockSpec(memory_space=pl.ANY)
        return pl.BlockSpec(memory_space=pltpu.SMEM if len(item.shape) == 1 else pltpu.VMEM)


    def operand(item):
        if isinstance(item, (Far, After)):
            return pltpu.with_memory_space_constraint(item.what, pltpu.HBM)
        return item

    args = [operand(item) for item in ins]
    shapes = [
        pltpu.HBM(item.what.shape, item.what.dtype) if isinstance(item, Far) else item
        for item in outs
    ]
    return pl.pallas_call(
        functools.partial(staged_kernel, kernel, ins, outs, len(scratch)),
        out_shape=shapes,
        in_specs=[spec(item) for item in ins],
        out_specs=[spec(item) for item in outs],
        scratch_shapes=list(scratch) + rooms,
        compiler_params=pltpu.CompilerParams(vmem_limit_bytes=24 << 20),
        cost_estimate=pl.CostEstimate(flops=flops, bytes_accessed=size, transcendentals=0),
    )(*args)


def pack_kernel(qkv, out, router, attn_gain, moe_gain, mine):
    to = mine.ref
    share = router()[0].shape[0]
    width = qkv()[0, 0].shape[1]
    experts = router()[0].shape[1]
    for c in range(3):
        to[:, c * width : (c + 1) * width] = qkv()[0, c]
    row = lax.broadcasted_iota(jnp.int32, (share, share), 0)
    lane = lax.broadcasted_iota(jnp.int32, (share, share), 1)
    eye = row == lane
    to[:, 3 * width : 4 * width] = out()[0]
    to[:, 4 * width :] = jnp.zeros((share, LANES), BF16)
    to[:, 4 * width : 4 * width + experts] = router()[0]
    for index, gain in enumerate((attn_gain, moe_gain)):
        spread = jnp.where(eye, jnp.broadcast_to(gain()[...].astype(F32), (share, share)), 0.0)
        at = 4 * width + experts + index
        to[:, at : at + 1] = jnp.sum(spread, axis=1, keepdims=True).astype(BF16)


def spread_kernel(parts, mine, theirs, section, copies, other):
    share = mine().shape[0]
    first = section()[0] == 0
    own, came = mine()[...].astype(F32), theirs()[...].astype(F32)
    zero = jnp.where(first, own, came)
    other.ref[...] = jnp.where(first, came, own).astype(BF16)
    several = 2
    block = jnp.concatenate([zero] * several, axis=0).astype(BF16)
    for part in range(parts // several):
        copies.ref[part * several * share : (part + 1) * several * share] = block


def attend(hidden, weight, layout, marks, rows, qkv, mixed, lse, part):
    width = layout["width"]
    weight_ref = weight()
    turned = tail_rows(weight_ref.at[:, layout["tail"] :])
    attn_gain = turned[layout["experts"] : layout["experts"] + 1]
    _, normed = norm_parts(hidden)
    low = (normed * attn_gain).astype(BF16)
    qkv.put(dot(low, weight_ref[:, : 3 * width], 1, 0).astype(BF16))
    same = marks()[:, 6:7] == rows()[2:3]
    for head in range(width // HEAD_DIM):
        at = head * HEAD_DIM
        queries = qkv.ref[:, at : at + HEAD_DIM]
        keys = qkv.ref[:, width + at : width + at + HEAD_DIM]
        values = qkv.ref[:, 2 * width + at : 2 * width + at + HEAD_DIM]
        scores = dot(queries, keys, 1, 1) * HEAD_DIM ** (-0.5)
        scores = jnp.where(same, scores, MASK_FILL)
        top = jnp.max(scores, axis=-1, keepdims=True)
        exponent = jnp.exp(scores - top)
        total = jnp.sum(exponent, axis=-1, keepdims=True)
        soft = (exponent * (1.0 / total)).astype(BF16)
        mixed.ref[:, at : at + HEAD_DIM] = dot(soft, values, 1, 0).astype(BF16)
        lse.ref[:, head : head + 1] = top + jnp.log(total)
    mixed.start()
    lse.start()
    part.ref[...] = dot(mixed.ref[...], weight_ref[:, 3 * width : 4 * width], 1, 1)


def attend_first_kernel(layout, hidden, weight, marks, rows, *outs):
    attend(hidden()[...].astype(F32), weight, layout, marks, rows, *outs)


def attend_next_kernel(
    layout, hidden, gate, block_own, block_other, weight, marks, rows, layer, back, qkv, mixed, lse, part, wide_ref, rows_ref
):
    returned = gather_back(layout, block_own(), block_other(), marks, 0, wide_ref, rows_ref, 0)
    back.put(returned.astype(BF16))
    layer.put(hidden()[...] + gate()[...] * returned)
    attend(layer.ref[...], weight, layout, marks, rows, qkv, mixed, lse, part)


def gather_back(layout, block_own, block_other, marks, layer, wide_ref, rows_ref, base):
    half = layout["half"]
    per = block_own.shape[0] // layout["experts"]
    count = rows_ref.shape[0]
    total = 0.0
    for which, block in enumerate((block_own, block_other)):
        at = 3 * layer + which
        unpack_rows(block, wide_ref, rows_ref, base, per, half)
        total = total + dot(
            one_hot_columns(marks()[:, at : at + 1], count), rows_ref[...], 1, 0
        )
    return total


def send_slots(layout, slot_row, pieces, wide_ref, out_ref):
    half, experts = layout["half"], layout["experts"]
    per = wide_ref.shape[0] // experts
    placed = one_hot_rows(slot_row, half * experts)
    wide_ref[...] = jnp.zeros_like(wide_ref)
    for index, piece in enumerate(pieces):
        pack_rows(dot(placed, piece, 1, 0), wide_ref, index * layout["block"], per, half)
    low = wide_ref[...].astype(BF16)
    size = wide_ref.shape[0]
    out_ref[:size] = low
    out_ref[size:] = low


def router_parts(layout, layer, hidden, tail_ref, marks):
    experts = layout["experts"]
    moe_gain = tail_rows(tail_ref)[experts + 1 : experts + 2]
    inv_scale, normed = norm_parts(hidden)
    low = (normed * moe_gain).astype(BF16)
    logits = dot(low, tail_ref[...], 1, 0)
    lane = lax.broadcasted_iota(jnp.int32, logits.shape, 1)
    logits = jnp.where(lane < experts, logits, MASK_FILL)
    exponent = jnp.exp(logits - jnp.max(logits, axis=-1, keepdims=True))
    prob = exponent * (1.0 / jnp.sum(exponent, axis=-1, keepdims=True))
    at = 3 * layer + 2
    chosen = lane == marks()[:, at : at + 1]
    gate = jnp.sum(jnp.where(chosen, prob, 0.0), axis=-1, keepdims=True)
    return (inv_scale, normed, moe_gain, low, prob, chosen.astype(F32), gate)


def route_kernel(layout, layer, hidden_in, part_own, part_other, tail, marks, rows, *rest):
    if layer == 1:
        target, h1, gate_out, send, wide_ref = rest
    else:
        h1, gate_out, send, wide_ref = rest
    hidden = hidden_in()[...].astype(F32) + (part_own()[...] + part_other()[...])
    h1.put(hidden)
    _, _, _, low, _, _, gate = router_parts(layout, layer, hidden, tail(), marks)
    gate_out.put(gate)
    pieces = [low]
    if layer == 1:
        pieces.append((gate * target()[...].astype(F32)).astype(BF16))
    send_slots(layout, rows()[layer : layer + 1], pieces, wide_ref, send.ref)


def backward_kernel(layout, layer, h1, block_own, block_other, grad, weight, marks, rows, qkv, lse, *rest):
    if layer == 1:
        layer_out, hidden_grad, part, grad_qkv, small, moe_gain_grad = rest[:6]
        rest = rest[6:]
    else:
        returned_in, mixed_in, layer_in, hidden_grad, part, dense_out = rest[:6]
        rest = rest[6:]
    wide_ref, rows_ref, mixed_ref = rest[:3]
    grad_qkv_ref = grad_qkv.ref if layer == 1 else rest[3]
    width = layout["width"]
    experts = layout["experts"]
    scaling = HEAD_DIM ** (-0.5)
    grad_out = grad()[...].astype(F32)
    hidden = h1()[...]
    weight_ref = weight()
    tail_ref = weight_ref.at[:, layout["tail"] :]
    inv_scale, normed, moe_gain, moe, prob, chosen, gate = router_parts(
        layout, layer, hidden, tail_ref, marks
    )
    own, other = block_own(), block_other()
    if layer == 1:
        returned = gather_back(layout, own, other, marks, layer, wide_ref, rows_ref, 0)
        layer_out.put(hidden + gate * returned)
    else:
        returned = returned_in()[...].astype(F32)
    base = layout["block"] if layer == 1 else 0
    grad_back = gather_back(layout, own, other, marks, layer, wide_ref, rows_ref, base)
    grad_gate = jnp.sum(grad_out * returned, axis=-1, keepdims=True)
    grad_logits = (grad_gate * gate * (chosen - prob)).astype(BF16)
    router_grad = dot(moe, grad_logits, 0, 0)
    grad_moe = grad_back + dot(grad_logits, tail_ref[...], 1, 1)
    grad_norm, gain_grad = norm_back(grad_moe, inv_scale, normed, moe_gain)
    if layer == 1:
        small.put(router_grad)
        moe_gain_grad.put(gain_grad)
    grad_hidden = grad_out + grad_norm
    hidden_grad.put(grad_hidden)
    mixed_ref[...] = dot(
        grad_hidden.astype(BF16), weight_ref[:, 3 * width : 4 * width], 1, 0
    ).astype(BF16)
    same = marks()[:, 6:7] == rows()[2:3]
    qkv_ref, lse_ref = qkv(), lse()
    for head in range(width // HEAD_DIM):
        at = head * HEAD_DIM
        queries = qkv_ref[:, at : at + HEAD_DIM]
        keys = qkv_ref[:, width + at : width + at + HEAD_DIM]
        values = qkv_ref[:, 2 * width + at : 2 * width + at + HEAD_DIM]
        grad_mixed = mixed_ref[:, at : at + HEAD_DIM]
        scores = dot(queries, keys, 1, 1) * scaling
        soft = jnp.exp(jnp.where(same, scores - lse_ref[:, head : head + 1], MASK_FILL))
        grad_soft = dot(grad_mixed, values, 1, 1)
        delta = jnp.sum(soft * grad_soft, axis=-1, keepdims=True)
        grad_scores = (soft * (grad_soft - delta)).astype(BF16)
        grad_qkv_ref[:, at : at + HEAD_DIM] = (dot(grad_scores, keys, 1, 0) * scaling).astype(BF16)
        grad_qkv_ref[:, width + at : width + at + HEAD_DIM] = (
            dot(grad_scores, queries, 0, 0) * scaling
        ).astype(BF16)
        grad_qkv_ref[:, 2 * width + at : 2 * width + at + HEAD_DIM] = dot(
            soft.astype(BF16), grad_mixed, 0, 0
        ).astype(BF16)
    if layer == 1:
        grad_qkv.start()
    part.ref[...] = dot(grad_qkv_ref[...], weight_ref[:, : 3 * width], 1, 1)
    if layer == 0:
        dense_grads(
            layout,
            layer_in()[...].astype(F32),
            tail_ref,
            grad_qkv_ref,
            grad_hidden,
            mixed_in(),
            part.ref,
            router_grad,
            gain_grad,
            dense_out.ref,
        )


def dense_grads(
    layout, layer_in, tail_ref, grad_qkv_ref, grad_hidden, mixed_ref, part_ref, router_grad, moe_gain_grad, out_ref
):
    width = layout["width"]
    experts = layout["experts"]
    _, normed = norm_parts(layer_in)
    attn_gain = tail_rows(tail_ref)[experts : experts + 1]
    low = (normed * attn_gain).astype(BF16)
    out_ref[:, : 3 * width] = dot(low, grad_qkv_ref[...], 0, 0).astype(BF16)
    out_ref[:, 3 * width : 4 * width] = dot(
        grad_hidden.astype(BF16), mixed_ref[...], 0, 0
    ).astype(BF16)
    attn_gain_grad = jnp.sum(part_ref[...] * normed, axis=0, keepdims=True)
    lane = lax.broadcasted_iota(jnp.int32, router_grad.shape, 1)
    size = router_grad.shape[0]
    attn_col = jnp.broadcast_to(attn_gain_grad, (LANES, size)).T
    moe_col = jnp.broadcast_to(moe_gain_grad, (LANES, size)).T
    small = jnp.where(lane == experts, attn_col, router_grad)
    small = jnp.where(lane == experts + 1, moe_col, small)
    out_ref[:, 4 * width : 4 * width + LANES] = small.astype(BF16)


def dense_grad_kernel(
    layout, layer_in, tail, grad_qkv, hidden_grad, mixed, part, small, moe_gain_grad, out
):
    dense_grads(
        layout,
        layer_in()[...],
        tail(),
        grad_qkv(),
        hidden_grad()[...],
        mixed(),
        part(),
        small()[...],
        moe_gain_grad()[...],
        out.ref,
    )


def choose_kernel(section, *refs):
    half = len(refs) // 3
    ins, outs = refs[: 2 * half], refs[2 * half :]
    first = section()[0] == 0
    for index, out in enumerate(outs):
        zero, one = ins[2 * index]()[...], ins[2 * index + 1]()[...]
        out.put(jnp.where(first, zero.astype(F32), one.astype(F32)).astype(out.ref.dtype))


def settle_kernel(place, zero, one, kept, going):
    first = place()[0] == 0
    width = kept.ref.shape[1]
    left = place()[1] == 0
    of_zero = jnp.where(left, zero()[:, :width], zero()[:, width:])
    of_one = jnp.where(left, one()[:, :width], one()[:, width:])
    going.put(jnp.where(first, of_one, of_zero).astype(BF16))
    kept.put(jnp.where(first, of_zero, of_one))


def join_kernel(section, kept, came, out):
    count = kept().shape[0]
    first = section()[0] == 0
    arrived = came()[...].astype(F32)
    out.ref[:count] = jnp.where(first, kept()[...], arrived)
    out.ref[count:] = jnp.where(first, arrived, kept()[...])
    out.start()


def input_grad_kernel(layout, send, part_own, part_other, layer_in, hidden_grad, tail, *rest):
    experts = layout["experts"]
    attn_gain = tail_rows(tail())[experts : experts + 1]
    inv_scale, normed = norm_parts(layer_in()[...].astype(F32))
    grad_norm, _ = norm_back(part_own()[...] + part_other()[...], inv_scale, normed, attn_gain)
    grad_in = hidden_grad()[...] + grad_norm
    if send:
        gate, rows, grad, send_out, wide_ref = rest
        grad.put(grad_in)
        pieces = [(gate()[...] * grad_in).astype(BF16)]
        send_slots(layout, rows()[0:1], pieces, wide_ref, send_out.ref)
    else:
        (grad,) = rest
        grad.put(grad_in)


def sum_pieces(pieces, total, parts):
    share, cols = total.shape
    pair = 2 * share
    for at in range(0, cols, LANES):
        value = pieces[:pair, at : at + LANES].astype(F32)
        for part in range(1, parts // 2):
            value = value + pieces[part * pair : (part + 1) * pair, at : at + LANES].astype(F32)
        total[:, at : at + LANES] = value[:share] + value[share:]


def sum_one_kernel(parts, pieces, total):
    sum_pieces(pieces(), total.ref, parts)


def sum_both_kernel(parts, section, pieces, one, mine, going, wide_ref):
    sum_pieces(pieces(), wide_ref, parts)
    first = section()[0] == 0
    zero, one = wide_ref[...], one()[...]
    mine.ref[...] = jnp.where(first, zero, one)
    going.ref[...] = jnp.where(first, one, zero)


def finish_kernel(layout, mine, theirs, core, across, qkv, out, router, attn_gain, moe_gain):
    width, experts = layout["width"], layout["experts"]
    whole = mine()[...] + theirs()[...]
    small = whole[:, 4 * width :]
    lane = lax.broadcasted_iota(jnp.int32, small.shape, 1)
    small = small + jnp.where(lane == experts, core()[...] + across()[...], 0.0)
    for c in range(3):
        qkv.ref[c] = whole[:, c * width : (c + 1) * width]
    out.ref[...] = whole[:, 3 * width : 4 * width]
    router.ref[...] = small[:, :experts]
    share = small.shape[0]
    turned = jnp.concatenate([small, jnp.zeros((LANES - share, LANES), F32)], axis=0).T
    attn_gain.ref[...] = turned[experts : experts + 1, :share]
    moe_gain.ref[...] = turned[experts + 1 : experts + 2, :share]


GELU_SCALE = 0.7978845608028654
GELU_CUBE = 0.044715


def gelu_parts(values):
    square = values * values
    bend = jnp.tanh(GELU_SCALE * (values + GELU_CUBE * (values * square)))
    return (square, bend)


def gelu_of(values, bend):
    return 0.5 * values * (1.0 + bend)


def gelu_slope(values, square, bend):
    inner = GELU_SCALE * (1.0 + 3.0 * GELU_CUBE * square)
    return 0.5 * (1.0 + bend) + 0.5 * values * (1.0 - bend * bend) * inner


def expert_kernel(layout, mode, *refs):
    half = layout["half"]
    step = pl.program_id(0)
    block_ref, refs = refs[0], refs[1:]
    if mode == "backward":
        x_ref, refs = refs[0], refs[1:]
    in_a, in_b, out_a, out_b = refs[:4]
    refs = refs[4:]
    if mode == "forward":
        send_ref, x_ref, wide_ref, y_acc = refs
    elif mode == "both":
        send_ref, x_ref, g_ref, wide_ref, y_acc, dx_acc = refs
    else:
        send_ref, g_ref, wide_ref, dx_acc = refs
    per = block_ref.shape[0] // layout["sequences"]

    @pl.when(step == 0)
    def _():
        if mode != "backward":
            unpack_rows(block_ref, wide_ref, x_ref, 0, per, half)
            y_acc[...] = jnp.zeros_like(y_acc)
        if mode != "forward":
            unpack_rows(
                block_ref, wide_ref, g_ref, layout["block"] if mode == "both" else 0, per, half
            )
            dx_acc[...] = jnp.zeros_like(dx_acc)

    rows = x_ref[...]
    y_sum, dx_sum = 0.0, 0.0
    for w_in, w_out in ((in_a, out_a), (in_b, out_b)):
        hidden = dot(rows, w_in[...], 1, 0)
        square, bend = gelu_parts(hidden)
        if mode != "backward":
            y_sum = y_sum + dot(gelu_of(hidden, bend).astype(BF16), w_out[...], 1, 0)
        if mode != "forward":
            grad_act = dot(g_ref[...], w_out[...], 1, 1)
            grad_pre = (grad_act * gelu_slope(hidden, square, bend)).astype(BF16)
            dx_sum = dx_sum + dot(grad_pre, w_in[...], 1, 1)
    if mode != "backward":
        y_acc[...] += y_sum
    if mode != "forward":
        dx_acc[...] += dx_sum

    @pl.when(step == pl.num_programs(0) - 1)
    def _():
        wide_ref[...] = jnp.zeros_like(wide_ref)
        if mode != "backward":
            pack_rows(y_acc[...], wide_ref, 0, per, half)
        if mode != "forward":
            pack_rows(dx_acc[...], wide_ref, layout["block"] if mode == "both" else 0, per, half)
        send_ref[...] = wide_ref[...].astype(BF16)


def run_experts(layout, mode, block, x_rows, halves_in, halves_out):
    rows = layout["half"] * layout["sequences"]
    width, hidden = halves_in[0].shape
    chunk = 768
    whole = lambda array: pl.BlockSpec(array.shape, lambda i: (0, 0))
    args, specs = [block], [whole(block)]
    if mode == "backward":
        args.append(pltpu.with_memory_space_constraint(x_rows, pltpu.HBM))
        specs.append(whole(x_rows))
    args += [pltpu.with_memory_space_constraint(w, pltpu.HBM) for w in (*halves_in, *halves_out)]
    specs += [pl.BlockSpec((width, chunk), lambda i: (0, i))] * 2
    specs += [pl.BlockSpec((chunk, width), lambda i: (i, 0))] * 2
    outs = [shape(block.shape, BF16)]
    row_far = pltpu.HBM((rows, width), BF16)
    if mode != "backward":
        outs.append(row_far)
    if mode != "forward":
        outs.append(row_far)
    scratch = [pltpu.VMEM(block.shape, F32), pltpu.VMEM((rows, width), F32)]
    if mode == "both":
        scratch.append(pltpu.VMEM((rows, width), F32))
    passes = {"forward": 4, "both": 8, "backward": 6}[mode]
    return pl.pallas_call(
        functools.partial(expert_kernel, layout, mode),
        grid=(hidden // chunk,),
        in_specs=specs,
        out_specs=[whole(out) for out in outs],
        out_shape=outs,
        scratch_shapes=scratch,
        compiler_params=pltpu.CompilerParams(
            vmem_limit_bytes=24 << 20, dimension_semantics=("arbitrary",)
        ),
        cost_estimate=pl.CostEstimate(
            flops=2 * passes * rows * width * hidden, bytes_accessed=8 * width * hidden, transcendentals=0
        ),
    )(*args)


def expert_grad_kernel(rows_own, rows_other, grad_own, grad_other, w_in, w_out, grad_in, grad_out, x_ref, g_ref):
    size = rows_own.shape[0]

    @pl.when(pl.program_id(0) == 0)
    def _():
        x_ref[:size] = rows_own[...]
        x_ref[size:] = rows_other[...]
        g_ref[:size] = grad_own[...]
        g_ref[size:] = grad_other[...]

    hidden = dot(x_ref[...], w_in[...], 1, 0)
    square, bend = gelu_parts(hidden)
    grad_act = dot(g_ref[...], w_out[...], 1, 1)
    grad_pre = (grad_act * gelu_slope(hidden, square, bend)).astype(BF16)
    grad_in[...] = dot(x_ref[...], grad_pre, 0, 0)
    grad_out[...] = dot(gelu_of(hidden, bend).astype(BF16), g_ref[...], 0, 0)


def expert_weight_grads(rows_own, rows_other, grad_own, grad_other, half_in, half_out):
    size, width = rows_own.shape
    hidden = half_in.shape[1]
    chunk = 256
    whole = pl.BlockSpec((size, width), lambda i: (0, 0))
    by_in = pl.BlockSpec((width, chunk), lambda i: (0, i))
    by_out = pl.BlockSpec((chunk, width), lambda i: (i, 0))
    pin = lambda array: pltpu.with_memory_space_constraint(array, pltpu.HBM)
    return pl.pallas_call(
        expert_grad_kernel,
        grid=(hidden // chunk,),
        in_specs=[whole] * 4 + [by_in, by_out],
        out_specs=[by_in, by_out],
        out_shape=[pltpu.HBM((width, hidden), F32), pltpu.HBM((hidden, width), F32)],
        scratch_shapes=[pltpu.VMEM((2 * size, width), BF16)] * 2,
        compiler_params=pltpu.CompilerParams(
            vmem_limit_bytes=24 << 20, dimension_semantics=("arbitrary",)
        ),
        cost_estimate=pl.CostEstimate(
            flops=16 * size * width * hidden, bytes_accessed=12 * width * hidden, transcendentals=0
        ),
    )(rows_own, rows_other, grad_own, grad_other, pin(half_in), pin(half_out))


def exchange(blocks, sequences):
    cut = blocks.reshape(sequences, -1, blocks.shape[1])
    came = lax.all_to_all(cut, ("section", "dp"), split_axis=0, concat_axis=0, tiled=True)
    return came.reshape(blocks.shape)


def local(
    tokens,
    cotangent,
    segments,
    routes,
    keeps,
    attn_gain,
    moe_gain,
    qkv_weight,
    out_weight,
    router_weight,
    expert_in,
    expert_out,
):
    section = lax.axis_index("section")
    core = lax.axis_index("tensor")
    first = section == 0
    seq_len = segments.shape[1]
    model_width = tokens.shape[1]
    experts = router_weight.shape[2]
    parts = lax.axis_size("dp")
    capacity = max(2, 5 * seq_len // (4 * experts))
    half = capacity // 2
    width = qkv_weight.shape[3]
    share = model_width // parts
    sequences = parts * lax.axis_size("section")
    block = -(-half * (model_width // LANES) // 16) * 16
    tail = 4 * width
    layout = {
        "width": width,
        "tail": tail,
        "experts": experts,
        "half": half,
        "block": block,
        "sequences": sequences,
    }
    packed = tail + LANES
    section_ref = section.reshape(1).astype(jnp.int32)

    far = lambda dims, dtype: Far(shape(dims, dtype))

    (mine,) = call(
        pack_kernel,
        [shape((share, packed), BF16)],
        Far(qkv_weight),
        Far(out_weight.swapaxes(1, 2)),
        Far(router_weight),
        Far(attn_gain),
        Far(moe_gain),
    )
    coded = (routes[0] + experts * keeps[0]).reshape(2, seq_len)
    coded_own = jnp.where(first, coded[0], coded[1])
    coded_other = swap(jnp.where(first, coded[1], coded[0]), "section")
    copies, shard_one = call(
        functools.partial(spread_kernel, parts),
        [far((parts * share, packed), BF16), shape((share, packed), BF16)],
        mine,
        swap(mine, "section"),
        section_ref,
        After(coded_other),
    )
    dense_zero = lax.all_to_all(
        copies.reshape(parts, share, packed), "dp", split_axis=0, concat_axis=0, tiled=True
    ).reshape(model_width, packed)
    dense_one = lax.all_gather(shard_one, "dp", axis=0, tiled=True)

    half_in = expert_in[0, 0]
    half_out = expert_out[0, 0]
    halves_in = (half_in, swap(half_in, "tensor"))
    halves_out = (half_out, swap(half_out, "tensor"))

    hidden_in = lax.dynamic_slice_in_dim(tokens, section * seq_len, seq_len, 0)
    target = lax.dynamic_slice_in_dim(cotangent, section * seq_len, seq_len, 0)
    seg_row = jnp.where(first, segments[0], segments[1])
    columns, slot_rows = [], []
    for code in (
        jnp.where(first, coded_own, coded_other),
        jnp.where(first, coded_other, coded_own),
    ):
        route, keep = code % experts, code // experts
        index = jnp.arange(seq_len)
        earlier = (route[:, None] == route[None, :]) & (index[:, None] > index[None, :])
        rank = jnp.sum(jnp.where(earlier, keep[None, :], 0), axis=1)
        slot = (rank % half) * experts + route
        kept = keep == 1
        own = jnp.where(kept & (rank // half == core), slot, -1)
        other = jnp.where(kept & (rank // half == 1 - core), slot, -1)
        columns += [own, other, route]
        slot_rows.append(own)
    columns = jnp.stack(columns + [seg_row], axis=1)
    marks = Far(jnp.pad(columns, ((0, 0), (0, LANES - columns.shape[1]))))
    rows = Far(jnp.pad(jnp.stack(slot_rows + [seg_row], axis=0), ((0, 5), (0, 0))))

    rows_shape = (seq_len, model_width)
    wide_rows = far(rows_shape, F32)
    near_rows = shape(rows_shape, F32)
    attend_outs = [
        far((seq_len, 3 * width), BF16),
        far((seq_len, width), BF16),
        far((seq_len, LANES), F32),
        near_rows,
    ]
    gate_shape = far((seq_len, 1), F32)
    slot_scratch = pltpu.VMEM((half * experts, model_width), BF16)
    wide_one = pltpu.VMEM((experts * block, LANES), F32)
    wide_two = pltpu.VMEM((experts * 2 * block, LANES), F32)
    mixed_scratch = pltpu.VMEM((seq_len, width), BF16)
    attn_cost = dict(flops=2 * seq_len * model_width * 5 * width, size=8 << 20)

    def returned(blocks, layer):
        size = blocks.shape[0] // 2
        own = blocks[layer * size : (layer + 1) * size]
        return (own, swap(own, "tensor"))

    qkv_zero, mixed_zero, lse_zero, part = call(
        functools.partial(attend_first_kernel, layout),
        attend_outs,
        Far(hidden_in),
        dense_zero,
        marks,
        rows,
        **attn_cost,
    )
    h1_zero, gate_zero, send = call(
        functools.partial(route_kernel, layout, 0),
        [wide_rows, gate_shape, shape((sequences * block, LANES), BF16)],
        Far(hidden_in),
        part,
        swap(part, "tensor"),
        Far(dense_zero, tail),
        marks,
        rows,
        scratch=[wide_one],
        size=4 << 20,
    )
    send, x_zero = run_experts(
        layout, "forward", exchange(send, sequences), None, halves_in, halves_out
    )
    own, other = returned(exchange(send, sequences), 0)

    layer_zero, back_zero, qkv_one, mixed_one, lse_one, part = call(
        functools.partial(attend_next_kernel, layout),
        [wide_rows, far(rows_shape, BF16)] + attend_outs,
        Far(h1_zero),
        Far(gate_zero),
        own,
        other,
        Far(dense_one),
        marks,
        rows,
        scratch=[wide_one, slot_scratch],
        **attn_cost,
    )
    h1_one, _, send = call(
        functools.partial(route_kernel, layout, 1),
        [wide_rows, gate_shape, shape((2 * sequences * block, LANES), BF16)],
        Far(layer_zero),
        part,
        swap(part, "tensor"),
        Far(dense_one, tail),
        marks,
        rows,
        Far(target),
        scratch=[wide_two],
        size=4 << 20,
    )
    send, x_one, g_one = run_experts(
        layout, "both", exchange(send, sequences), None, halves_in, halves_out
    )
    own, other = returned(exchange(send, sequences), 1)

    layer_one, hidden_grad_one, part_one, grad_qkv_one, small_one, moe_gain_one = call(
        functools.partial(backward_kernel, layout, 1),
        [
            wide_rows,
            wide_rows,
            near_rows,
            far((seq_len, 3 * width), BF16),
            far((model_width, LANES), F32),
            far((1, model_width), F32),
        ],
        Far(h1_one),
        own,
        other,
        Far(target),
        Far(dense_one),
        marks,
        rows,
        Far(qkv_one),
        Far(lse_one),
        scratch=[wide_two, slot_scratch, mixed_scratch],
        **attn_cost,
    )
    grad_mid, send = call(
        functools.partial(input_grad_kernel, layout, True),
        [wide_rows, shape((sequences * block, LANES), BF16)],
        part_one,
        swap(part_one, "tensor"),
        Far(layer_zero),
        Far(hidden_grad_one),
        Far(dense_one, tail),
        Far(gate_zero),
        rows,
        scratch=[wide_one],
        size=4 << 20,
    )
    def settle(of_zero, of_one, *after):
        place = jnp.stack([section, core]).astype(jnp.int32)
        kept, going = call(
            settle_kernel,
            [far((seq_len, width), F32), shape((seq_len, width), BF16)],
            place,
            Far(of_zero),
            Far(of_one),
            *after,
        )
        return (kept, swap(going, "section"))

    def join(kept, came, *after):
        (out,) = call(
            join_kernel,
            [far((2 * seq_len, width), F32)],
            section_ref,
            Far(kept),
            came,
            *after,
        )
        return out[None]

    send, g_zero = run_experts(
        layout, "backward", exchange(send, sequences), x_zero, halves_in, halves_out
    )
    layer_pair = settle(layer_zero, layer_one, After(g_zero))
    (grads_one,) = call(
        functools.partial(dense_grad_kernel, layout),
        [far((model_width, packed), BF16)],
        Far(layer_zero),
        Far(dense_one, tail),
        Far(grad_qkv_one),
        Far(hidden_grad_one),
        Far(mixed_one),
        part_one,
        Far(small_one),
        Far(moe_gain_one),
        After(layer_pair[0]),
        **attn_cost,
    )
    own, other = returned(exchange(send, sequences), 0)
    hidden_grad, part, grads_zero = call(
        functools.partial(backward_kernel, layout, 0),
        [wide_rows, near_rows, far((model_width, packed), BF16)],
        Far(h1_zero),
        own,
        other,
        Far(grad_mid),
        Far(dense_zero),
        marks,
        rows,
        Far(qkv_zero),
        Far(lse_zero),
        Far(back_zero),
        Far(mixed_zero),
        Far(hidden_in),
        scratch=[wide_one, slot_scratch, mixed_scratch, pltpu.VMEM((seq_len, 3 * width), BF16)],
        **attn_cost,
    )
    (grad_first,) = call(
        functools.partial(input_grad_kernel, layout, False),
        [wide_rows],
        part,
        swap(part, "tensor"),
        Far(hidden_in),
        Far(hidden_grad),
        Far(dense_zero, tail),
        size=4 << 20,
    )

    rows_own, grad_rows_own = call(
        choose_kernel,
        [shape(x_zero.shape, BF16)] * 2,
        section_ref,
        Far(x_zero),
        Far(x_one),
        Far(g_zero),
        Far(g_one),
        After(grads_zero),
    )
    expert_in_grad, expert_out_grad = expert_weight_grads(
        rows_own,
        swap(rows_own, "tensor"),
        grad_rows_own,
        swap(grad_rows_own, "tensor"),
        half_in,
        half_out,
    )

    def spread(grads):
        cut = grads.reshape(parts, share, packed)
        pieces = lax.all_to_all(cut, "dp", split_axis=0, concat_axis=0, tiled=True)
        return pieces.reshape(model_width, packed)

    (sum_one,) = call(
        functools.partial(sum_one_kernel, parts), [far((share, packed), F32)], spread(grads_one)
    )
    grad_pair = settle(grad_first, grad_mid)
    mine, going = call(
        functools.partial(sum_both_kernel, parts),
        [shape((share, packed), F32), shape((share, packed), F32)],
        section_ref,
        spread(grads_zero),
        Far(sum_one),
        After(expert_in_grad),
        After(grad_pair[0]),
        scratch=[pltpu.VMEM((share, packed), F32)],
    )
    diagonal = [(i, 3 - i) for i in range(4)]
    qkv_grad, out_grad, router_grad, attn_gain_grad, moe_gain_grad = call(
        functools.partial(finish_kernel, layout),
        [
            shape((3, share, width), F32),
            shape((share, width), F32),
            shape((share, experts), F32),
            shape((1, share), F32),
            shape((1, share), F32),
        ],
        mine,
        swap(going, "section"),
        swap(mine[:, tail:], "tensor"),
        lax.ppermute(going[:, tail:], ("section", "tensor"), diagonal),
    )

    layer_outputs = join(*layer_pair, After(mine))
    input_grads = join(*grad_pair, After(mine))

    return (
        layer_outputs,
        input_grads,
        attn_gain_grad,
        moe_gain_grad,
        qkv_grad[None],
        out_grad.T[None],
        router_grad[None],
        expert_in_grad[None, None],
        expert_out_grad[None, None],
    )


def solution(mesh):
    placed = (
        P("dp", None),
        P("dp", None),
        P("dp", None),
        P("section", "dp"),
        P("section", "dp"),
        P("section", "dp"),
        P("section", "dp"),
        P("section", None, "dp", "tensor"),
        P("section", "tensor", "dp"),
        P("section", "dp", None),
        P("section", "dp", None, "tensor"),
        P("section", "dp", "tensor", None),
    )
    return jax.shard_map(
        local,
        mesh=mesh,
        in_specs=placed,
        out_specs=(
            P("section", "dp", "tensor"),
            P("section", "dp", "tensor"),
            P("section", "dp"),
            P("section", "dp"),
            P("section", None, "dp", "tensor"),
            P("section", "tensor", "dp"),
            P("section", "dp", None),
            P("section", "dp", None, "tensor"),
            P("section", "dp", "tensor", None),
        ),
        check_vma=False,
    )
```

```python
import functools

import jax
import jax.numpy as jnp
from jax import lax
from jax.experimental import pallas as pl
from jax.experimental.pallas import tpu as pltpu
from jax.sharding import PartitionSpec as P

HEAD_DIM = 64
EPS = 1e-06
MASK_FILL = -1e30
LANES = 128

F32 = jnp.float32
BF16 = jnp.bfloat16


def swap(value, axis):
    return lax.ppermute(value, axis, [(0, 1), (1, 0)])


def dot(left, right, left_dim, right_dim):
    return lax.dot_general(
        left, right, (((left_dim,), (right_dim,)), ((), ())), preferred_element_type=F32
    )


def unpack_rows(block_ref, wide_ref, rows_ref, base, per, half):
    count = block_ref.shape[0] // per
    wide_ref[...] = block_ref[...].astype(F32)
    for c in range(half):
        for j in range(rows_ref.shape[1] // LANES):
            piece = wide_ref[pl.ds(base + j * half + c, count, stride=per), :]
            rows_ref[c * count : (c + 1) * count, j * LANES : (j + 1) * LANES] = piece.astype(BF16)


def pack_rows(rows, wide_ref, base, per, half):
    count = rows.shape[0] // half
    for c in range(half):
        for j in range(rows.shape[1] // LANES):
            wide_ref[pl.ds(base + j * half + c, count, stride=per), :] = rows[
                c * count : (c + 1) * count, j * LANES : (j + 1) * LANES
            ]


def mean_of(values):
    return jnp.sum(values, axis=-1, keepdims=True) * (1.0 / values.shape[-1])


def norm_parts(rows):
    inv_scale = lax.rsqrt(mean_of(rows * rows) + EPS)
    return (inv_scale, rows * inv_scale)


def norm_back(grad_out, inv_scale, normed, gain_row):
    grad_normed = grad_out * gain_row
    gain_grad = jnp.sum(grad_out * normed, axis=0, keepdims=True)
    return (inv_scale * (grad_normed - normed * mean_of(grad_normed * normed)), gain_grad)


def tail_rows(tail_ref):
    return tail_ref[...].astype(F32).T


def one_hot_columns(slot_col, count):
    return (slot_col == lax.broadcasted_iota(jnp.int32, (slot_col.shape[0], count), 1)).astype(BF16)


def one_hot_rows(slot_row, count):
    return (slot_row == lax.broadcasted_iota(jnp.int32, (count, slot_row.shape[1]), 0)).astype(BF16)


class Staged:
    def __init__(self, ref, copy=None):
        self.ref, self.copy, self.waited, self.started = ref, copy, False, False

    def start(self):
        if self.copy is not None and not self.started:
            self.copy.start()
            self.started = True

    def __call__(self):
        if self.copy is not None and not self.waited:
            self.copy.wait()
            self.waited = True
        return self.ref

    def put(self, value):
        self.ref[...] = value
        self.start()


def shape(dims, dtype):
    return jax.ShapeDtypeStruct(dims, dtype)


class After:
    def __init__(self, what):
        self.what = what


class Far:
    def __init__(self, what, lane=0):
        self.what, self.lane = what, lane


def staged_kernel(kernel, ins, outs, scratch_count, *refs):
    count = len(ins) + len(outs)
    rest = list(refs[count:])
    scratch, rest = rest[:scratch_count], rest[scratch_count:]
    far = [item for item in list(ins) + list(outs) if isinstance(item, Far)]
    rooms, sems = rest[: len(far)], rest[len(far)] if far else None
    staged = []
    index = 0
    for place, (item, ref) in enumerate(zip(list(ins) + list(outs), refs)):
        if isinstance(item, After):
            continue
        if not isinstance(item, Far):
            staged.append(Staged(ref))
            continue
        if place < len(ins):
            source = ref if item.lane == 0 else ref.at[:, item.lane :]
            copy = pltpu.make_async_copy(source, rooms[index], sems.at[index])
        else:
            copy = pltpu.make_async_copy(rooms[index], ref, sems.at[index])
        staged.append(Staged(rooms[index], copy))
        index += 1
    given = sum(not isinstance(item, After) for item in ins)
    for item in staged[:given]:
        item.start()
    kernel(*staged, *scratch)
    for item in staged[:given]:
        item()
    for item in staged[given:]:
        item.start()
    for item in staged[given:]:
        item()


def call(kernel, outs, *ins, scratch=(), flops=0, size=0):
    far = [item for item in list(ins) + list(outs) if isinstance(item, Far)]
    rooms = [
        pltpu.VMEM(item.what.shape[:-1] + (item.what.shape[-1] - item.lane,), item.what.dtype)
        for item in far
    ]
    if far:
        rooms.append(pltpu.SemaphoreType.DMA((len(far),)))

    def spec(item):
        if isinstance(item, (Far, After)):
            return pl.BlockSpec(memory_space=pl.ANY)
        return pl.BlockSpec(memory_space=pltpu.SMEM if len(item.shape) == 1 else pltpu.VMEM)


    def operand(item):
        if isinstance(item, (Far, After)):
            return pltpu.with_memory_space_constraint(item.what, pltpu.HBM)
        return item

    args = [operand(item) for item in ins]
    shapes = [
        pltpu.HBM(item.what.shape, item.what.dtype) if isinstance(item, Far) else item
        for item in outs
    ]
    return pl.pallas_call(
        functools.partial(staged_kernel, kernel, ins, outs, len(scratch)),
        out_shape=shapes,
        in_specs=[spec(item) for item in ins],
        out_specs=[spec(item) for item in outs],
        scratch_shapes=list(scratch) + rooms,
        compiler_params=pltpu.CompilerParams(vmem_limit_bytes=24 << 20),
        cost_estimate=pl.CostEstimate(flops=flops, bytes_accessed=size, transcendentals=0),
    )(*args)


def pack_kernel(qkv, out, router, attn_gain, moe_gain, mine):
    to = mine.ref
    share = router()[0].shape[0]
    width = qkv()[0, 0].shape[1]
    experts = router()[0].shape[1]
    for c in range(3):
        to[:, c * width : (c + 1) * width] = qkv()[0, c]
    row = lax.broadcasted_iota(jnp.int32, (share, share), 0)
    lane = lax.broadcasted_iota(jnp.int32, (share, share), 1)
    eye = row == lane
    to[:, 3 * width : 4 * width] = out()[0]
    to[:, 4 * width :] = jnp.zeros((share, LANES), BF16)
    to[:, 4 * width : 4 * width + experts] = router()[0]
    for index, gain in enumerate((attn_gain, moe_gain)):
        spread = jnp.where(eye, jnp.broadcast_to(gain()[...].astype(F32), (share, share)), 0.0)
        at = 4 * width + experts + index
        to[:, at : at + 1] = jnp.sum(spread, axis=1, keepdims=True).astype(BF16)


def spread_kernel(parts, mine, theirs, section, copies, other):
    share = mine().shape[0]
    first = section()[0] == 0
    own, came = mine()[...].astype(F32), theirs()[...].astype(F32)
    zero = jnp.where(first, own, came)
    other.ref[...] = jnp.where(first, came, own).astype(BF16)
    several = 2
    block = jnp.concatenate([zero] * several, axis=0).astype(BF16)
    for part in range(parts // several):
        copies.ref[part * several * share : (part + 1) * several * share] = block


def attend(hidden, weight, layout, marks, rows, qkv, mixed, lse, part):
    width = layout["width"]
    weight_ref = weight()
    turned = tail_rows(weight_ref.at[:, layout["tail"] :])
    attn_gain = turned[layout["experts"] : layout["experts"] + 1]
    _, normed = norm_parts(hidden)
    low = (normed * attn_gain).astype(BF16)
    qkv.put(dot(low, weight_ref[:, : 3 * width], 1, 0).astype(BF16))
    same = marks()[:, 6:7] == rows()[2:3]
    for head in range(width // HEAD_DIM):
        at = head * HEAD_DIM
        queries = qkv.ref[:, at : at + HEAD_DIM]
        keys = qkv.ref[:, width + at : width + at + HEAD_DIM]
        values = qkv.ref[:, 2 * width + at : 2 * width + at + HEAD_DIM]
        scores = dot(queries, keys, 1, 1) * HEAD_DIM ** (-0.5)
        scores = jnp.where(same, scores, MASK_FILL)
        top = jnp.max(scores, axis=-1, keepdims=True)
        exponent = jnp.exp(scores - top)
        total = jnp.sum(exponent, axis=-1, keepdims=True)
        soft = (exponent * (1.0 / total)).astype(BF16)
        mixed.ref[:, at : at + HEAD_DIM] = dot(soft, values, 1, 0).astype(BF16)
        lse.ref[:, head : head + 1] = top + jnp.log(total)
    mixed.start()
    lse.start()
    part.ref[...] = dot(mixed.ref[...], weight_ref[:, 3 * width : 4 * width], 1, 1).astype(BF16)


def attend_first_kernel(layout, hidden, weight, marks, rows, *outs):
    attend(hidden()[...].astype(F32), weight, layout, marks, rows, *outs)


def attend_next_kernel(
    layout, hidden, gate, block_own, block_other, weight, marks, rows, layer, back, qkv, mixed, lse, part, wide_ref, rows_ref
):
    returned = gather_back(layout, block_own(), block_other(), marks, 0, wide_ref, rows_ref, 0)
    back.put(returned.astype(BF16))
    layer.put(hidden()[...] + gate()[...] * returned)
    attend(layer.ref[...], weight, layout, marks, rows, qkv, mixed, lse, part)


def gather_back(layout, block_own, block_other, marks, layer, wide_ref, rows_ref, base):
    half = layout["half"]
    per = block_own.shape[0] // layout["experts"]
    count = rows_ref.shape[0]
    total = 0.0
    for which, block in enumerate((block_own, block_other)):
        at = 3 * layer + which
        unpack_rows(block, wide_ref, rows_ref, base, per, half)
        total = total + dot(
            one_hot_columns(marks()[:, at : at + 1], count), rows_ref[...], 1, 0
        )
    return total


def send_slots(layout, slot_row, pieces, wide_ref, out_ref):
    half, experts = layout["half"], layout["experts"]
    per = wide_ref.shape[0] // experts
    placed = one_hot_rows(slot_row, half * experts)
    wide_ref[...] = jnp.zeros_like(wide_ref)
    for index, piece in enumerate(pieces):
        pack_rows(dot(placed, piece, 1, 0), wide_ref, index * layout["block"], per, half)
    low = wide_ref[...].astype(BF16)
    size = wide_ref.shape[0]
    out_ref[:size] = low
    out_ref[size:] = low


def router_parts(layout, layer, hidden, tail_ref, marks):
    experts = layout["experts"]
    moe_gain = tail_rows(tail_ref)[experts + 1 : experts + 2]
    inv_scale, normed = norm_parts(hidden)
    low = (normed * moe_gain).astype(BF16)
    logits = dot(low, tail_ref[...], 1, 0)
    lane = lax.broadcasted_iota(jnp.int32, logits.shape, 1)
    logits = jnp.where(lane < experts, logits, MASK_FILL)
    exponent = jnp.exp(logits - jnp.max(logits, axis=-1, keepdims=True))
    prob = exponent * (1.0 / jnp.sum(exponent, axis=-1, keepdims=True))
    at = 3 * layer + 2
    chosen = lane == marks()[:, at : at + 1]
    gate = jnp.sum(jnp.where(chosen, prob, 0.0), axis=-1, keepdims=True)
    return (inv_scale, normed, moe_gain, low, prob, chosen.astype(F32), gate)


def route_kernel(layout, layer, hidden_in, part_own, part_other, tail, marks, rows, *rest):
    if layer == 1:
        target, h1, gate_out, send, wide_ref = rest
    else:
        h1, gate_out, send, wide_ref = rest
    attention = part_own()[...].astype(F32) + part_other()[...].astype(F32)
    hidden = hidden_in()[...].astype(F32) + attention
    h1.put(hidden)
    _, _, _, low, _, _, gate = router_parts(layout, layer, hidden, tail(), marks)
    gate_out.put(gate)
    pieces = [low]
    if layer == 1:
        pieces.append((gate * target()[...].astype(F32)).astype(BF16))
    send_slots(layout, rows()[layer : layer + 1], pieces, wide_ref, send.ref)


def backward_kernel(layout, layer, h1, block_own, block_other, grad, weight, marks, rows, qkv, lse, *rest):
    if layer == 1:
        layer_out, hidden_grad, part, grad_qkv, small, moe_gain_grad = rest[:6]
        rest = rest[6:]
    else:
        returned_in, mixed_in, layer_in, hidden_grad, part, dense_out = rest[:6]
        rest = rest[6:]
    wide_ref, rows_ref, mixed_ref = rest[:3]
    grad_qkv_ref = grad_qkv.ref if layer == 1 else rest[3]
    width = layout["width"]
    experts = layout["experts"]
    scaling = HEAD_DIM ** (-0.5)
    own, other = block_own(), block_other()
    if layer == 1:
        returned = gather_back(layout, own, other, marks, layer, wide_ref, rows_ref, 0)
    base = layout["block"] if layer == 1 else 0
    grad_back = gather_back(layout, own, other, marks, layer, wide_ref, rows_ref, base)
    grad_out = grad()[...].astype(F32)
    hidden = h1()[...]
    weight_ref = weight()
    tail_ref = weight_ref.at[:, layout["tail"] :]
    inv_scale, normed, moe_gain, moe, prob, chosen, gate = router_parts(
        layout, layer, hidden, tail_ref, marks
    )
    if layer == 1:
        layer_out.put(hidden + gate * returned)
    else:
        returned = returned_in()[...].astype(F32)
    grad_gate = jnp.sum(grad_out * returned, axis=-1, keepdims=True)
    grad_logits = (grad_gate * gate * (chosen - prob)).astype(BF16)
    router_grad = dot(moe, grad_logits, 0, 0)
    grad_moe = grad_back + dot(grad_logits, tail_ref[...], 1, 1)
    grad_norm, gain_grad = norm_back(grad_moe, inv_scale, normed, moe_gain)
    if layer == 1:
        small.put(router_grad)
        moe_gain_grad.put(gain_grad)
    grad_hidden = grad_out + grad_norm
    hidden_grad.put(grad_hidden)
    mixed_ref[...] = dot(
        grad_hidden.astype(BF16), weight_ref[:, 3 * width : 4 * width], 1, 0
    ).astype(BF16)
    same = marks()[:, 6:7] == rows()[2:3]
    qkv_ref, lse_ref = qkv(), lse()
    for head in range(width // HEAD_DIM):
        at = head * HEAD_DIM
        queries = qkv_ref[:, at : at + HEAD_DIM]
        keys = qkv_ref[:, width + at : width + at + HEAD_DIM]
        values = qkv_ref[:, 2 * width + at : 2 * width + at + HEAD_DIM]
        grad_mixed = mixed_ref[:, at : at + HEAD_DIM]
        scores = dot(queries, keys, 1, 1) * scaling
        soft = jnp.exp(jnp.where(same, scores - lse_ref[:, head : head + 1], MASK_FILL))
        grad_soft = dot(grad_mixed, values, 1, 1)
        delta = jnp.sum(soft * grad_soft, axis=-1, keepdims=True)
        grad_scores = (soft * (grad_soft - delta)).astype(BF16)
        grad_qkv_ref[:, at : at + HEAD_DIM] = (dot(grad_scores, keys, 1, 0) * scaling).astype(BF16)
        grad_qkv_ref[:, width + at : width + at + HEAD_DIM] = (
            dot(grad_scores, queries, 0, 0) * scaling
        ).astype(BF16)
        grad_qkv_ref[:, 2 * width + at : 2 * width + at + HEAD_DIM] = dot(
            soft.astype(BF16), grad_mixed, 0, 0
        ).astype(BF16)
    if layer == 1:
        grad_qkv.start()
    part.ref[...] = dot(grad_qkv_ref[...], weight_ref[:, : 3 * width], 1, 1).astype(BF16)
    if layer == 0:
        dense_grads(
            layout,
            layer_in()[...].astype(F32),
            tail_ref,
            grad_qkv_ref,
            grad_hidden,
            mixed_in(),
            part.ref,
            router_grad,
            gain_grad,
            dense_out.ref,
        )


def dense_grads(
    layout, layer_in, tail_ref, grad_qkv_ref, grad_hidden, mixed_ref, part_ref, router_grad, moe_gain_grad, out_ref
):
    width = layout["width"]
    experts = layout["experts"]
    _, normed = norm_parts(layer_in)
    attn_gain = tail_rows(tail_ref)[experts : experts + 1]
    low = (normed * attn_gain).astype(BF16)
    out_ref[:, : 3 * width] = dot(low, grad_qkv_ref[...], 0, 0).astype(BF16)
    out_ref[:, 3 * width : 4 * width] = dot(
        grad_hidden.astype(BF16), mixed_ref[...], 0, 0
    ).astype(BF16)
    attn_gain_grad = jnp.sum(part_ref[...].astype(F32) * normed, axis=0, keepdims=True)
    lane = lax.broadcasted_iota(jnp.int32, router_grad.shape, 1)
    size = router_grad.shape[0]
    attn_col = jnp.broadcast_to(attn_gain_grad, (LANES, size)).T
    moe_col = jnp.broadcast_to(moe_gain_grad, (LANES, size)).T
    small = jnp.where(lane == experts, attn_col, router_grad)
    small = jnp.where(lane == experts + 1, moe_col, small)
    out_ref[:, 4 * width : 4 * width + LANES] = small.astype(BF16)


def dense_grad_kernel(
    layout, layer_in, tail, grad_qkv, hidden_grad, mixed, part, small, moe_gain_grad, out
):
    dense_grads(
        layout,
        layer_in()[...],
        tail(),
        grad_qkv(),
        hidden_grad()[...],
        mixed(),
        part(),
        small()[...],
        moe_gain_grad()[...],
        out.ref,
    )


def choose_kernel(section, *refs):
    half = len(refs) // 3
    ins, outs = refs[: 2 * half], refs[2 * half :]
    first = section()[0] == 0
    for index, out in enumerate(outs):
        zero, one = ins[2 * index]()[...], ins[2 * index + 1]()[...]
        out.put(jnp.where(first, zero.astype(F32), one.astype(F32)).astype(out.ref.dtype))


def settle_kernel(place, zero, one, kept, going):
    first = place()[0] == 0
    width = kept.ref.shape[1]
    left = place()[1] == 0
    of_zero = jnp.where(left, zero()[:, :width], zero()[:, width:])
    of_one = jnp.where(left, one()[:, :width], one()[:, width:])
    going.put(jnp.where(first, of_one, of_zero).astype(BF16))
    kept.put(jnp.where(first, of_zero, of_one))


def join_kernel(section, kept, came, out):
    count = kept().shape[0]
    first = section()[0] == 0
    arrived = came()[...].astype(F32)
    out.ref[:count] = jnp.where(first, kept()[...], arrived)
    out.ref[count:] = jnp.where(first, arrived, kept()[...])
    out.start()


def input_grad_kernel(layout, send, part_own, part_other, layer_in, hidden_grad, tail, *rest):
    experts = layout["experts"]
    attn_gain = tail_rows(tail())[experts : experts + 1]
    inv_scale, normed = norm_parts(layer_in()[...].astype(F32))
    grad_normed = part_own()[...].astype(F32) + part_other()[...].astype(F32)
    grad_norm, _ = norm_back(grad_normed, inv_scale, normed, attn_gain)
    grad_in = hidden_grad()[...] + grad_norm
    if send:
        gate, rows, grad, send_out, wide_ref = rest
        grad.put(grad_in)
        pieces = [(gate()[...] * grad_in).astype(BF16)]
        send_slots(layout, rows()[0:1], pieces, wide_ref, send_out.ref)
    else:
        (grad,) = rest
        grad.put(grad_in)


def sum_pieces(pieces, total, parts):
    share, cols = total.shape
    pair = 2 * share
    for at in range(0, cols, LANES):
        value = pieces[:pair, at : at + LANES].astype(F32)
        for part in range(1, parts // 2):
            value = value + pieces[part * pair : (part + 1) * pair, at : at + LANES].astype(F32)
        total[:, at : at + LANES] = value[:share] + value[share:]


def sum_one_kernel(parts, pieces, total):
    sum_pieces(pieces(), total.ref, parts)


def sum_both_kernel(parts, section, pieces, one, mine, going, done, wide_ref):
    sum_pieces(pieces(), wide_ref, parts)
    first = section()[0] == 0
    zero, one = wide_ref[...], one()[...]
    mine.ref[...] = jnp.where(first, zero, one)
    going.ref[...] = jnp.where(first, one, zero)
    done.put(jnp.zeros(done.ref.shape, F32))


def finish_kernel(layout, mine, theirs, core, across, qkv, out, router, attn_gain, moe_gain):
    width, experts = layout["width"], layout["experts"]
    whole = mine()[...] + theirs()[...]
    small = whole[:, 4 * width :]
    lane = lax.broadcasted_iota(jnp.int32, small.shape, 1)
    small = small + jnp.where(lane == experts, core()[...] + across()[...], 0.0)
    for c in range(3):
        qkv.ref[c] = whole[:, c * width : (c + 1) * width]
    out.ref[...] = whole[:, 3 * width : 4 * width]
    router.ref[...] = small[:, :experts]
    share = small.shape[0]
    turned = jnp.concatenate([small, jnp.zeros((LANES - share, LANES), F32)], axis=0).T
    attn_gain.ref[...] = turned[experts : experts + 1, :share]
    moe_gain.ref[...] = turned[experts + 1 : experts + 2, :share]


GELU_SCALE = 0.7978845608028654
GELU_CUBE = 0.044715


def gelu_parts(values):
    square = values * values
    bend = jnp.tanh(GELU_SCALE * (values + GELU_CUBE * (values * square)))
    return (square, bend)


def gelu_of(values, bend):
    return 0.5 * values * (1.0 + bend)


def gelu_slope(values, square, bend):
    inner = GELU_SCALE * (1.0 + 3.0 * GELU_CUBE * square)
    return 0.5 * (1.0 + bend) + 0.5 * values * (1.0 - bend * bend) * inner


def expert_kernel(layout, mode, *refs):
    half = layout["half"]
    step = pl.program_id(0)
    block_ref, refs = refs[0], refs[1:]
    if mode == "backward":
        x_ref, refs = refs[0], refs[1:]
    in_a, in_b, out_a, out_b = refs[:4]
    refs = refs[4:]
    if mode == "forward":
        send_ref, x_ref, wide_ref, y_acc = refs
    elif mode == "both":
        send_ref, x_ref, g_ref, wide_ref, y_acc, dx_acc = refs
    else:
        send_ref, g_ref, wide_ref, dx_acc = refs
    per = block_ref.shape[0] // layout["sequences"]

    @pl.when(step == 0)
    def _():
        if mode != "backward":
            unpack_rows(block_ref, wide_ref, x_ref, 0, per, half)
            y_acc[...] = jnp.zeros_like(y_acc)
        if mode != "forward":
            unpack_rows(
                block_ref, wide_ref, g_ref, layout["block"] if mode == "both" else 0, per, half
            )
            dx_acc[...] = jnp.zeros_like(dx_acc)

    rows = x_ref[...]
    y_sum, dx_sum = 0.0, 0.0
    for w_in, w_out in ((in_a, out_a), (in_b, out_b)):
        hidden = dot(rows, w_in[...], 1, 0)
        square, bend = gelu_parts(hidden)
        if mode != "backward":
            y_sum = y_sum + dot(gelu_of(hidden, bend).astype(BF16), w_out[...], 1, 0)
        if mode != "forward":
            grad_act = dot(g_ref[...], w_out[...], 1, 1)
            grad_pre = (grad_act * gelu_slope(hidden, square, bend)).astype(BF16)
            dx_sum = dx_sum + dot(grad_pre, w_in[...], 1, 1)
    if mode != "backward":
        y_acc[...] += y_sum
    if mode != "forward":
        dx_acc[...] += dx_sum

    @pl.when(step == pl.num_programs(0) - 1)
    def _():
        wide_ref[...] = jnp.zeros_like(wide_ref)
        if mode != "backward":
            pack_rows(y_acc[...], wide_ref, 0, per, half)
        if mode != "forward":
            pack_rows(dx_acc[...], wide_ref, layout["block"] if mode == "both" else 0, per, half)
        send_ref[...] = wide_ref[...].astype(BF16)


def run_experts(layout, mode, block, x_rows, halves_in, halves_out):
    rows = layout["half"] * layout["sequences"]
    width, hidden = halves_in[0].shape
    chunk = 768
    whole = lambda array: pl.BlockSpec(array.shape, lambda i: (0, 0))
    args, specs = [block], [whole(block)]
    if mode == "backward":
        args.append(pltpu.with_memory_space_constraint(x_rows, pltpu.HBM))
        specs.append(whole(x_rows))
    args += [pltpu.with_memory_space_constraint(w, pltpu.HBM) for w in (*halves_in, *halves_out)]
    specs += [pl.BlockSpec((width, chunk), lambda i: (0, i))] * 2
    specs += [pl.BlockSpec((chunk, width), lambda i: (i, 0))] * 2
    outs = [shape(block.shape, BF16)]
    row_far = pltpu.HBM((rows, width), BF16)
    if mode != "backward":
        outs.append(row_far)
    if mode != "forward":
        outs.append(row_far)
    scratch = [pltpu.VMEM(block.shape, F32), pltpu.VMEM((rows, width), F32)]
    if mode == "both":
        scratch.append(pltpu.VMEM((rows, width), F32))
    passes = {"forward": 4, "both": 8, "backward": 6}[mode]
    return pl.pallas_call(
        functools.partial(expert_kernel, layout, mode),
        grid=(hidden // chunk,),
        in_specs=specs,
        out_specs=[whole(out) for out in outs],
        out_shape=outs,
        scratch_shapes=scratch,
        compiler_params=pltpu.CompilerParams(
            vmem_limit_bytes=24 << 20, dimension_semantics=("arbitrary",)
        ),
        cost_estimate=pl.CostEstimate(
            flops=2 * passes * rows * width * hidden, bytes_accessed=8 * width * hidden, transcendentals=0
        ),
    )(*args)


def expert_grad_kernel(rows_own, rows_other, grad_own, grad_other, w_in, w_out, grad_in, grad_out, x_ref, g_ref):
    size = rows_own.shape[0]

    @pl.when(pl.program_id(0) == 0)
    def _():
        x_ref[:size] = rows_own[...]
        x_ref[size:] = rows_other[...]
        g_ref[:size] = grad_own[...]
        g_ref[size:] = grad_other[...]

    hidden = dot(x_ref[...], w_in[...], 1, 0)
    square, bend = gelu_parts(hidden)
    grad_act = dot(g_ref[...], w_out[...], 1, 1)
    grad_pre = (grad_act * gelu_slope(hidden, square, bend)).astype(BF16)
    grad_in[...] = dot(x_ref[...], grad_pre, 0, 0)
    grad_out[...] = dot(gelu_of(hidden, bend).astype(BF16), g_ref[...], 0, 0)


def expert_weight_grads(rows_own, rows_other, grad_own, grad_other, half_in, half_out):
    size, width = rows_own.shape
    hidden = half_in.shape[1]
    chunk = 256
    whole = pl.BlockSpec((size, width), lambda i: (0, 0))
    by_in = pl.BlockSpec((width, chunk), lambda i: (0, i))
    by_out = pl.BlockSpec((chunk, width), lambda i: (i, 0))
    pin = lambda array: pltpu.with_memory_space_constraint(array, pltpu.HBM)
    return pl.pallas_call(
        expert_grad_kernel,
        grid=(hidden // chunk,),
        in_specs=[whole] * 4 + [by_in, by_out],
        out_specs=[by_in, by_out],
        out_shape=[pltpu.HBM((width, hidden), F32), pltpu.HBM((hidden, width), F32)],
        scratch_shapes=[pltpu.VMEM((2 * size, width), BF16)] * 2,
        compiler_params=pltpu.CompilerParams(
            vmem_limit_bytes=24 << 20, dimension_semantics=("arbitrary",)
        ),
        cost_estimate=pl.CostEstimate(
            flops=16 * size * width * hidden, bytes_accessed=12 * width * hidden, transcendentals=0
        ),
    )(rows_own, rows_other, grad_own, grad_other, pin(half_in), pin(half_out))


def exchange(blocks, sequences):
    cut = blocks.reshape(sequences, -1, blocks.shape[1])
    came = lax.all_to_all(cut, ("section", "dp"), split_axis=0, concat_axis=0, tiled=True)
    return came.reshape(blocks.shape)


def local(
    tokens,
    cotangent,
    segments,
    routes,
    keeps,
    attn_gain,
    moe_gain,
    qkv_weight,
    out_weight,
    router_weight,
    expert_in,
    expert_out,
):
    section = lax.axis_index("section")
    core = lax.axis_index("tensor")
    first = section == 0
    seq_len = segments.shape[1]
    model_width = tokens.shape[1]
    experts = router_weight.shape[2]
    parts = lax.axis_size("dp")
    capacity = max(2, 5 * seq_len // (4 * experts))
    half = capacity // 2
    width = qkv_weight.shape[3]
    share = model_width // parts
    sequences = parts * lax.axis_size("section")
    block = -(-half * (model_width // LANES) // 16) * 16
    tail = 4 * width
    layout = {
        "width": width,
        "tail": tail,
        "experts": experts,
        "half": half,
        "block": block,
        "sequences": sequences,
    }
    packed = tail + LANES
    section_ref = section.reshape(1).astype(jnp.int32)

    far = lambda dims, dtype: Far(shape(dims, dtype))

    (mine,) = call(
        pack_kernel,
        [shape((share, packed), BF16)],
        Far(qkv_weight),
        Far(out_weight.swapaxes(1, 2)),
        Far(router_weight),
        Far(attn_gain),
        Far(moe_gain),
    )
    coded = (routes[0] + experts * keeps[0]).reshape(2, seq_len)
    coded_own = jnp.where(first, coded[0], coded[1])
    coded_other = swap(jnp.where(first, coded[1], coded[0]), "section")
    copies, shard_one = call(
        functools.partial(spread_kernel, parts),
        [far((parts * share, packed), BF16), shape((share, packed), BF16)],
        mine,
        swap(mine, "section"),
        section_ref,
        After(coded_other),
    )
    dense_zero = lax.all_to_all(
        copies.reshape(parts, share, packed), "dp", split_axis=0, concat_axis=0, tiled=True
    ).reshape(model_width, packed)
    dense_one = lax.all_gather(shard_one, "dp", axis=0, tiled=True)

    half_in = expert_in[0, 0]
    half_out = expert_out[0, 0]
    halves_in = (half_in, swap(half_in, "tensor"))
    halves_out = (half_out, swap(half_out, "tensor"))

    hidden_in = lax.dynamic_slice_in_dim(tokens, section * seq_len, seq_len, 0)
    target = lax.dynamic_slice_in_dim(cotangent, section * seq_len, seq_len, 0)
    seg_row = jnp.where(first, segments[0], segments[1])
    columns, slot_rows = [], []
    for code in (
        jnp.where(first, coded_own, coded_other),
        jnp.where(first, coded_other, coded_own),
    ):
        route, keep = code % experts, code // experts
        index = jnp.arange(seq_len)
        earlier = (route[:, None] == route[None, :]) & (index[:, None] > index[None, :])
        rank = jnp.sum(jnp.where(earlier, keep[None, :], 0), axis=1)
        slot = (rank % half) * experts + route
        kept = keep == 1
        own = jnp.where(kept & (rank // half == core), slot, -1)
        other = jnp.where(kept & (rank // half == 1 - core), slot, -1)
        columns += [own, other, route]
        slot_rows.append(own)
    columns = jnp.stack(columns + [seg_row], axis=1)
    marks = Far(jnp.pad(columns, ((0, 0), (0, LANES - columns.shape[1]))))
    rows = Far(jnp.pad(jnp.stack(slot_rows + [seg_row], axis=0), ((0, 5), (0, 0))))

    rows_shape = (seq_len, model_width)
    wide_rows = far(rows_shape, F32)
    attend_outs = [
        far((seq_len, 3 * width), BF16),
        far((seq_len, width), BF16),
        far((seq_len, LANES), F32),
        shape(rows_shape, BF16),
    ]
    gate_shape = far((seq_len, 1), F32)
    slot_scratch = pltpu.VMEM((half * experts, model_width), BF16)
    wide_one = pltpu.VMEM((experts * block, LANES), F32)
    wide_two = pltpu.VMEM((experts * 2 * block, LANES), F32)
    mixed_scratch = pltpu.VMEM((seq_len, width), BF16)
    attn_cost = dict(flops=2 * seq_len * model_width * 5 * width, size=8 << 20)

    def returned(blocks, layer):
        size = blocks.shape[0] // 2
        own = blocks[layer * size : (layer + 1) * size]
        return (own, swap(own, "tensor"))

    qkv_zero, mixed_zero, lse_zero, part = call(
        functools.partial(attend_first_kernel, layout),
        attend_outs,
        Far(hidden_in),
        dense_zero,
        marks,
        rows,
        **attn_cost,
    )
    h1_zero, gate_zero, send = call(
        functools.partial(route_kernel, layout, 0),
        [wide_rows, gate_shape, shape((sequences * block, LANES), BF16)],
        Far(hidden_in),
        part,
        swap(part, "tensor"),
        Far(dense_zero, tail),
        marks,
        rows,
        scratch=[wide_one],
        size=4 << 20,
    )
    send, x_zero = run_experts(
        layout, "forward", exchange(send, sequences), None, halves_in, halves_out
    )
    own, other = returned(exchange(send, sequences), 0)

    layer_zero, back_zero, qkv_one, mixed_one, lse_one, part = call(
        functools.partial(attend_next_kernel, layout),
        [wide_rows, far(rows_shape, BF16)] + attend_outs,
        Far(h1_zero),
        Far(gate_zero),
        own,
        other,
        Far(dense_one),
        marks,
        rows,
        scratch=[wide_one, slot_scratch],
        **attn_cost,
    )
    h1_one, _, send = call(
        functools.partial(route_kernel, layout, 1),
        [wide_rows, gate_shape, shape((2 * sequences * block, LANES), BF16)],
        Far(layer_zero),
        part,
        swap(part, "tensor"),
        Far(dense_one, tail),
        marks,
        rows,
        Far(target),
        scratch=[wide_two],
        size=4 << 20,
    )
    send, x_one, g_one = run_experts(
        layout, "both", exchange(send, sequences), None, halves_in, halves_out
    )
    own, other = returned(exchange(send, sequences), 1)

    layer_one, hidden_grad_one, part_one, grad_qkv_one, small_one, moe_gain_one = call(
        functools.partial(backward_kernel, layout, 1),
        [
            wide_rows,
            wide_rows,
            shape(rows_shape, BF16),
            far((seq_len, 3 * width), BF16),
            far((model_width, LANES), F32),
            far((1, model_width), F32),
        ],
        Far(h1_one),
        own,
        other,
        Far(target),
        Far(dense_one),
        marks,
        rows,
        Far(qkv_one),
        Far(lse_one),
        scratch=[wide_two, slot_scratch, mixed_scratch],
        **attn_cost,
    )
    grad_mid, send = call(
        functools.partial(input_grad_kernel, layout, True),
        [wide_rows, shape((sequences * block, LANES), BF16)],
        part_one,
        swap(part_one, "tensor"),
        Far(layer_zero),
        Far(hidden_grad_one),
        Far(dense_one, tail),
        Far(gate_zero),
        rows,
        scratch=[wide_one],
        size=4 << 20,
    )
    def settle(of_zero, of_one, *after):
        place = jnp.stack([section, core]).astype(jnp.int32)
        kept, going = call(
            settle_kernel,
            [far((seq_len, width), F32), shape((seq_len, width), BF16)],
            place,
            Far(of_zero),
            Far(of_one),
            *after,
        )
        return (kept, swap(going, "section"))

    def join(kept, came, *after):
        (out,) = call(
            join_kernel,
            [far((2 * seq_len, width), F32)],
            section_ref,
            Far(kept),
            came,
            *after,
        )
        return out[None]

    send, g_zero = run_experts(
        layout, "backward", exchange(send, sequences), x_zero, halves_in, halves_out
    )
    layer_pair = settle(layer_zero, layer_one, After(g_zero))
    (grads_one,) = call(
        functools.partial(dense_grad_kernel, layout),
        [far((model_width, packed), BF16)],
        Far(layer_zero),
        Far(dense_one, tail),
        Far(grad_qkv_one),
        Far(hidden_grad_one),
        Far(mixed_one),
        part_one,
        Far(small_one),
        Far(moe_gain_one),
        After(layer_pair[0]),
        **attn_cost,
    )
    own, other = returned(exchange(send, sequences), 0)
    hidden_grad, part, grads_zero = call(
        functools.partial(backward_kernel, layout, 0),
        [wide_rows, shape(rows_shape, BF16), far((model_width, packed), BF16)],
        Far(h1_zero),
        own,
        other,
        Far(grad_mid),
        Far(dense_zero),
        marks,
        rows,
        Far(qkv_zero),
        Far(lse_zero),
        Far(back_zero),
        Far(mixed_zero),
        Far(hidden_in),
        scratch=[wide_one, slot_scratch, mixed_scratch, pltpu.VMEM((seq_len, 3 * width), BF16)],
        **attn_cost,
    )
    (grad_first,) = call(
        functools.partial(input_grad_kernel, layout, False),
        [wide_rows],
        part,
        swap(part, "tensor"),
        Far(hidden_in),
        Far(hidden_grad),
        Far(dense_zero, tail),
        size=4 << 20,
    )

    def spread(grads):
        cut = grads.reshape(parts, share, packed)
        pieces = lax.all_to_all(cut, "dp", split_axis=0, concat_axis=0, tiled=True)
        return pieces.reshape(model_width, packed)

    (sum_one,) = call(
        functools.partial(sum_one_kernel, parts),
        [far((share, packed), F32)],
        Far(spread(grads_one)),
    )
    rows_own, grad_rows_own = call(
        choose_kernel,
        [shape(x_zero.shape, BF16)] * 2,
        section_ref,
        Far(x_zero),
        Far(x_one),
        Far(g_zero),
        Far(g_one),
        After(grads_zero),
        After(sum_one),
    )
    expert_in_grad, expert_out_grad = expert_weight_grads(
        rows_own,
        swap(rows_own, "tensor"),
        grad_rows_own,
        swap(grad_rows_own, "tensor"),
        half_in,
        half_out,
    )

    grad_pair = settle(grad_first, grad_mid)
    mine, going, done = call(
        functools.partial(sum_both_kernel, parts),
        [shape((share, packed), F32), shape((share, packed), F32), far((8, LANES), F32)],
        section_ref,
        spread(grads_zero),
        Far(sum_one),
        After(expert_in_grad),
        After(grad_pair[0]),
        scratch=[pltpu.VMEM((share, packed), F32)],
    )
    diagonal = [(i, 3 - i) for i in range(4)]
    qkv_grad, out_grad, router_grad, attn_gain_grad, moe_gain_grad = call(
        functools.partial(finish_kernel, layout),
        [
            shape((3, share, width), F32),
            shape((share, width), F32),
            shape((share, experts), F32),
            shape((1, share), F32),
            shape((1, share), F32),
        ],
        mine,
        swap(going, "section"),
        swap(mine[:, tail:], "tensor"),
        lax.ppermute(going[:, tail:], ("section", "tensor"), diagonal),
    )

    layer_outputs = join(*layer_pair, After(done))
    input_grads = join(*grad_pair, After(done))

    return (
        layer_outputs,
        input_grads,
        attn_gain_grad,
        moe_gain_grad,
        qkv_grad[None],
        out_grad.T[None],
        router_grad[None],
        expert_in_grad[None, None],
        expert_out_grad[None, None],
    )


def solution(mesh):
    placed = (
        P("dp", None),
        P("dp", None),
        P("dp", None),
        P("section", "dp"),
        P("section", "dp"),
        P("section", "dp"),
        P("section", "dp"),
        P("section", None, "dp", "tensor"),
        P("section", "tensor", "dp"),
        P("section", "dp", None),
        P("section", "dp", None, "tensor"),
        P("section", "dp", "tensor", None),
    )
    return jax.shard_map(
        local,
        mesh=mesh,
        in_specs=placed,
        out_specs=(
            P("section", "dp", "tensor"),
            P("section", "dp", "tensor"),
            P("section", "dp"),
            P("section", "dp"),
            P("section", None, "dp", "tensor"),
            P("section", "tensor", "dp"),
            P("section", "dp", None),
            P("section", "dp", None, "tensor"),
            P("section", "dp", "tensor", None),
        ),
        check_vma=False,
    )
```
